128 devices in a mesh: sec: 16 (over z_lo, x, core), img: 8 (over y, z_hi).
Axes of the slice: x: 4, y: 4, z: 4 (z_hi: 2, z_lo: 2; z = z_hi * 2 + z_lo), core: 2. Of those that a mesh axis runs over, the one named last changes fastest.
Arguments:
- saved_last: bfloat16 [16, 4, 8, 21, 21, 384], P('sec', None, 'img'), may hold values from -6 to 6
- saved_older: bfloat16 [16, 4, 8, 21, 21, 384], P('sec', None, 'img'), may hold values from -6 to 6
- arriving: bfloat16 [16, 2, 8, 21, 21, 384], P('sec', None, 'img'), may hold values from -6 to 6
- head_adjoint: bfloat16 [3, 2, 8, 21, 21, 384], P(None, None, 'img'), may hold values from -6 to 6
- plan: int32 [16, 4], P('sec'), may hold values from 0 to 3, each once within a row
- depth_five: bfloat16 [16, 25, 384], P('sec'), may hold values from -1.25 to 1.25
- depth_three: bfloat16 [16, 9, 384], P('sec'), may hold values from -2 to 2
- point_five: bfloat16 [16, 384, 384], P('sec'), may hold values from -0.3125 to 0.3125
- point_three: bfloat16 [16, 384, 384], P('sec'), may hold values from -0.3125 to 0.3125
Outputs:
- outgoing: bfloat16 [16, 2, 8, 21, 21, 384], P('sec', None, 'img')
- grad_point_five: float32 [16, 384, 384], P('sec', 'img')
- grad_depth_five: float32 [16, 384, 25], P('sec', 'img')
- grad_point_three: float32 [16, 384, 384], P('sec', 'img')
- grad_depth_three: float32 [16, 384, 9], P('sec', 'img')
The draws below stay inside these ranges and needn't reach their ends.
Inputs may be any that keep to these rules, and one draw needn't show every extreme that they name: `plan`: each row is a permutation of the stash slots.
All inputs are finite; a program needn't handle non-finite values.
Results may differ from the reference program's by a relative error of at most 0.012.
Values may be sent and summed in bfloat16 or wider, within the bound.
No kernel may reach another device: no remote copies, remote signals or barrier semaphores. Data moves between devices by JAX's collectives and lax.ppermute only.
A program may use at most 128 MiB of HBM per device.

```python
import jax
import jax.numpy as jnp
from jax import lax

C = 384
HGT = 21
WID = 21
KFIVE = 5
KTHREE = 3
STEPS = 4
IMAGES = 8
CELLS = 16


def block_scale(own_key, dims, pieces, low, high):
    level, own = 1.0, jax.random.fold_in(own_key, 6)
    for dim, blocks in pieces:
        steps = jnp.exp(jax.random.uniform(jax.random.fold_in(own, dim), (blocks,), jnp.float32, low / len(pieces), high / len(pieces)))
        level = level * jnp.repeat(steps, dims[dim] // blocks).reshape([-1 if axis == dim else 1 for axis in range(len(dims))])
    return level


def bell_draw(rng, shape, scale, reach, split=(), dtype=jnp.bfloat16):
    drawn = scale * jax.random.normal(rng, shape, jnp.float32)
    if split:
        drawn = drawn * block_scale(rng, shape, split, -0.22, 0.18)
    return jnp.clip(drawn, -reach, reach).astype(dtype)


def setup_inputs(seed: int = 0) -> dict:
    keys = jax.random.split(jax.random.key(seed), 10)
    return {
        "saved_last": bell_draw(keys[0], (CELLS, STEPS, IMAGES, HGT, WID, C), 1.0, 6.0, ((0, 16), (2, 8))),
        "saved_older": bell_draw(keys[1], (CELLS, STEPS, IMAGES, HGT, WID, C), 1.0, 6.0, ((0, 16), (2, 8))),
        "arriving": bell_draw(keys[2], (CELLS, 2, IMAGES, HGT, WID, C), 1.0, 6.0, ((0, 16), (2, 8))),
        "head_adjoint": bell_draw(keys[3], (STEPS - 1, 2, IMAGES, HGT, WID, C), 1.0, 6.0, ((2, 8),)),
        "plan": jax.vmap(lambda own: jax.random.permutation(own, STEPS))(jax.random.split(keys[4], CELLS)).reshape((CELLS, STEPS)).astype(jnp.int32),
        "depth_five": bell_draw(keys[5], (CELLS, KFIVE * KFIVE, C), (KFIVE * KFIVE) ** -0.5, 1.25, ((0, 16),)),
        "depth_three": bell_draw(keys[6], (CELLS, KTHREE * KTHREE, C), (KTHREE * KTHREE) ** -0.5, 2.0, ((0, 16),)),
        "point_five": bell_draw(keys[7], (CELLS, C, C), C ** -0.5, 0.3125, ((0, 16),)),
        "point_three": bell_draw(keys[8], (CELLS, C, C), C ** -0.5, 0.3125, ((0, 16),)),
    }


def depth_apply(active, taps, kernel):
    radius = kernel // 2
    height, breadth = active.shape[1], active.shape[2]
    padded = jnp.pad(active, ((0, 0), (radius, radius), (radius, radius), (0, 0)))
    summed = jnp.zeros(active.shape, jnp.float32)
    for row_tap in range(kernel):
        for col_tap in range(kernel):
            window = padded[:, row_tap:row_tap + height, col_tap:col_tap + breadth, :].astype(jnp.float32)
            summed = summed + taps[row_tap * kernel + col_tap].astype(jnp.float32) * window
    return summed


def depth_transpose(back, taps, kernel):
    radius = kernel // 2
    height, breadth = back.shape[1], back.shape[2]
    padded = jnp.pad(back, ((0, 0), (radius, radius), (radius, radius), (0, 0)))
    summed = jnp.zeros(back.shape, jnp.float32)
    for row_tap in range(kernel):
        for col_tap in range(kernel):
            first_row = 2 * radius - row_tap
            first_col = 2 * radius - col_tap
            window = padded[:, first_row:first_row + height, first_col:first_col + breadth, :]
            summed = summed + taps[row_tap * kernel + col_tap].astype(jnp.float32) * window
    return summed


def depth_taps(active, back, kernel):
    radius = kernel // 2
    height, breadth = active.shape[1], active.shape[2]
    padded = jnp.pad(active, ((0, 0), (radius, radius), (radius, radius), (0, 0)))
    columns = []
    for row_tap in range(kernel):
        for col_tap in range(kernel):
            window = padded[:, row_tap:row_tap + height, col_tap:col_tap + breadth, :].astype(jnp.float32)
            columns.append(jnp.sum(window * back, axis=(0, 1, 2)))
    return jnp.stack(columns, 0)


def cell_backward(last_in, older_in, grad_out, grad_pass, taps_five, taps_three, weight_five, weight_three):
    channels = last_in.shape[3]
    pixels = last_in.shape[0] * last_in.shape[1] * last_in.shape[2]
    factor = 1.0 / (last_in.shape[1] * last_in.shape[2])
    active_last = jax.nn.relu(last_in)
    active_older = jax.nn.relu(older_in)
    mixed_five = depth_apply(active_last, taps_five, 5).astype(jnp.bfloat16)
    mixed_three = depth_apply(active_older, taps_three, 3).astype(jnp.bfloat16)
    flat_grad = grad_out.reshape(pixels, channels)
    back_five = jnp.dot(flat_grad, weight_five.T, preferred_element_type=jnp.float32).reshape(last_in.shape)
    back_three = jnp.dot(flat_grad, weight_three.T, preferred_element_type=jnp.float32).reshape(last_in.shape)
    through_five = depth_transpose(back_five, taps_five, 5)
    grad_last = (grad_pass.astype(jnp.float32) + grad_out.astype(jnp.float32)
                 + jnp.where(last_in > 0, through_five, 0.0)).astype(jnp.bfloat16)
    grad_older = jnp.where(older_in > 0, depth_transpose(back_three, taps_three, 3), 0.0).astype(jnp.bfloat16)
    point_grad_five = jnp.dot(mixed_five.reshape(pixels, channels).T, flat_grad, preferred_element_type=jnp.float32)
    point_grad_three = jnp.dot(mixed_three.reshape(pixels, channels).T, flat_grad, preferred_element_type=jnp.float32)
    taps_grad_five = depth_taps(active_last, back_five, 5)
    taps_grad_three = depth_taps(active_older, back_three, 3)
    grads_five = jnp.concatenate([point_grad_five, taps_grad_five.T], 1) * factor
    grads_three = jnp.concatenate([point_grad_three, taps_grad_three.T], 1) * factor
    return grad_last, grad_older, grads_five, grads_three


def reference(saved_last, saved_older, arriving, head_adjoint, plan, depth_five, depth_three, point_five, point_three):
    sections = saved_last.shape[0]
    turns = saved_last.shape[1]
    channels = saved_last.shape[5]
    totals_five = jnp.zeros((sections, channels, channels + 25), jnp.float32)
    totals_three = jnp.zeros((sections, channels, channels + 9), jnp.float32)
    pairs = arriving
    for turn_index in range(turns):
        if turn_index > 0:
            pairs = jnp.concatenate([pairs[1:], head_adjoint[turn_index - 1][None]], 0)

        def one_section(inputs):
            stash_last, stash_older, slot_index, adjoint_pair, taps_five, taps_three, weight_five, weight_three = inputs
            last_in = lax.dynamic_index_in_dim(stash_last, slot_index, 0, keepdims=False)
            older_in = lax.dynamic_index_in_dim(stash_older, slot_index, 0, keepdims=False)
            grad_last, grad_older, grads_five, grads_three = cell_backward(
                last_in, older_in, adjoint_pair[0], adjoint_pair[1], taps_five, taps_three, weight_five, weight_three)
            return jnp.stack([grad_last, grad_older], 0), grads_five, grads_three

        pairs, grads_five, grads_three = lax.map(one_section, (
            saved_last, saved_older, plan[:, turn_index], pairs, depth_five, depth_three, point_five, point_three))
        totals_five = totals_five + grads_five
        totals_three = totals_three + grads_three
    return (pairs, totals_five[:, :, :channels], totals_five[:, :, channels:],
            totals_three[:, :, :channels], totals_three[:, :, channels:])
```

```python
import functools

import jax
import jax.numpy as jnp
from jax import lax
from jax.experimental import pallas as pl
from jax.experimental.pallas import tpu as pltpu
from jax.sharding import PartitionSpec as P

SIDE = 21
PIXELS = SIDE * SIDE
ROWS = 448
CH = 384
BLOCKS = CH // 128
PITCH = 24
EDGE = 8
PITCHED = EDGE + (SIDE + 4) * PITCH + 8
F32 = jnp.float32
BF16 = jnp.bfloat16


def from_next(block):
    size = lax.axis_size("sec")
    return lax.ppermute(block, "sec", [(i + 1, i) for i in range(size - 1)])


def lanes(c):
    return slice(c * 128, (c + 1) * 128)


def spread_taps(taps_ref, wide, count):
    for k in range(count):
        row = taps_ref[k : k + 1, :].astype(F32)
        for c in range(BLOCKS):
            wide[k, c] = jnp.broadcast_to(row[:, lanes(c)], (8, 128))


def clear_edges(pitched):
    top = EDGE + 2 * PITCH
    bottom = EDGE + (SIDE + 2) * PITCH
    for c in range(BLOCKS):
        pitched[c, 0:top, :] = jnp.zeros((top, 128), F32)
        pitched[c, bottom:PITCHED, :] = jnp.zeros((PITCHED - bottom, 128), F32)


def to_pitched(dense, pitched):
    inside = lax.broadcasted_iota(jnp.int32, (PITCH, 128), 0) < SIDE
    clear_edges(pitched)

    def row(i, carry):
        for c in range(BLOCKS):
            got = dense[c, pl.ds(i * SIDE, PITCH), :]
            at = pl.multiple_of(EDGE + (i + 2) * PITCH, 8)
            pitched[c, pl.ds(at, PITCH), :] = jnp.where(inside, got, 0.0)
        return carry

    lax.fori_loop(0, SIDE, row, 0, unroll=3)


def spread_conv(pitched, wide, dense, kernel, flipped):
    radius = kernel // 2
    last = kernel * kernel - 1

    def group(g, carry):
        for c in range(BLOCKS):
            sums = [[None] * 3 for _ in range(3)]
            start = EDGE + (3 * g + 2 - radius) * PITCH
            for b in range(kernel + 2):
                for shift in range(-radius, 3 + radius):
                    got = pitched[c, pl.ds(start + b * PITCH + shift, 8, stride=3), :]
                    for a in range(3):
                        p = b - a
                        if p < 0 or p >= kernel:
                            continue
                        for r in range(3):
                            q = shift - r + radius
                            if q < 0 or q >= kernel:
                                continue
                            k = p * kernel + q
                            term = wide[last - k if flipped else k, c] * got
                            old = sums[a][r]
                            sums[a][r] = term if old is None else old + term
            for a in range(3):
                for r in range(3):
                    dense[c, pl.ds((3 * g + a) * SIDE + r, 8, stride=3), :] = sums[a][r]
        return carry

    lax.fori_loop(0, SIDE // 3, group, 0)


def tap_sums(back, active, sums_ref, kernel):
    radius = kernel // 2
    count = kernel * kernel
    for c in range(BLOCKS):

        def row(i, sums):
            sums = list(sums)
            here = EDGE + (i + 2) * PITCH
            centre = [back[c, pl.ds(here + r, 8, stride=3), :] for r in range(3)]
            for p in range(kernel):
                for shift in range(-radius, 3 + radius):
                    got = active[c, pl.ds(here + (p - radius) * PITCH + shift, 8, stride=3), :]
                    for r in range(3):
                        q = shift - r + radius
                        if 0 <= q < kernel:
                            sums[p * kernel + q] = sums[p * kernel + q] + got * centre[r]
            return tuple(sums)

        sums = lax.fori_loop(0, SIDE, row, tuple(jnp.zeros((8, 128), F32) for _ in range(count)))
        for k in range(count):
            sums_ref[k : k + 1, lanes(c)] = jnp.sum(sums[k], axis=0, keepdims=True)


def pieces(ref, width):
    whole = PIXELS // 16

    def read(i):
        return ref[pl.ds(i * 16, 16)]

    tail = jnp.concatenate(
        [ref[whole * 16 : PIXELS], jnp.zeros((16 - PIXELS % 16, width, CH), BF16)], 0
    )
    return whole, read, tail


def unpack(ref, width, put):
    whole, read, tail = pieces(ref, width)

    def body(i, carry):
        put(pl.multiple_of(i * 16, 16), jnp.swapaxes(read(i), 0, 1))
        return carry

    lax.fori_loop(0, whole, body, 0)
    put(whole * 16, jnp.swapaxes(tail, 0, 1))


def prepare_kernel(turn_ref, last_ref, older_ref, arriving_ref, act_last, act_older, pair):
    for source, target in ((last_ref, act_last), (older_ref, act_older)):

        def put(at, block, target=target):
            block = jnp.maximum(block, 0)
            for k in range(4):
                target[turn_ref[k], pl.ds(at, 16), :] = block[k]

        unpack(source, 4, put)

    def put_pair(at, block):
        pair[:, pl.ds(at, 16), :] = block

    unpack(arriving_ref, 2, put_pair)


def dense_product(left, weight_ref, dense):
    for c in range(BLOCKS):
        dense[c, 0:ROWS, :] = lax.dot_general(
            left, weight_ref[lanes(c), :], (((1,), (1,)), ((), ())), preferred_element_type=F32
        )


def step_kernel(first, final, *refs):
    refs = list(refs)
    if first:
        pair_ref = refs.pop(0)
        grad_out, grad_pass = pair_ref.at[0], pair_ref.at[1]
    else:
        top_ref, out_in, pass_in, head_ref = refs[:4]
        refs = refs[4:]
    last_ref, older_ref, weight_five, weight_three, taps_five, taps_three = refs[:6]
    refs = refs[6:]
    if final:
        outgoing = refs.pop(0)
    else:
        grad_last, grad_older = refs[:2]
        refs = refs[2:]
    back_five, back_three = refs[:2]
    refs = refs[2:]
    if not first:
        grad_out = refs.pop(0)
    wide_five, wide_three, dense, dense_three, chosen_pass = refs
    if not first:
        grad_pass = chosen_pass

        @pl.when(top_ref[0] == 1)
        def _():
            def put(at, block):
                grad_out[pl.ds(at, 16), :] = block[0]
                grad_pass[pl.ds(at, 16), :] = block[1]

            unpack(head_ref, 2, put)

        @pl.when(top_ref[0] != 1)
        def _():
            grad_out[...] = out_in[...]
            grad_pass[...] = pass_in[...]

    spread_taps(taps_five, wide_five, 25)
    spread_taps(taps_three, wide_three, 9)
    left = grad_out[...]
    dense_product(left, weight_three, dense)
    to_pitched(dense, back_three)
    spread_conv(back_three, wide_three, dense_three, 3, True)
    dense_product(left, weight_five, dense)
    to_pitched(dense, back_five)
    spread_conv(back_five, wide_five, dense, 5, True)

    def finish(i, carry):
        at = pl.multiple_of(i * 16, 16)
        for c in range(BLOCKS):
            spot = (pl.ds(at, 16), lanes(c))
            older = jnp.where(older_ref[spot].astype(F32) > 0, dense_three[c, pl.ds(at, 16), :], 0.0)
            through = jnp.where(last_ref[spot].astype(F32) > 0, dense[c, pl.ds(at, 16), :], 0.0)
            last = grad_pass[spot].astype(F32) + grad_out[spot].astype(F32) + through
            if final:
                both = jnp.stack([last.astype(BF16), older.astype(BF16)], 0)
                outgoing[pl.ds(at, 16), :, lanes(c)] = jnp.swapaxes(both, 0, 1)
            else:
                grad_last[spot] = last.astype(BF16)
                grad_older[spot] = older.astype(BF16)
        return carry

    if final:
        lax.fori_loop(0, PIXELS // 16, finish, 0)
        at = PIXELS // 16 * 16
        for c in range(BLOCKS):
            spot = (slice(at, at + 16), lanes(c))
            older = jnp.where(older_ref[spot].astype(F32) > 0, dense_three[c, at : at + 16, :], 0.0)
            through = jnp.where(last_ref[spot].astype(F32) > 0, dense[c, at : at + 16, :], 0.0)
            last = grad_pass[spot].astype(F32) + grad_out[spot].astype(F32) + through
            both = jnp.stack([last.astype(BF16), older.astype(BF16)], 0)
            outgoing[at:PIXELS, :, lanes(c)] = jnp.swapaxes(both, 0, 1)[: PIXELS - at]
    else:
        lax.fori_loop(0, ROWS // 16, finish, 0)


def mix_kernel(act, taps, mixed, pitched, dense, wide, kernel):
    def widen(i, carry):
        at = pl.multiple_of(i * 16, 16)
        for c in range(BLOCKS):
            dense[c, pl.ds(at, 16), :] = act[pl.ds(at, 16), lanes(c)].astype(F32)
        return carry

    lax.fori_loop(0, ROWS // 16, widen, 0)
    to_pitched(dense, pitched)
    spread_taps(taps, wide, kernel * kernel)
    for c in range(BLOCKS):
        dense[c, ROWS - 8 : ROWS, :] = jnp.zeros((8, 128), F32)
    spread_conv(pitched, wide, dense, kernel, False)

    def narrow(i, carry):
        at = pl.multiple_of(i * 16, 16)
        for c in range(BLOCKS):
            mixed[pl.ds(at, 16), lanes(c)] = dense[c, pl.ds(at, 16), :].astype(BF16)
        return carry

    lax.fori_loop(0, ROWS // 16, narrow, 0)


def grads_kernel(first, *refs):
    refs = list(refs)
    grad_out, last_ref, older_ref, taps_five, taps_three, back_five, back_three = refs[:7]
    refs = refs[7:]
    olds = None
    if not first:
        olds = refs[:4]
        refs = refs[4:]
    sums = refs[:4]
    pitched, dense, wide, mixed = refs[4:]
    left = grad_out[0] if first else grad_out[...]
    for which, act, taps, back, kernel in (
        (0, last_ref, taps_five, back_five, 5),
        (2, older_ref, taps_three, back_three, 3),
    ):
        mix_kernel(act, taps, mixed, pitched, dense, wide, kernel)
        got = lax.dot_general(
            mixed[...], left, (((0,), (0,)), ((), ())), preferred_element_type=F32
        )
        sums[which][...] = got if first else got + olds[which][...]
        tap_sums(back, pitched, sums[which + 1], kernel)
        if not first:
            sums[which + 1][...] = sums[which + 1][...] + olds[which + 1][...]


def in_vmem():
    return pl.BlockSpec(memory_space=pltpu.VMEM)


def in_smem():
    return pl.BlockSpec(memory_space=pltpu.SMEM)


def picked(t):
    return pl.BlockSpec((None, ROWS, CH), lambda i: (t, 0, 0))


def whole(shape):
    zeros = (0,) * len(shape)
    return pl.BlockSpec(shape, lambda i: zeros)


PARAMS = pltpu.CompilerParams(vmem_limit_bytes=48 << 20)
FLAT = jax.ShapeDtypeStruct((ROWS, CH), BF16)
BACK = jax.ShapeDtypeStruct((BLOCKS, PITCHED, 128), F32)
SUMS = (
    jax.ShapeDtypeStruct((CH, CH), F32),
    jax.ShapeDtypeStruct((32, CH), F32),
    jax.ShapeDtypeStruct((CH, CH), F32),
    jax.ShapeDtypeStruct((16, CH), F32),
)


def call_prepare(turns, last, older, arriving):
    return pl.pallas_call(
        prepare_kernel,
        out_shape=(
            jax.ShapeDtypeStruct((4, ROWS, CH), BF16),
            jax.ShapeDtypeStruct((4, ROWS, CH), BF16),
            jax.ShapeDtypeStruct((2, ROWS, CH), BF16),
        ),
        in_specs=[in_smem(), in_vmem(), in_vmem(), in_vmem()],
        out_specs=(in_vmem(), in_vmem(), in_vmem()),
        compiler_params=PARAMS,
        name="prepare",
    )(turns, last, older, arriving)


def call_step(t, turns, given, act_last, act_older, weights, taps):
    first, final = t == 0, t == turns - 1
    if first:
        specs = [whole((2, ROWS, CH))]
    else:
        specs = [
            in_smem(),
            whole((ROWS, CH)),
            whole((ROWS, CH)),
            pl.BlockSpec((None, PIXELS, 2, CH), lambda i: (t - 1, 0, 0, 0)),
        ]
    specs += [picked(t), picked(t), whole((CH, CH)), whole((CH, CH)), whole((25, CH)), whole((9, CH))]
    shapes = [jax.ShapeDtypeStruct((PIXELS, 2, CH), BF16)] if final else [FLAT, FLAT]
    shapes += [BACK, BACK]
    if not first:
        shapes += [FLAT]
    return pl.pallas_call(
        functools.partial(step_kernel, first, final),
        grid=(1,),
        out_shape=tuple(shapes),
        in_specs=specs,
        out_specs=tuple(whole(s.shape) for s in shapes),
        scratch_shapes=[
            pltpu.VMEM((25, BLOCKS, 8, 128), F32),
            pltpu.VMEM((9, BLOCKS, 8, 128), F32),
            pltpu.VMEM((BLOCKS, ROWS + 8, 128), F32),
            pltpu.VMEM((BLOCKS, ROWS + 8, 128), F32),
            pltpu.VMEM((ROWS, CH), BF16),
        ],
        compiler_params=PARAMS,
        name=f"step_{t}",
    )(*given, act_last, act_older, *weights, *taps)


def call_grads(t, grad_out, act_last, act_older, taps, backs, olds):
    first = t == 0
    specs = [whole((1, ROWS, CH)) if first else whole((ROWS, CH))]
    specs += [picked(t), picked(t), whole((25, CH)), whole((9, CH)), whole(BACK.shape), whole(BACK.shape)]
    if not first:
        specs += [whole(s.shape) for s in SUMS]
    return pl.pallas_call(
        functools.partial(grads_kernel, first),
        grid=(1,),
        out_shape=SUMS,
        in_specs=specs,
        out_specs=tuple(whole(s.shape) for s in SUMS),
        scratch_shapes=[
            pltpu.VMEM((BLOCKS, PITCHED, 128), F32),
            pltpu.VMEM((BLOCKS, ROWS + 8, 128), F32),
            pltpu.VMEM((25, BLOCKS, 8, 128), F32),
            pltpu.VMEM((ROWS, CH), BF16),
        ],
        compiler_params=PARAMS,
        name=f"grads_{t}",
    )(grad_out, act_last, act_older, *taps, *backs, *olds)


def by_pixel(stack):
    return jnp.transpose(stack, (0, 2, 3, 4, 1, 5)).reshape(PIXELS, stack.shape[1], CH)


def local(
    saved_last,
    saved_older,
    arriving,
    head_adjoint,
    plan,
    depth_five,
    depth_three,
    point_five,
    point_three,
):
    turns = saved_last.shape[1]
    top = (lax.axis_index("sec") == lax.axis_size("sec") - 1).astype(jnp.int32)[None]
    slots = lax.broadcasted_iota(jnp.int32, (turns, turns), 0)
    steps = lax.broadcasted_iota(jnp.int32, (turns, turns), 1)
    turn_of_slot = jnp.sum(jnp.where(plan == slots, steps, 0), axis=1)
    head = jnp.transpose(head_adjoint, (0, 2, 3, 4, 1, 5)).reshape(turns - 1, PIXELS, 2, CH)
    act_last, act_older, pair = call_prepare(
        turn_of_slot, by_pixel(saved_last), by_pixel(saved_older), by_pixel(arriving)
    )
    weights = (point_five[0], point_three[0])
    taps = (depth_five[0], depth_three[0])
    given = (pair,)
    sums = ()
    for t in range(turns):
        made = list(call_step(t, turns, given, act_last, act_older, weights, taps))
        if t < turns - 1:
            next_pass = from_next(made[1])
            next_out = from_next(made[0])
            made = made[2:]
        else:
            outgoing = made.pop(0)
        backs = made[:2]
        used = pair if t == 0 else made[2]
        sums = call_grads(t, used, act_last, act_older, taps, backs, sums)
        if t < turns - 1:
            given = (top, next_out, next_pass, head)
    scale = 1.0 / PIXELS
    tap_rows = jnp.concatenate([sums[1][:25], sums[3][:9]], 0).T
    packed = jnp.concatenate([sums[0], sums[2], tap_rows], 1) * scale
    packed = packed.astype(BF16)
    devices = lax.axis_size("img")
    packed = packed.reshape(devices, CH // devices, packed.shape[1])
    landed = lax.all_to_all(packed, "img", 0, 0, tiled=True)
    total = jnp.sum(landed.astype(F32), axis=0)[None]
    outgoing = outgoing.reshape(1, 1, SIDE, SIDE, 2, CH).transpose(0, 4, 1, 2, 3, 5)
    return (
        outgoing,
        total[:, :, :CH],
        total[:, :, 2 * CH : 2 * CH + 25],
        total[:, :, CH : 2 * CH],
        total[:, :, 2 * CH + 25 :],
    )


def solution(mesh):
    placed = (
        P("sec", None, "img", None, None, None),
        P("sec", None, "img", None, None, None),
        P("sec", None, "img", None, None, None),
        P(None, None, "img", None, None, None),
        P("sec", None),
        P("sec", None, None),
        P("sec", None, None),
        P("sec", None, None),
        P("sec", None, None),
    )
    return jax.shard_map(
        local,
        mesh=mesh,
        in_specs=placed,
        out_specs=(
            P("sec", None, "img", None, None, None),
            P("sec", "img", None),
            P("sec", "img", None),
            P("sec", "img", None),
            P("sec", "img", None),
        ),
        check_vma=False,
    )
```

```python
import functools

import jax
import jax.numpy as jnp
from jax import lax
from jax.experimental import pallas as pl
from jax.experimental.pallas import tpu as pltpu
from jax.sharding import PartitionSpec as P

SIDE = 21
PIXELS = SIDE * SIDE
ROWS = 448
CH = 384
BLOCKS = CH // 128
PITCH = 24
EDGE = 8
PITCHED = EDGE + (SIDE + 4) * PITCH + 8
F32 = jnp.float32
BF16 = jnp.bfloat16


def from_next(block):
    size = lax.axis_size("sec")
    return lax.ppermute(block, "sec", [(i + 1, i) for i in range(size - 1)])


def lanes(c):
    return slice(c * 128, (c + 1) * 128)


def spread_taps(taps_ref, wide, count):
    for k in range(count):
        row = taps_ref[k : k + 1, :].astype(F32)
        for c in range(BLOCKS):
            wide[k, c] = jnp.broadcast_to(row[:, lanes(c)], (8, 128))


def clear_edges(pitched):
    top = EDGE + 2 * PITCH
    bottom = EDGE + (SIDE + 2) * PITCH
    for c in range(BLOCKS):
        pitched[c, 0:top, :] = jnp.zeros((top, 128), F32)
        pitched[c, bottom:PITCHED, :] = jnp.zeros((PITCHED - bottom, 128), F32)


def to_pitched(dense, pitched):
    inside = lax.broadcasted_iota(jnp.int32, (PITCH, 128), 0) < SIDE
    clear_edges(pitched)

    def row(i, carry):
        for c in range(BLOCKS):
            got = dense[c, pl.ds(i * SIDE, PITCH), :]
            at = pl.multiple_of(EDGE + (i + 2) * PITCH, 8)
            pitched[c, pl.ds(at, PITCH), :] = jnp.where(inside, got, 0.0)
        return carry

    lax.fori_loop(0, SIDE, row, 0, unroll=3)


def spread_conv(pitched, wide, dense, kernel, flipped):
    radius = kernel // 2
    last = kernel * kernel - 1

    def group(g, carry):
        for c in range(BLOCKS):
            sums = [[None] * 3 for _ in range(3)]
            start = EDGE + (3 * g + 2 - radius) * PITCH
            for b in range(kernel + 2):
                for shift in range(-radius, 3 + radius):
                    got = pitched[c, pl.ds(start + b * PITCH + shift, 8, stride=3), :]
                    for a in range(3):
                        p = b - a
                        if p < 0 or p >= kernel:
                            continue
                        for r in range(3):
                            q = shift - r + radius
                            if q < 0 or q >= kernel:
                                continue
                            k = p * kernel + q
                            term = wide[last - k if flipped else k, c] * got
                            old = sums[a][r]
                            sums[a][r] = term if old is None else old + term
            for a in range(3):
                for r in range(3):
                    dense[c, pl.ds((3 * g + a) * SIDE + r, 8, stride=3), :] = sums[a][r]
        return carry

    lax.fori_loop(0, SIDE // 3, group, 0)


def tap_sums(back, active, sums_ref, kernel):
    radius = kernel // 2
    count = kernel * kernel
    for c in range(BLOCKS):

        def row(i, sums):
            sums = list(sums)
            here = EDGE + (i + 2) * PITCH
            centre = [back[c, pl.ds(here + r, 8, stride=3), :] for r in range(3)]
            for p in range(kernel):
                for shift in range(-radius, 3 + radius):
                    got = active[c, pl.ds(here + (p - radius) * PITCH + shift, 8, stride=3), :]
                    for r in range(3):
                        q = shift - r + radius
                        if 0 <= q < kernel:
                            sums[p * kernel + q] = sums[p * kernel + q] + got * centre[r]
            return tuple(sums)

        sums = lax.fori_loop(0, SIDE, row, tuple(jnp.zeros((8, 128), F32) for _ in range(count)))
        for k in range(count):
            sums_ref[k : k + 1, lanes(c)] = jnp.sum(sums[k], axis=0, keepdims=True)


def pieces(ref, width):
    whole = PIXELS // 16

    def read(i):
        return ref[pl.ds(i * 16, 16)]

    tail = jnp.concatenate(
        [ref[whole * 16 : PIXELS], jnp.zeros((16 - PIXELS % 16, width, CH), BF16)], 0
    )
    return whole, read, tail


def unpack(ref, width, put):
    whole, read, tail = pieces(ref, width)

    def body(i, carry):
        put(pl.multiple_of(i * 16, 16), jnp.swapaxes(read(i), 0, 1))
        return carry

    lax.fori_loop(0, whole, body, 0)
    put(whole * 16, jnp.swapaxes(tail, 0, 1))


def dense_product(left, weight_ref, dense):
    for c in range(BLOCKS):
        dense[c, 0:ROWS, :] = lax.dot_general(
            left, weight_ref[lanes(c), :], (((1,), (1,)), ((), ())), preferred_element_type=F32
        )


def masked(act, t, dense, c, rows):
    return jnp.where(act[t, rows, lanes(c)].astype(F32) > 0, dense[c, rows, :], 0.0)


def finish_older(act_older, t, dense, grad_older):
    def body(i, carry):
        rows = pl.ds(pl.multiple_of(i * 16, 16), 16)
        for c in range(BLOCKS):
            grad_older[rows, lanes(c)] = masked(act_older, t, dense, c, rows).astype(BF16)
        return carry

    lax.fori_loop(0, ROWS // 16, body, 0)


def last_piece(act_last, t, dense, grad_out, grad_pass, c, rows):
    skip = grad_pass[rows, lanes(c)].astype(F32) + grad_out[rows, lanes(c)].astype(F32)
    return (skip + masked(act_last, t, dense, c, rows)).astype(BF16)


def finish_last(act_last, t, dense, grad_out, grad_pass, grad_last):
    def body(i, carry):
        rows = pl.ds(pl.multiple_of(i * 16, 16), 16)
        for c in range(BLOCKS):
            grad_last[rows, lanes(c)] = last_piece(act_last, t, dense, grad_out, grad_pass, c, rows)
        return carry

    lax.fori_loop(0, ROWS // 16, body, 0)


def copies(pairs, sems):
    return [pltpu.make_async_copy(a, b, sems.at[n]) for n, (a, b) in enumerate(pairs)]


def relay(
    t,
    grad_out,
    grad_pass,
    act_last,
    act_older,
    weight_five,
    weight_three,
    taps_five,
    taps_three,
    back_five,
    back_three,
    made_last,
    made_older,
    wide_five,
    wide_three,
    dense,
    older_ready,
    last_ready,
):
    spread_taps(taps_five, wide_five, 25)
    spread_taps(taps_three, wide_three, 9)
    left = grad_out[...]
    dense_product(left, weight_three, dense)
    to_pitched(dense, back_three)
    spread_conv(back_three, wide_three, dense, 3, True)
    older_ready()
    finish_older(act_older, t, dense, made_older)
    dense_product(left, weight_five, dense)
    to_pitched(dense, back_five)
    spread_conv(back_five, wide_five, dense, 5, True)
    last_ready()
    finish_last(act_last, t, dense, grad_out, grad_pass, made_last)


def first_kernel(
    turn_ref,
    last_hbm,
    older_hbm,
    arriving_hbm,
    weight_five,
    weight_three,
    taps_five,
    taps_three,
    grad_last,
    grad_older,
    act_last,
    act_older,
    grad_out,
    back_five,
    back_three,
    last_in,
    older_in,
    arriving_in,
    grad_pass,
    wide_five,
    wide_three,
    dense,
    sems,
):
    half = 224
    gets = copies(
        [
            (arriving_hbm.at[0:half], arriving_in.at[0:half]),
            (arriving_hbm.at[half:], arriving_in.at[half:]),
            (older_hbm.at[0:half], older_in.at[0:half]),
            (older_hbm.at[half:], older_in.at[half:]),
            (last_hbm.at[0:half], last_in.at[0:half]),
            (last_hbm.at[half:], last_in.at[half:]),
        ],
        sems,
    )
    for get in gets:
        get.start()

    def put_pair(at, block):
        grad_out[pl.ds(at, 16), :] = block[0]
        grad_pass[pl.ds(at, 16), :] = block[1]

    gets[0].wait()
    gets[1].wait()
    unpack(arriving_in, 2, put_pair)

    def ready(one, two, source, target):
        def run():
            gets[one].wait()
            gets[two].wait()

            def put(at, block):
                block = jnp.maximum(block, 0)
                for k in range(4):
                    target[turn_ref[k], pl.ds(at, 16), :] = block[k]

            unpack(source, 4, put)

        return run

    relay(
        0,
        grad_out,
        grad_pass,
        act_last,
        act_older,
        weight_five,
        weight_three,
        taps_five,
        taps_three,
        back_five,
        back_three,
        grad_last,
        grad_older,
        wide_five,
        wide_three,
        dense,
        ready(2, 3, older_in, act_older),
        ready(4, 5, last_in, act_last),
    )


def take(t, top_ref, out_in, pass_in, head_hbm, grad_out, grad_pass, head_in, sem):
    @pl.when(top_ref[0] == 1)
    def _():
        get = pltpu.make_async_copy(head_hbm.at[t - 1], head_in, sem)
        get.start()
        get.wait()

        def put(at, block):
            grad_out[pl.ds(at, 16), :] = block[0]
            grad_pass[pl.ds(at, 16), :] = block[1]

        unpack(head_in, 2, put)

    @pl.when(top_ref[0] != 1)
    def _():
        grad_out[...] = out_in[...]
        grad_pass[...] = pass_in[...]


def middle_kernel(
    t,
    top_ref,
    out_in,
    pass_in,
    head_hbm,
    act_last,
    act_older,
    weight_five,
    weight_three,
    taps_five,
    taps_three,
    grad_last,
    grad_older,
    grad_out,
    back_five,
    back_three,
    head_in,
    grad_pass,
    wide_five,
    wide_three,
    dense,
    sem,
):
    take(t, top_ref, out_in, pass_in, head_hbm, grad_out, grad_pass, head_in, sem)
    relay(
        t,
        grad_out,
        grad_pass,
        act_last,
        act_older,
        weight_five,
        weight_three,
        taps_five,
        taps_three,
        back_five,
        back_three,
        grad_last,
        grad_older,
        wide_five,
        wide_three,
        dense,
        lambda: None,
        lambda: None,
    )


def widened(act, t, dense):
    def body(i, carry):
        rows = pl.ds(pl.multiple_of(i * 16, 16), 16)
        for c in range(BLOCKS):
            dense[c, rows, :] = act[t, rows, lanes(c)].astype(F32)
        return carry

    lax.fori_loop(0, ROWS // 16, body, 0)


def mix(act, t, taps, mixed, pitched, dense, wide, kernel):
    widened(act, t, dense)
    to_pitched(dense, pitched)
    spread_taps(taps, wide, kernel * kernel)
    for c in range(BLOCKS):
        dense[c, ROWS - 8 : ROWS, :] = jnp.zeros((8, 128), F32)
    spread_conv(pitched, wide, dense, kernel, False)

    def body(i, carry):
        rows = pl.ds(pl.multiple_of(i * 16, 16), 16)
        for c in range(BLOCKS):
            mixed[rows, lanes(c)] = dense[c, rows, :].astype(BF16)
        return carry

    lax.fori_loop(0, ROWS // 16, body, 0)


def across(mixed, left):
    return lax.dot_general(mixed, left, (((0,), (0,)), ((), ())), preferred_element_type=F32)


def grads_kernel(t, ahead, *refs):
    refs = list(refs)
    grad_out, act_last, act_older, taps_five, taps_three, back_five, back_three = refs[:7]
    refs = refs[7:]
    olds = None
    if t > 0:
        olds = refs[:4]
        refs = refs[4:]
    sums = refs[:4]
    refs = refs[4:]
    if ahead is not None:
        later = refs[:2]
        refs = refs[2:]
    pitched, dense, wide, mixed = refs
    left = grad_out[...]
    for n, (act, taps, back, kernel) in enumerate(
        ((act_last, taps_five, back_five, 5), (act_older, taps_three, back_three, 3))
    ):
        if ahead is not None:
            mix(act, ahead, taps, later[n], pitched, dense, wide, kernel)
        mix(act, t, taps, mixed, pitched, dense, wide, kernel)
        got = across(mixed[...], left)
        sums[2 * n][...] = got if olds is None else got + olds[2 * n][...]
        tap_sums(back, pitched, sums[2 * n + 1], kernel)
        if olds is not None:
            sums[2 * n + 1][...] = sums[2 * n + 1][...] + olds[2 * n + 1][...]


def last_grads_kernel(
    t,
    top_ref,
    out_in,
    pass_in,
    head_hbm,
    act_last,
    act_older,
    weight_five,
    weight_three,
    mixed_five,
    mixed_three,
    old_five,
    old_taps_five,
    old_three,
    old_taps_three,
    packed_hbm,
    out_hbm,
    pass_hbm,
    back_five_hbm,
    back_three_hbm,
    last_hbm,
    older_hbm,
    packed,
    grad_out,
    grad_pass,
    back_five,
    back_three,
    head_in,
    pitched,
    dense,
    rows_ref,
    sems,
):
    scale = 1.0 / PIXELS
    keep = copies(
        [
            (act_last.at[t], last_hbm),
            (act_older.at[t], older_hbm),
            (grad_out, out_hbm),
            (grad_pass, pass_hbm),
            (back_five, back_five_hbm),
            (back_three, back_three_hbm),
        ],
        sems,
    )
    points, columns = copies(
        [
            (packed.at[:, pl.ds(0, 2 * CH)], packed_hbm.at[:, pl.ds(0, 2 * CH)]),
            (packed.at[:, pl.ds(2 * CH, 128)], packed_hbm.at[:, pl.ds(2 * CH, 128)]),
        ],
        sems.at[pl.ds(6, 2)],
    )
    keep[0].start()
    keep[1].start()
    take(t, top_ref, out_in, pass_in, head_hbm, grad_out, grad_pass, head_in, sems.at[8])
    keep[2].start()
    keep[3].start()
    left = grad_out[...]
    packed[:, 0:CH] = ((across(mixed_five[...], left) + old_five[...]) * scale).astype(BF16)
    packed[:, CH : 2 * CH] = ((across(mixed_three[...], left) + old_three[...]) * scale).astype(BF16)
    points.start()
    rows_ref[...] = jnp.zeros(rows_ref.shape, F32)
    for act, weight, back, old, at, kernel, kept in (
        (act_last, weight_five, back_five, old_taps_five, 0, 5, keep[4]),
        (act_older, weight_three, back_three, old_taps_three, 32, 3, keep[5]),
    ):
        dense_product(left, weight, dense)
        to_pitched(dense, back)
        kept.start()
        widened(act, t, dense)
        to_pitched(dense, pitched)
        count = kernel * kernel
        tap_sums(back, pitched, rows_ref.at[pl.ds(at, old.shape[0])], kernel)
        rows_ref[at : at + count, :] = (rows_ref[at : at + count, :] + old[0:count, :]) * scale
    for c in range(BLOCKS):
        packed[lanes(c), 2 * CH : 2 * CH + 128] = rows_ref[:, lanes(c)].T.astype(BF16)
    columns.start()
    for copy in keep:
        copy.wait()
    points.wait()
    columns.wait()


def last_kernel(
    grad_out_hbm,
    grad_pass_hbm,
    back_five_hbm,
    back_three_hbm,
    act_last_hbm,
    act_older_hbm,
    taps_five,
    taps_three,
    outgoing_hbm,
    grad_out,
    grad_pass,
    back_five,
    back_three,
    act_last,
    act_older,
    wide_five,
    wide_three,
    dense,
    made_older,
    outgoing,
    sems,
):
    gets = copies(
        [
            (back_three_hbm, back_three),
            (act_older_hbm, act_older.at[0]),
            (back_five_hbm, back_five),
            (act_last_hbm, act_last.at[0]),
            (grad_out_hbm, grad_out),
            (grad_pass_hbm, grad_pass),
        ],
        sems,
    )
    for get in gets:
        get.start()
    spread_taps(taps_five, wide_five, 25)
    spread_taps(taps_three, wide_three, 9)
    gets[0].wait()
    spread_conv(back_three, wide_three, dense, 3, True)
    gets[1].wait()
    finish_older(act_older, 0, dense, made_older)
    gets[2].wait()
    spread_conv(back_five, wide_five, dense, 5, True)
    for get in gets[3:]:
        get.wait()

    def both(rows, c):
        last = last_piece(act_last, 0, dense, grad_out, grad_pass, c, rows)
        return jnp.swapaxes(jnp.stack([last, made_older[rows, lanes(c)]], 0), 0, 1)

    def body(i, carry):
        rows = pl.ds(pl.multiple_of(i * 16, 16), 16)
        for c in range(BLOCKS):
            outgoing[rows, :, lanes(c)] = both(rows, c)
        return carry

    half = 224
    lax.fori_loop(0, half // 16, body, 0)
    put = copies(
        [
            (outgoing.at[pl.ds(0, half)], outgoing_hbm.at[pl.ds(0, half)]),
            (outgoing.at[pl.ds(half, PIXELS - half)], outgoing_hbm.at[pl.ds(half, PIXELS - half)]),
        ],
        sems.at[pl.ds(6, 2)],
    )
    put[0].start()
    lax.fori_loop(half // 16, PIXELS // 16, body, 0)
    at = PIXELS // 16 * 16
    for c in range(BLOCKS):
        outgoing[at:PIXELS, :, lanes(c)] = both(slice(at, at + 16), c)[: PIXELS - at]
    put[1].start()
    put[0].wait()
    put[1].wait()


def total_kernel(landed, five, three, taps):
    def summed(columns):
        total = landed[0, :, columns].astype(F32)
        for n in range(1, landed.shape[0]):
            total = total + landed[n, :, columns].astype(F32)
        return total

    five[...] = summed(slice(0, CH))
    three[...] = summed(slice(CH, 2 * CH))
    taps[...] = summed(slice(2 * CH, 2 * CH + 128)).T


VMEM = pl.BlockSpec(memory_space=pltpu.VMEM)
SMEM = pl.BlockSpec(memory_space=pltpu.SMEM)
ANY = pl.BlockSpec(memory_space=pl.ANY)
ALONE = 16 << 20
OPENING = 32 << 20
FLAT = jax.ShapeDtypeStruct((ROWS, CH), BF16)
PACKED = jax.ShapeDtypeStruct((CH, 2 * CH + 128), BF16)
ACTS = jax.ShapeDtypeStruct((4, ROWS, CH), BF16)
BACK = jax.ShapeDtypeStruct((BLOCKS, PITCHED, 128), F32)
SUMS = (
    jax.ShapeDtypeStruct((CH, CH), F32),
    jax.ShapeDtypeStruct((32, CH), F32),
    jax.ShapeDtypeStruct((CH, CH), F32),
    jax.ShapeDtypeStruct((16, CH), F32),
)
FLAT_SCRATCH = pltpu.VMEM((ROWS, CH), BF16)
PAIR_SCRATCH = pltpu.VMEM((PIXELS, 2, CH), BF16)
WIDE_FIVE = pltpu.VMEM((25, BLOCKS, 8, 128), F32)
WIDE_THREE = pltpu.VMEM((9, BLOCKS, 8, 128), F32)
DENSE = pltpu.VMEM((BLOCKS, ROWS + 8, 128), F32)
PITCHED_SCRATCH = pltpu.VMEM((BLOCKS, PITCHED, 128), F32)


def run(kernel, name, operands, specs, shapes, out_specs, scratch, micros, limit=12 << 20):
    cost = pl.CostEstimate(flops=int(micros * 1e9), bytes_accessed=0, transcendentals=0)
    return pl.pallas_call(
        kernel,
        out_shape=tuple(shapes),
        in_specs=specs,
        out_specs=tuple(out_specs),
        scratch_shapes=scratch,
        compiler_params=pltpu.CompilerParams(vmem_limit_bytes=limit),
        cost_estimate=cost,
        name=name,
    )(*operands)


def call_first(turns, last, older, arriving, weights, taps):
    return run(
        first_kernel,
        "first",
        (turns, last, older, arriving, *weights, *taps),
        [SMEM, ANY, ANY, ANY] + [VMEM] * 4,
        (FLAT, FLAT, ACTS, ACTS, FLAT, BACK, BACK),
        (VMEM,) * 7,
        [
            pltpu.VMEM((PIXELS, 4, CH), BF16),
            pltpu.VMEM((PIXELS, 4, CH), BF16),
            PAIR_SCRATCH,
            FLAT_SCRATCH,
            WIDE_FIVE,
            WIDE_THREE,
            DENSE,
            pltpu.SemaphoreType.DMA((6,)),
        ],
        8,
        OPENING,
    )


def call_middle(t, given, acts, weights, taps):
    return run(
        functools.partial(middle_kernel, t),
        f"middle_{t}",
        (*given, *acts, *weights, *taps),
        [SMEM, VMEM, VMEM, ANY] + [VMEM] * 6,
        (FLAT, FLAT, FLAT, BACK, BACK),
        (VMEM,) * 5,
        [
            PAIR_SCRATCH,
            FLAT_SCRATCH,
            WIDE_FIVE,
            WIDE_THREE,
            DENSE,
            pltpu.SemaphoreType.DMA,
        ],
        5,
    )


def call_grads(t, ahead, grad_out, acts, taps, backs, olds):
    shapes = SUMS if ahead is None else SUMS + (FLAT, FLAT)
    operands = (grad_out, *acts, *taps, *backs, *olds)
    return run(
        functools.partial(grads_kernel, t, ahead),
        f"grads_{t}",
        operands,
        [VMEM] * len(operands),
        shapes,
        (VMEM,) * len(shapes),
        [PITCHED_SCRATCH, DENSE, WIDE_FIVE, FLAT_SCRATCH],
        6 if ahead is None else 8,
    )


def call_last_grads(t, given, acts, weights, mixed, olds):
    return run(
        functools.partial(last_grads_kernel, t),
        "last_grads",
        (*given, *acts, *weights, *mixed, *olds),
        [SMEM, VMEM, VMEM, ANY] + [VMEM] * 10,
        (PACKED, FLAT, FLAT, BACK, BACK, FLAT, FLAT),
        (ANY,) * 7,
        [
            pltpu.VMEM(PACKED.shape, BF16),
            FLAT_SCRATCH,
            FLAT_SCRATCH,
            PITCHED_SCRATCH,
            PITCHED_SCRATCH,
            PAIR_SCRATCH,
            PITCHED_SCRATCH,
            DENSE,
            pltpu.VMEM((128, CH), F32),
            pltpu.SemaphoreType.DMA((9,)),
        ],
        6,
        ALONE,
    )


def call_last(kept, taps):
    (outgoing,) = run(
        last_kernel,
        "last",
        (*kept, *taps),
        [ANY] * 6 + [VMEM] * 2,
        (jax.ShapeDtypeStruct((PIXELS, 2, CH), BF16),),
        (ANY,),
        [
            FLAT_SCRATCH,
            FLAT_SCRATCH,
            PITCHED_SCRATCH,
            PITCHED_SCRATCH,
            pltpu.VMEM((1, ROWS, CH), BF16),
            pltpu.VMEM((1, ROWS, CH), BF16),
            WIDE_FIVE,
            WIDE_THREE,
            DENSE,
            FLAT_SCRATCH,
            PAIR_SCRATCH,
            pltpu.SemaphoreType.DMA((8,)),
        ],
        4,
    )
    return outgoing


def call_total(landed):
    rows = landed.shape[1]
    shapes = [(rows, CH), (rows, CH), (128, rows)]
    return pl.pallas_call(
        total_kernel,
        grid=(1,),
        out_shape=tuple(jax.ShapeDtypeStruct(shape, F32) for shape in shapes),
        in_specs=[pl.BlockSpec(landed.shape, lambda i: (0, 0, 0))],
        out_specs=tuple(pl.BlockSpec(shape, lambda i: (0, 0)) for shape in shapes),
        compiler_params=pltpu.CompilerParams(vmem_limit_bytes=12 << 20),
        name="total",
    )(landed)


def by_pixel(stack):
    return jnp.transpose(stack, (0, 2, 3, 4, 1, 5)).reshape(PIXELS, stack.shape[1], CH)


def local(
    saved_last,
    saved_older,
    arriving,
    head_adjoint,
    plan,
    depth_five,
    depth_three,
    point_five,
    point_three,
):
    turns = saved_last.shape[1]
    top = (lax.axis_index("sec") == lax.axis_size("sec") - 1).astype(jnp.int32)[None]
    slots = lax.broadcasted_iota(jnp.int32, (turns, turns), 0)
    steps = lax.broadcasted_iota(jnp.int32, (turns, turns), 1)
    turn_of_slot = jnp.sum(jnp.where(plan == slots, steps, 0), axis=1)
    turn_of_slot, top = lax.optimization_barrier((turn_of_slot, top))
    head = jnp.transpose(head_adjoint, (0, 2, 3, 4, 1, 5)).reshape(turns - 1, PIXELS, 2, CH)
    weights = (point_five[0], point_three[0])
    taps = (depth_five[0], depth_three[0])
    grad_last, grad_older, act_last, act_older, grad_out, *backs = call_first(
        turn_of_slot,
        by_pixel(saved_last),
        by_pixel(saved_older),
        by_pixel(arriving),
        weights,
        taps,
    )
    acts = (act_last, act_older)
    sums = ()
    for t in range(turns - 1):
        next_pass = from_next(grad_older)
        next_out = from_next(grad_last)
        ahead = turns - 1 if t == turns - 2 else None
        made = call_grads(t, ahead, grad_out, acts, taps, backs, sums)
        next_out, next_pass, made = lax.optimization_barrier((next_out, next_pass, made))
        sums = made[:4]
        given = (top, next_out, next_pass, head)
        if t < turns - 2:
            grad_last, grad_older, grad_out, *backs = call_middle(t + 1, given, acts, weights, taps)
    packed, *kept = call_last_grads(
        turns - 1, given, acts, weights, made[4:], sums
    )
    devices = lax.axis_size("img")
    packed = packed.reshape(devices, CH // devices, packed.shape[1])
    landed = lax.all_to_all(packed, "img", 0, 0, tiled=True)
    outgoing = call_last(kept, taps)
    five, three, tap_rows = call_total(landed)
    outgoing = outgoing.reshape(1, 1, SIDE, SIDE, 2, CH).transpose(0, 4, 1, 2, 3, 5)
    return (
        outgoing,
        five[None],
        tap_rows[:25].T[None],
        three[None],
        tap_rows[32:41].T[None],
    )


def solution(mesh):
    placed = (
        P("sec", None, "img", None, None, None),
        P("sec", None, "img", None, None, None),
        P("sec", None, "img", None, None, None),
        P(None, None, "img", None, None, None),
        P("sec", None),
        P("sec", None, None),
        P("sec", None, None),
        P("sec", None, None),
        P("sec", None, None),
    )
    return jax.shard_map(
        local,
        mesh=mesh,
        in_specs=placed,
        out_specs=(
            P("sec", None, "img", None, None, None),
            P("sec", "img", None),
            P("sec", "img", None),
            P("sec", "img", None),
            P("sec", "img", None),
        ),
        check_vma=False,
    )
```

```python
import functools

import jax
import jax.numpy as jnp
from jax import lax
from jax.experimental import pallas as pl
from jax.experimental.pallas import tpu as pltpu
from jax.sharding import PartitionSpec as P

SIDE = 21
PIXELS = SIDE * SIDE
ROWS = 448
CH = 384
BLOCKS = CH // 128
PITCH = 24
EDGE = 8
PITCHED = EDGE + (SIDE + 4) * PITCH + 8
F32 = jnp.float32
BF16 = jnp.bfloat16


def from_next(block):
    size = lax.axis_size("sec")
    return lax.ppermute(block, "sec", [(i + 1, i) for i in range(size - 1)])


def lanes(c):
    return slice(c * 128, (c + 1) * 128)


def spread_taps(taps_ref, wide, count):
    for k in range(count):
        row = taps_ref[k : k + 1, :].astype(F32)
        for c in range(BLOCKS):
            wide[k, c] = jnp.broadcast_to(row[:, lanes(c)], (8, 128))


def clear_edges(pitched):
    top = EDGE + 2 * PITCH
    bottom = EDGE + (SIDE + 2) * PITCH
    for c in range(BLOCKS):
        pitched[c, 0:top, :] = jnp.zeros((top, 128), F32)
        pitched[c, bottom:PITCHED, :] = jnp.zeros((PITCHED - bottom, 128), F32)


def to_pitched(dense, pitched):
    inside = lax.broadcasted_iota(jnp.int32, (PITCH, 128), 0) < SIDE
    clear_edges(pitched)

    def row(i, carry):
        for c in range(BLOCKS):
            got = dense[c, pl.ds(i * SIDE, PITCH), :]
            at = pl.multiple_of(EDGE + (i + 2) * PITCH, 8)
            pitched[c, pl.ds(at, PITCH), :] = jnp.where(inside, got, 0.0)
        return carry

    lax.fori_loop(0, SIDE, row, 0, unroll=3)


def spread_conv(pitched, wide, dense, kernel, flipped):
    radius = kernel // 2
    last = kernel * kernel - 1

    def group(g, carry):
        for c in range(BLOCKS):
            sums = [[None] * 3 for _ in range(3)]
            start = EDGE + (3 * g + 2 - radius) * PITCH
            for b in range(kernel + 2):
                for shift in range(-radius, 3 + radius):
                    got = pitched[c, pl.ds(start + b * PITCH + shift, 8, stride=3), :]
                    for a in range(3):
                        p = b - a
                        if p < 0 or p >= kernel:
                            continue
                        for r in range(3):
                            q = shift - r + radius
                            if q < 0 or q >= kernel:
                                continue
                            k = p * kernel + q
                            term = wide[last - k if flipped else k, c] * got
                            old = sums[a][r]
                            sums[a][r] = term if old is None else old + term
            for a in range(3):
                for r in range(3):
                    dense[c, pl.ds((3 * g + a) * SIDE + r, 8, stride=3), :] = sums[a][r]
        return carry

    lax.fori_loop(0, SIDE // 3, group, 0)


def tap_sums(back, active, sums_ref, kernel):
    radius = kernel // 2
    count = kernel * kernel
    for c in range(BLOCKS):

        def row(i, sums):
            sums = list(sums)
            here = EDGE + (i + 2) * PITCH
            centre = [back[c, pl.ds(here + r, 8, stride=3), :] for r in range(3)]
            for p in range(kernel):
                for shift in range(-radius, 3 + radius):
                    got = active[c, pl.ds(here + (p - radius) * PITCH + shift, 8, stride=3), :]
                    for r in range(3):
                        q = shift - r + radius
                        if 0 <= q < kernel:
                            sums[p * kernel + q] = sums[p * kernel + q] + got * centre[r]
            return tuple(sums)

        sums = lax.fori_loop(0, SIDE, row, tuple(jnp.zeros((8, 128), F32) for _ in range(count)))
        for k in range(count):
            sums_ref[k : k + 1, lanes(c)] = jnp.sum(sums[k], axis=0, keepdims=True)


def pieces(ref, width):
    whole = PIXELS // 16

    def read(i):
        return ref[pl.ds(i * 16, 16)]

    tail = jnp.concatenate(
        [ref[whole * 16 : PIXELS], jnp.zeros((16 - PIXELS % 16, width, CH), BF16)], 0
    )
    return whole, read, tail


def unpack(ref, width, put):
    whole, read, tail = pieces(ref, width)

    def body(i, carry):
        put(pl.multiple_of(i * 16, 16), jnp.swapaxes(read(i), 0, 1))
        return carry

    lax.fori_loop(0, whole, body, 0)
    put(whole * 16, jnp.swapaxes(tail, 0, 1))


def dense_product(left, weight_ref, dense):
    for c in range(BLOCKS):
        dense[c, 0:ROWS, :] = lax.dot_general(
            left, weight_ref[lanes(c), :], (((1,), (1,)), ((), ())), preferred_element_type=F32
        )


def masked(act, t, dense, c, rows):
    return jnp.where(act[t, rows, lanes(c)].astype(F32) > 0, dense[c, rows, :], 0.0)


def finish_older(act_older, t, dense, grad_older):
    def body(i, carry):
        rows = pl.ds(pl.multiple_of(i * 16, 16), 16)
        for c in range(BLOCKS):
            grad_older[rows, lanes(c)] = masked(act_older, t, dense, c, rows).astype(BF16)
        return carry

    lax.fori_loop(0, ROWS // 16, body, 0)


def last_piece(act_last, t, dense, grad_out, grad_pass, c, rows):
    skip = grad_pass[rows, lanes(c)].astype(F32) + grad_out[rows, lanes(c)].astype(F32)
    return (skip + masked(act_last, t, dense, c, rows)).astype(BF16)


def finish_last(act_last, t, dense, grad_out, grad_pass, grad_last):
    def body(i, carry):
        rows = pl.ds(pl.multiple_of(i * 16, 16), 16)
        for c in range(BLOCKS):
            grad_last[rows, lanes(c)] = last_piece(act_last, t, dense, grad_out, grad_pass, c, rows)
        return carry

    lax.fori_loop(0, ROWS // 16, body, 0)


def three_part(t, grad_out, act_older, weight, taps, back, grad_older, wide, dense, ready):
    spread_taps(taps, wide, 9)
    dense_product(grad_out[...], weight, dense)
    to_pitched(dense, back)
    spread_conv(back, wide, dense, 3, True)
    ready()
    finish_older(act_older, t, dense, grad_older)


def five_part(t, grad_out, grad_pass, act_last, weight, taps, back, grad_last, wide, dense, ready):
    spread_taps(taps, wide, 25)
    dense_product(grad_out[...], weight, dense)
    to_pitched(dense, back)
    spread_conv(back, wide, dense, 5, True)
    ready()
    finish_last(act_last, t, dense, grad_out, grad_pass, grad_last)


def order_kernel(plan_ref, turn_ref):
    for t in range(turn_ref.shape[0]):
        turn_ref[plan_ref[0, t]] = t


def slots_unpacked(turn_ref, source, target):
    def put(at, block):
        block = jnp.maximum(block, 0)
        for k in range(4):
            target[turn_ref[k], pl.ds(at, 16), :] = block[k]

    unpack(source, 4, put)


def pair_unpacked(source, grad_out, grad_pass):
    def put(at, block):
        grad_out[pl.ds(at, 16), :] = block[0]
        grad_pass[pl.ds(at, 16), :] = block[1]

    unpack(source, 2, put)


def first_three_kernel(
    turn_ref, older_in, arriving_in, weight, taps, grad_older, act_older, grad_out, grad_pass, back, wide, dense
):
    pair_unpacked(arriving_in, grad_out, grad_pass)

    def ready():
        slots_unpacked(turn_ref, older_in, act_older)

    three_part(0, grad_out, act_older, weight, taps, back, grad_older, wide, dense, ready)


def first_five_kernel(
    turn_ref, last_in, grad_out, grad_pass, weight, taps, grad_last, act_last, back, wide, dense
):
    def ready():
        slots_unpacked(turn_ref, last_in, act_last)

    five_part(0, grad_out, grad_pass, act_last, weight, taps, back, grad_last, wide, dense, ready)


def take(t, top_ref, out_in, pass_in, head_hbm, grad_out, grad_pass, head_in, sem):
    @pl.when(top_ref[0] == 1)
    def _():
        get = pltpu.make_async_copy(head_hbm.at[t - 1], head_in, sem)
        get.start()
        get.wait()
        pair_unpacked(head_in, grad_out, grad_pass)

    @pl.when(top_ref[0] != 1)
    def _():
        grad_out[...] = out_in[...]
        grad_pass[...] = pass_in[...]


def three_kernel(
    t,
    top_ref,
    out_in,
    pass_in,
    head_hbm,
    act_older,
    weight,
    taps,
    grad_older,
    grad_out,
    grad_pass,
    back,
    head_in,
    wide,
    dense,
    sem,
):
    take(t, top_ref, out_in, pass_in, head_hbm, grad_out, grad_pass, head_in, sem)
    three_part(t, grad_out, act_older, weight, taps, back, grad_older, wide, dense, lambda: None)


def five_kernel(t, grad_out, grad_pass, act_last, weight, taps, grad_last, back, wide, dense):
    five_part(t, grad_out, grad_pass, act_last, weight, taps, back, grad_last, wide, dense, lambda: None)


def copies(pairs, sems):
    return [pltpu.make_async_copy(a, b, sems.at[n]) for n, (a, b) in enumerate(pairs)]


def widened(act, t, dense):
    def body(i, carry):
        rows = pl.ds(pl.multiple_of(i * 16, 16), 16)
        for c in range(BLOCKS):
            dense[c, rows, :] = act[t, rows, lanes(c)].astype(F32)
        return carry

    lax.fori_loop(0, ROWS // 16, body, 0)


def mix(act, t, taps, mixed, pitched, dense, wide, kernel):
    widened(act, t, dense)
    to_pitched(dense, pitched)
    spread_taps(taps, wide, kernel * kernel)
    for c in range(BLOCKS):
        dense[c, ROWS - 8 : ROWS, :] = jnp.zeros((8, 128), F32)
    spread_conv(pitched, wide, dense, kernel, False)

    def body(i, carry):
        rows = pl.ds(pl.multiple_of(i * 16, 16), 16)
        for c in range(BLOCKS):
            mixed[rows, lanes(c)] = dense[c, rows, :].astype(BF16)
        return carry

    lax.fori_loop(0, ROWS // 16, body, 0)


def across(mixed, left):
    return lax.dot_general(mixed, left, (((0,), (0,)), ((), ())), preferred_element_type=F32)


def grads_kernel(t, ahead, *refs):
    refs = list(refs)
    grad_out, act_last, act_older, taps_five, taps_three, back_five, back_three = refs[:7]
    refs = refs[7:]
    olds = None
    if t > 0:
        olds = refs[:4]
        refs = refs[4:]
    sums = refs[:4]
    refs = refs[4:]
    if ahead is not None:
        later = refs[:2]
        refs = refs[2:]
    pitched, dense, wide, mixed = refs
    left = grad_out[...]
    for n, (act, taps, back, kernel) in enumerate(
        ((act_last, taps_five, back_five, 5), (act_older, taps_three, back_three, 3))
    ):
        if ahead is not None:
            mix(act, ahead, taps, later[n], pitched, dense, wide, kernel)
        mix(act, t, taps, mixed, pitched, dense, wide, kernel)
        got = across(mixed[...], left)
        sums[2 * n][...] = got if olds is None else got + olds[2 * n][...]
        tap_sums(back, pitched, sums[2 * n + 1], kernel)
        if olds is not None:
            sums[2 * n + 1][...] = sums[2 * n + 1][...] + olds[2 * n + 1][...]


def last_grads_kernel(
    t,
    top_ref,
    out_in,
    pass_in,
    head_hbm,
    act_last,
    act_older,
    weight_five,
    weight_three,
    mixed_five,
    mixed_three,
    old_five,
    old_taps_five,
    old_three,
    old_taps_three,
    packed_hbm,
    out_hbm,
    pass_hbm,
    back_five_hbm,
    back_three_hbm,
    last_hbm,
    older_hbm,
    packed,
    grad_out,
    grad_pass,
    back_five,
    back_three,
    head_in,
    pitched,
    dense,
    rows_ref,
    sems,
):
    scale = 1.0 / PIXELS
    keep = copies(
        [
            (act_last.at[t], last_hbm),
            (act_older.at[t], older_hbm),
            (grad_out, out_hbm),
            (grad_pass, pass_hbm),
            (back_five, back_five_hbm),
            (back_three, back_three_hbm),
        ],
        sems,
    )
    points, columns = copies(
        [
            (packed.at[:, pl.ds(0, 2 * CH)], packed_hbm.at[:, pl.ds(0, 2 * CH)]),
            (packed.at[:, pl.ds(2 * CH, 128)], packed_hbm.at[:, pl.ds(2 * CH, 128)]),
        ],
        sems.at[pl.ds(6, 2)],
    )
    keep[0].start()
    keep[1].start()
    take(t, top_ref, out_in, pass_in, head_hbm, grad_out, grad_pass, head_in, sems.at[8])
    keep[2].start()
    keep[3].start()
    left = grad_out[...]
    packed[:, 0:CH] = ((across(mixed_five[...], left) + old_five[...]) * scale).astype(BF16)
    packed[:, CH : 2 * CH] = ((across(mixed_three[...], left) + old_three[...]) * scale).astype(BF16)
    points.start()
    rows_ref[...] = jnp.zeros(rows_ref.shape, F32)
    for act, weight, back, old, at, kernel, kept in (
        (act_last, weight_five, back_five, old_taps_five, 0, 5, keep[4]),
        (act_older, weight_three, back_three, old_taps_three, 32, 3, keep[5]),
    ):
        dense_product(left, weight, dense)
        to_pitched(dense, back)
        kept.start()
        widened(act, t, dense)
        to_pitched(dense, pitched)
        count = kernel * kernel
        tap_sums(back, pitched, rows_ref.at[pl.ds(at, old.shape[0])], kernel)
        rows_ref[at : at + count, :] = (rows_ref[at : at + count, :] + old[0:count, :]) * scale
    for c in range(BLOCKS):
        packed[lanes(c), 2 * CH : 2 * CH + 128] = rows_ref[:, lanes(c)].T.astype(BF16)
    columns.start()
    for copy in keep:
        copy.wait()
    points.wait()
    columns.wait()


def last_kernel(
    grad_out_hbm,
    grad_pass_hbm,
    back_five_hbm,
    back_three_hbm,
    act_last_hbm,
    act_older_hbm,
    taps_five,
    taps_three,
    outgoing_hbm,
    grad_out,
    grad_pass,
    back_five,
    back_three,
    act_last,
    act_older,
    wide_five,
    wide_three,
    dense,
    made_older,
    outgoing,
    sems,
):
    gets = copies(
        [
            (back_three_hbm, back_three),
            (act_older_hbm, act_older.at[0]),
            (back_five_hbm, back_five),
            (act_last_hbm, act_last.at[0]),
            (grad_out_hbm, grad_out),
            (grad_pass_hbm, grad_pass),
        ],
        sems,
    )
    for get in gets:
        get.start()
    spread_taps(taps_five, wide_five, 25)
    spread_taps(taps_three, wide_three, 9)
    gets[0].wait()
    spread_conv(back_three, wide_three, dense, 3, True)
    gets[1].wait()
    finish_older(act_older, 0, dense, made_older)
    gets[2].wait()
    spread_conv(back_five, wide_five, dense, 5, True)
    for get in gets[3:]:
        get.wait()

    def both(rows, c):
        last = last_piece(act_last, 0, dense, grad_out, grad_pass, c, rows)
        return jnp.swapaxes(jnp.stack([last, made_older[rows, lanes(c)]], 0), 0, 1)

    def body(i, carry):
        rows = pl.ds(pl.multiple_of(i * 16, 16), 16)
        for c in range(BLOCKS):
            outgoing[rows, :, lanes(c)] = both(rows, c)
        return carry

    half = 224
    lax.fori_loop(0, half // 16, body, 0)
    put = copies(
        [
            (outgoing.at[pl.ds(0, half)], outgoing_hbm.at[pl.ds(0, half)]),
            (outgoing.at[pl.ds(half, PIXELS - half)], outgoing_hbm.at[pl.ds(half, PIXELS - half)]),
        ],
        sems.at[pl.ds(6, 2)],
    )
    put[0].start()
    lax.fori_loop(half // 16, PIXELS // 16, body, 0)
    at = PIXELS // 16 * 16
    for c in range(BLOCKS):
        outgoing[at:PIXELS, :, lanes(c)] = both(slice(at, at + 16), c)[: PIXELS - at]
    put[1].start()
    put[0].wait()
    put[1].wait()


def total_kernel(landed, five, three, taps_five, taps_three):
    def summed(columns):
        total = landed[0, :, columns].astype(F32)
        for n in range(1, landed.shape[0]):
            total = total + landed[n, :, columns].astype(F32)
        return total

    five[...] = summed(slice(0, CH))
    three[...] = summed(slice(CH, 2 * CH))
    rows = summed(slice(2 * CH, 2 * CH + 128)).T
    for taps, at in ((taps_five, 0), (taps_three, 32)):
        for k in range(taps.shape[0]):
            taps[k] = rows[at + k : at + k + 1, :]


VMEM = pl.BlockSpec(memory_space=pltpu.VMEM)
SMEM = pl.BlockSpec(memory_space=pltpu.SMEM)
ANY = pl.BlockSpec(memory_space=pl.ANY)
ALONE = 16 << 20
FLAT = jax.ShapeDtypeStruct((ROWS, CH), BF16)
PACKED = jax.ShapeDtypeStruct((CH, 2 * CH + 128), BF16)
ACTS = jax.ShapeDtypeStruct((4, ROWS, CH), BF16)
BACK = jax.ShapeDtypeStruct((BLOCKS, PITCHED, 128), F32)
SUMS = (
    jax.ShapeDtypeStruct((CH, CH), F32),
    jax.ShapeDtypeStruct((32, CH), F32),
    jax.ShapeDtypeStruct((CH, CH), F32),
    jax.ShapeDtypeStruct((16, CH), F32),
)
FLAT_SCRATCH = pltpu.VMEM((ROWS, CH), BF16)
PAIR_SCRATCH = pltpu.VMEM((PIXELS, 2, CH), BF16)
WIDE_FIVE = pltpu.VMEM((25, BLOCKS, 8, 128), F32)
WIDE_THREE = pltpu.VMEM((9, BLOCKS, 8, 128), F32)
DENSE = pltpu.VMEM((BLOCKS, ROWS + 8, 128), F32)
PITCHED_SCRATCH = pltpu.VMEM((BLOCKS, PITCHED, 128), F32)


def run(kernel, name, operands, specs, shapes, out_specs, scratch, micros, limit=12 << 20):
    cost = pl.CostEstimate(flops=int(micros * 1e9), bytes_accessed=0, transcendentals=0)
    return pl.pallas_call(
        kernel,
        out_shape=tuple(shapes),
        in_specs=specs,
        out_specs=tuple(out_specs),
        scratch_shapes=scratch,
        compiler_params=pltpu.CompilerParams(vmem_limit_bytes=limit),
        cost_estimate=cost,
        name=name,
    )(*operands)


def call_order(plan):
    (turns,) = run(
        order_kernel,
        "order",
        (plan,),
        [SMEM],
        (jax.ShapeDtypeStruct((plan.shape[1],), jnp.int32),),
        (SMEM,),
        [],
        6,
    )
    return turns


def call_first_three(turns, older, arriving, weight, taps):
    return run(
        first_three_kernel,
        "first_three",
        (turns, older, arriving, weight, taps),
        [SMEM] + [VMEM] * 4,
        (FLAT, ACTS, FLAT, FLAT, BACK),
        (VMEM,) * 5,
        [WIDE_THREE, DENSE],
        4,
    )


def call_first_five(turns, last, grad_out, grad_pass, weight, taps):
    return run(
        first_five_kernel,
        "first_five",
        (turns, last, grad_out, grad_pass, weight, taps),
        [SMEM] + [VMEM] * 5,
        (FLAT, ACTS, BACK),
        (VMEM,) * 3,
        [WIDE_FIVE, DENSE],
        4,
    )


def call_three(t, given, act, weight, taps):
    return run(
        functools.partial(three_kernel, t),
        f"three_{t}",
        (*given, act, weight, taps),
        [SMEM, VMEM, VMEM, ANY] + [VMEM] * 3,
        (FLAT, FLAT, FLAT, BACK),
        (VMEM,) * 4,
        [PAIR_SCRATCH, WIDE_THREE, DENSE, pltpu.SemaphoreType.DMA],
        2,
    )


def call_five(t, grad_out, grad_pass, act, weight, taps):
    return run(
        functools.partial(five_kernel, t),
        f"five_{t}",
        (grad_out, grad_pass, act, weight, taps),
        [VMEM] * 5,
        (FLAT, BACK),
        (VMEM,) * 2,
        [WIDE_FIVE, DENSE],
        3,
    )


def call_grads(t, ahead, grad_out, acts, taps, backs, olds):
    shapes = SUMS if ahead is None else SUMS + (FLAT, FLAT)
    operands = (grad_out, *acts, *taps, *backs, *olds)
    return run(
        functools.partial(grads_kernel, t, ahead),
        f"grads_{t}",
        operands,
        [VMEM] * len(operands),
        shapes,
        (VMEM,) * len(shapes),
        [PITCHED_SCRATCH, DENSE, WIDE_FIVE, FLAT_SCRATCH],
        6 if ahead is None else 8,
    )


def call_last_grads(t, given, acts, weights, mixed, olds):
    return run(
        functools.partial(last_grads_kernel, t),
        "last_grads",
        (*given, *acts, *weights, *mixed, *olds),
        [SMEM, VMEM, VMEM, ANY] + [VMEM] * 10,
        (PACKED, FLAT, FLAT, BACK, BACK, FLAT, FLAT),
        (ANY,) * 7,
        [
            pltpu.VMEM(PACKED.shape, BF16),
            FLAT_SCRATCH,
            FLAT_SCRATCH,
            PITCHED_SCRATCH,
            PITCHED_SCRATCH,
            PAIR_SCRATCH,
            PITCHED_SCRATCH,
            DENSE,
            pltpu.VMEM((128, CH), F32),
            pltpu.SemaphoreType.DMA((9,)),
        ],
        6,
        ALONE,
    )


def call_last(kept, taps):
    (outgoing,) = run(
        last_kernel,
        "last",
        (*kept, *taps),
        [ANY] * 6 + [VMEM] * 2,
        (jax.ShapeDtypeStruct((PIXELS, 2, CH), BF16),),
        (ANY,),
        [
            FLAT_SCRATCH,
            FLAT_SCRATCH,
            PITCHED_SCRATCH,
            PITCHED_SCRATCH,
            pltpu.VMEM((1, ROWS, CH), BF16),
            pltpu.VMEM((1, ROWS, CH), BF16),
            WIDE_FIVE,
            WIDE_THREE,
            DENSE,
            FLAT_SCRATCH,
            PAIR_SCRATCH,
            pltpu.SemaphoreType.DMA((8,)),
        ],
        4,
    )
    return outgoing


def whole(shape):
    zeros = (0,) * len(shape)
    return pl.BlockSpec(shape, lambda i: zeros)


def call_total(landed):
    rows = landed.shape[1]
    shapes = [(rows, CH), (rows, CH), (25, 1, rows), (9, 1, rows)]
    return pl.pallas_call(
        total_kernel,
        grid=(1,),
        out_shape=tuple(jax.ShapeDtypeStruct(shape, F32) for shape in shapes),
        in_specs=[whole(landed.shape)],
        out_specs=tuple(whole(shape) for shape in shapes),
        compiler_params=pltpu.CompilerParams(vmem_limit_bytes=12 << 20),
        name="total",
    )(landed)


def by_pixel(stack):
    return jnp.transpose(stack, (0, 2, 3, 4, 1, 5)).reshape(PIXELS, stack.shape[1], CH)


def local(
    saved_last,
    saved_older,
    arriving,
    head_adjoint,
    plan,
    depth_five,
    depth_three,
    point_five,
    point_three,
):
    turns = saved_last.shape[1]
    top = (lax.axis_index("sec") == lax.axis_size("sec") - 1).astype(jnp.int32)[None]
    turn_of_slot = call_order(plan)
    turn_of_slot, top = lax.optimization_barrier((turn_of_slot, top))
    head = jnp.transpose(head_adjoint, (0, 2, 3, 4, 1, 5)).reshape(turns - 1, PIXELS, 2, CH)
    weights = (point_five[0], point_three[0])
    taps = (depth_five[0], depth_three[0])
    grad_older, act_older, grad_out, grad_pass, back_three = call_first_three(
        turn_of_slot, by_pixel(saved_older), by_pixel(arriving), weights[1], taps[1]
    )
    next_pass = from_next(grad_older)
    grad_last, act_last, back_five = call_first_five(
        turn_of_slot, by_pixel(saved_last), grad_out, grad_pass, weights[0], taps[0]
    )
    acts = (act_last, act_older)
    sums = ()
    for t in range(turns - 1):
        next_out = from_next(grad_last)
        ahead = turns - 1 if t == turns - 2 else None
        made = call_grads(t, ahead, grad_out, acts, taps, (back_five, back_three), sums)
        next_out, next_pass, made = lax.optimization_barrier((next_out, next_pass, made))
        sums = made[:4]
        given = (top, next_out, next_pass, head)
        if t < turns - 2:
            grad_older, grad_out, grad_pass, back_three = call_three(
                t + 1, given, act_older, weights[1], taps[1]
            )
            next_pass = from_next(grad_older)
            grad_last, back_five = call_five(
                t + 1, grad_out, grad_pass, act_last, weights[0], taps[0]
            )
    packed, *kept = call_last_grads(
        turns - 1, given, acts, weights, made[4:], sums
    )
    devices = lax.axis_size("img")
    packed = packed.reshape(devices, CH // devices, packed.shape[1])
    landed = lax.all_to_all(packed, "img", 0, 0, tiled=True)
    outgoing = call_last(kept, taps)
    five, three, tap_five, tap_three = call_total(landed)
    outgoing = outgoing.reshape(1, 1, SIDE, SIDE, 2, CH).transpose(0, 4, 1, 2, 3, 5)
    return (
        outgoing,
        five[None],
        jnp.transpose(tap_five, (1, 2, 0)),
        three[None],
        jnp.transpose(tap_three, (1, 2, 0)),
    )


def solution(mesh):
    placed = (
        P("sec", None, "img", None, None, None),
        P("sec", None, "img", None, None, None),
        P("sec", None, "img", None, None, None),
        P(None, None, "img", None, None, None),
        P("sec", None),
        P("sec", None, None),
        P("sec", None, None),
        P("sec", None, None),
        P("sec", None, None),
    )
    return jax.shard_map(
        local,
        mesh=mesh,
        in_specs=placed,
        out_specs=(
            P("sec", None, "img", None, None, None),
            P("sec", "img", None),
            P("sec", "img", None),
            P("sec", "img", None),
            P("sec", "img", None),
        ),
        check_vma=False,
    )
```

```python
import functools

import jax
import jax.numpy as jnp
from jax import lax
from jax.experimental import pallas as pl
from jax.experimental.pallas import tpu as pltpu
from jax.sharding import PartitionSpec as P

SIDE = 21
PIXELS = SIDE * SIDE
ROWS = 448
CH = 384
BLOCKS = CH // 128
PITCH = 24
EDGE = 8
PITCHED = EDGE + (SIDE + 4) * PITCH + 8
F32 = jnp.float32
BF16 = jnp.bfloat16


def from_next(block):
    size = lax.axis_size("sec")
    return lax.ppermute(block, "sec", [(i + 1, i) for i in range(size - 1)])


def lanes(c):
    return slice(c * 128, (c + 1) * 128)


def spread_taps(taps_ref, wide, count):
    for k in range(count):
        row = taps_ref[k : k + 1, :].astype(F32)
        for c in range(BLOCKS):
            wide[k, c] = jnp.broadcast_to(row[:, lanes(c)], (8, 128))


def clear_edges(pitched):
    top = EDGE + 2 * PITCH
    bottom = EDGE + (SIDE + 2) * PITCH
    for c in range(BLOCKS):
        pitched[c, 0:top, :] = jnp.zeros((top, 128), F32)
        pitched[c, bottom:PITCHED, :] = jnp.zeros((PITCHED - bottom, 128), F32)


def to_pitched(dense, pitched):
    inside = lax.broadcasted_iota(jnp.int32, (PITCH, 128), 0) < SIDE
    clear_edges(pitched)

    def row(i, carry):
        for c in range(BLOCKS):
            got = dense[c, pl.ds(i * SIDE, PITCH), :]
            at = pl.multiple_of(EDGE + (i + 2) * PITCH, 8)
            pitched[c, pl.ds(at, PITCH), :] = jnp.where(inside, got, 0.0)
        return carry

    lax.fori_loop(0, SIDE, row, 0, unroll=3)


def add_window(sums, got, weight_of, b, shift, rows, kernel):
    radius = kernel // 2
    for a in range(rows):
        p = b - a
        if p < 0 or p >= kernel:
            continue
        for r in range(3):
            q = shift - r + radius
            if q < 0 or q >= kernel:
                continue
            term = weight_of(p * kernel + q) * got
            old = sums[a][r]
            sums[a][r] = term if old is None else old + term


def spread_conv(pitched, wide, dense, kernel, flipped):
    radius = kernel // 2
    last = kernel * kernel - 1
    rows = 3 if kernel == 5 else 7

    def group(g, carry):
        for c in range(BLOCKS):
            sums = [[None] * 3 for _ in range(rows)]
            start = EDGE + (rows * g + 2 - radius) * PITCH
            for b in range(kernel + rows - 1):
                for shift in range(-radius, 3 + radius):
                    got = pitched[c, pl.ds(start + b * PITCH + shift, 8, stride=3), :]
                    add_window(
                        sums,
                        got,
                        lambda k: wide[last - k if flipped else k, c],
                        b,
                        shift,
                        rows,
                        kernel,
                    )
            for a in range(rows):
                for r in range(3):
                    dense[c, pl.ds((rows * g + a) * SIDE + r, 8, stride=3), :] = sums[a][r]
        return carry

    lax.fori_loop(0, SIDE // rows, group, 0)


def tap_sums(back, active, sums_ref, kernel):
    radius = kernel // 2
    count = kernel * kernel
    rows = 7
    for c in range(BLOCKS):

        def group(g, sums):
            sums = list(sums)
            here = EDGE + (rows * g + 2) * PITCH
            centre = [
                [back[c, pl.ds(here + a * PITCH + r, 8, stride=3), :] for r in range(3)]
                for a in range(rows)
            ]
            for b in range(kernel + rows - 1):
                for shift in range(-radius, 3 + radius):
                    at = here + (b - radius) * PITCH + shift
                    got = active[c, pl.ds(at, 8, stride=3), :]
                    for a in range(rows):
                        p = b - a
                        if p < 0 or p >= kernel:
                            continue
                        for r in range(3):
                            q = shift - r + radius
                            if 0 <= q < kernel:
                                k = p * kernel + q
                                sums[k] = sums[k] + got * centre[a][r]
            return tuple(sums)

        empty = tuple(jnp.zeros((8, 128), F32) for _ in range(count))
        sums = lax.fori_loop(0, SIDE // rows, group, empty)
        for k in range(count):
            sums_ref[k : k + 1, lanes(c)] = jnp.sum(sums[k], axis=0, keepdims=True)


def pieces(ref, width):
    whole = PIXELS // 16

    def read(i):
        return ref[pl.ds(i * 16, 16)]

    tail = jnp.concatenate(
        [ref[whole * 16 : PIXELS], jnp.zeros((16 - PIXELS % 16, width, CH), BF16)], 0
    )
    return whole, read, tail


def unpack(ref, width, put):
    whole, read, tail = pieces(ref, width)

    def body(i, carry):
        put(pl.multiple_of(i * 16, 16), jnp.swapaxes(read(i), 0, 1))
        return carry

    lax.fori_loop(0, whole, body, 0)
    put(whole * 16, jnp.swapaxes(tail, 0, 1))


def dense_product(left, weight_ref, dense):
    for first, blocks in ((0, 2), (2, 1)):
        got = lax.dot_general(
            left,
            weight_ref[first * 128 : (first + blocks) * 128, :],
            (((1,), (1,)), ((), ())),
            preferred_element_type=F32,
        )
        for c in range(blocks):
            dense[first + c, 0:ROWS, :] = got[:, lanes(c)]


def masked(act, t, dense, c, rows):
    return jnp.where(act[t, rows, lanes(c)].astype(F32) > 0, dense[c, rows, :], 0.0)


def finish_older(act_older, t, dense, grad_older):
    def body(i, carry):
        rows = pl.ds(pl.multiple_of(i * 16, 16), 16)
        for c in range(BLOCKS):
            grad_older[rows, lanes(c)] = masked(act_older, t, dense, c, rows).astype(BF16)
        return carry

    lax.fori_loop(0, ROWS // 16, body, 0)


def last_piece(act_last, t, dense, grad_out, grad_pass, c, rows):
    skip = grad_pass[rows, lanes(c)].astype(F32) + grad_out[rows, lanes(c)].astype(F32)
    return (skip + masked(act_last, t, dense, c, rows)).astype(BF16)


def finish_last(act_last, t, dense, grad_out, grad_pass, grad_last):
    def body(i, carry):
        rows = pl.ds(pl.multiple_of(i * 16, 16), 16)
        for c in range(BLOCKS):
            grad_last[rows, lanes(c)] = last_piece(act_last, t, dense, grad_out, grad_pass, c, rows)
        return carry

    lax.fori_loop(0, ROWS // 16, body, 0)


def three_part(t, grad_out, act_older, weight, taps, back, grad_older, wide, dense, ready):
    spread_taps(taps, wide, 9)
    dense_product(grad_out[...], weight, dense)
    to_pitched(dense, back)
    spread_conv(back, wide, dense, 3, True)
    ready()
    finish_older(act_older, t, dense, grad_older)


def five_part(t, grad_out, grad_pass, act_last, weight, taps, back, grad_last, wide, dense, ready):
    spread_taps(taps, wide, 25)
    dense_product(grad_out[...], weight, dense)
    to_pitched(dense, back)
    spread_conv(back, wide, dense, 5, True)
    ready()
    finish_last(act_last, t, dense, grad_out, grad_pass, grad_last)


def order_kernel(plan_ref, turn_ref):
    for t in range(turn_ref.shape[0]):
        turn_ref[plan_ref[0, t]] = t


def slots_unpacked(turn_ref, source, target):
    def put(at, block):
        block = jnp.maximum(block, 0)
        for k in range(4):
            target[turn_ref[k], pl.ds(at, 16), :] = block[k]

    unpack(source, 4, put)


def pair_unpacked(source, grad_out, grad_pass):
    def put(at, block):
        grad_out[pl.ds(at, 16), :] = block[0]
        grad_pass[pl.ds(at, 16), :] = block[1]

    unpack(source, 2, put)


def first_three_kernel(
    turn_ref, older_in, arriving_in, weight, taps, grad_older, act_older, grad_out, grad_pass, back, wide, dense
):
    pair_unpacked(arriving_in, grad_out, grad_pass)

    def ready():
        slots_unpacked(turn_ref, older_in, act_older)

    three_part(0, grad_out, act_older, weight, taps, back, grad_older, wide, dense, ready)


def first_five_kernel(
    turn_ref, last_in, grad_out, grad_pass, weight, taps, grad_last, act_last, back, wide, dense
):
    def ready():
        slots_unpacked(turn_ref, last_in, act_last)

    five_part(0, grad_out, grad_pass, act_last, weight, taps, back, grad_last, wide, dense, ready)


def take(t, top_ref, out_in, pass_in, head_hbm, grad_out, grad_pass, head_in, sem):
    @pl.when(top_ref[0] == 1)
    def _():
        get = pltpu.make_async_copy(head_hbm.at[t - 1], head_in, sem)
        get.start()
        get.wait()
        pair_unpacked(head_in, grad_out, grad_pass)

    @pl.when(top_ref[0] != 1)
    def _():
        grad_out[...] = out_in[...]
        grad_pass[...] = pass_in[...]


def three_kernel(
    t,
    top_ref,
    out_in,
    pass_in,
    head_hbm,
    act_older,
    weight,
    taps,
    grad_older,
    grad_out,
    grad_pass,
    back,
    head_in,
    wide,
    dense,
    sem,
):
    take(t, top_ref, out_in, pass_in, head_hbm, grad_out, grad_pass, head_in, sem)
    three_part(t, grad_out, act_older, weight, taps, back, grad_older, wide, dense, lambda: None)


def five_kernel(t, grad_out, grad_pass, act_last, weight, taps, grad_last, back, wide, dense):
    five_part(t, grad_out, grad_pass, act_last, weight, taps, back, grad_last, wide, dense, lambda: None)


def copies(pairs, sems):
    return [pltpu.make_async_copy(a, b, sems.at[n]) for n, (a, b) in enumerate(pairs)]


def widened(act, t, dense):
    def body(i, carry):
        rows = pl.ds(pl.multiple_of(i * 16, 16), 16)
        for c in range(BLOCKS):
            dense[c, rows, :] = act[t, rows, lanes(c)].astype(F32)
        return carry

    lax.fori_loop(0, ROWS // 16, body, 0)


def mix(act, t, taps, mixed, pitched, dense, wide, kernel):
    widened(act, t, dense)
    to_pitched(dense, pitched)
    spread_taps(taps, wide, kernel * kernel)
    for c in range(BLOCKS):
        dense[c, ROWS - 8 : ROWS, :] = jnp.zeros((8, 128), F32)
    spread_conv(pitched, wide, dense, kernel, False)

    def body(i, carry):
        rows = pl.ds(pl.multiple_of(i * 16, 16), 16)
        for c in range(BLOCKS):
            mixed[rows, lanes(c)] = dense[c, rows, :].astype(BF16)
        return carry

    lax.fori_loop(0, ROWS // 16, body, 0)


def across(mixed, left):
    return lax.dot_general(mixed, left, (((0,), (0,)), ((), ())), preferred_element_type=F32)


def grads_kernel(t, ahead, *refs):
    refs = list(refs)
    grad_out, act_last, act_older, taps_five, taps_three, back_five, back_three = refs[:7]
    refs = refs[7:]
    olds = None
    if t > 0:
        olds = refs[:4]
        refs = refs[4:]
    sums = refs[:4]
    refs = refs[4:]
    if ahead is not None:
        later = refs[:2]
        refs = refs[2:]
    pitched, dense, wide, mixed = refs
    left = grad_out[...]
    for n, (act, taps, back, kernel) in enumerate(
        ((act_last, taps_five, back_five, 5), (act_older, taps_three, back_three, 3))
    ):
        if ahead is not None:
            mix(act, ahead, taps, later[n], pitched, dense, wide, kernel)
        mix(act, t, taps, mixed, pitched, dense, wide, kernel)
        got = across(mixed[...], left)
        sums[2 * n][...] = got if olds is None else got + olds[2 * n][...]
        tap_sums(back, pitched, sums[2 * n + 1], kernel)
        if olds is not None:
            sums[2 * n + 1][...] = sums[2 * n + 1][...] + olds[2 * n + 1][...]


def last_grads_kernel(
    t,
    top_ref,
    out_in,
    pass_in,
    head_hbm,
    act_last,
    act_older,
    weight_five,
    weight_three,
    mixed_five,
    mixed_three,
    old_five,
    old_taps_five,
    old_three,
    old_taps_three,
    packed_hbm,
    flats_hbm,
    backs_hbm,
    packed,
    grad_out,
    grad_pass,
    back_five,
    back_three,
    head_in,
    pitched,
    dense,
    rows_ref,
    sems,
):
    scale = 1.0 / PIXELS
    keep = copies(
        [
            (act_last.at[t], flats_hbm.at[0]),
            (act_older.at[t], flats_hbm.at[1]),
            (grad_out, flats_hbm.at[2]),
            (grad_pass, flats_hbm.at[3]),
            (back_five, backs_hbm.at[0]),
            (back_three, backs_hbm.at[1]),
        ],
        sems,
    )
    points, columns = copies(
        [
            (packed.at[:, pl.ds(0, 2 * CH)], packed_hbm.at[:, pl.ds(0, 2 * CH)]),
            (packed.at[:, pl.ds(2 * CH, 128)], packed_hbm.at[:, pl.ds(2 * CH, 128)]),
        ],
        sems.at[pl.ds(6, 2)],
    )
    keep[0].start()
    keep[1].start()
    take(t, top_ref, out_in, pass_in, head_hbm, grad_out, grad_pass, head_in, sems.at[8])
    keep[2].start()
    keep[3].start()
    left = grad_out[...]
    packed[:, 0:CH] = ((across(mixed_five[...], left) + old_five[...]) * scale).astype(BF16)
    packed[:, CH : 2 * CH] = ((across(mixed_three[...], left) + old_three[...]) * scale).astype(BF16)
    points.start()
    rows_ref[...] = jnp.zeros(rows_ref.shape, F32)
    for act, weight, back, old, at, kernel, kept in (
        (act_last, weight_five, back_five, old_taps_five, 0, 5, keep[4]),
        (act_older, weight_three, back_three, old_taps_three, 32, 3, keep[5]),
    ):
        dense_product(left, weight, dense)
        to_pitched(dense, back)
        kept.start()
        widened(act, t, dense)
        to_pitched(dense, pitched)
        count = kernel * kernel
        tap_sums(back, pitched, rows_ref.at[pl.ds(at, old.shape[0])], kernel)
        rows_ref[at : at + count, :] = (rows_ref[at : at + count, :] + old[0:count, :]) * scale
    for c in range(BLOCKS):
        packed[lanes(c), 2 * CH : 2 * CH + 128] = rows_ref[:, lanes(c)].T.astype(BF16)
    columns.start()
    for copy in keep:
        copy.wait()
    points.wait()
    columns.wait()


def last_kernel(
    flats_hbm,
    backs_hbm,
    taps_five,
    taps_three,
    outgoing_hbm,
    grad_out,
    grad_pass,
    back_five,
    back_three,
    act_last,
    act_older,
    wide_five,
    wide_three,
    dense,
    made_older,
    outgoing,
    sems,
):
    gets = copies(
        [
            (backs_hbm.at[1], back_three),
            (flats_hbm.at[1], act_older.at[0]),
            (backs_hbm.at[0], back_five),
            (flats_hbm.at[0], act_last.at[0]),
            (flats_hbm.at[2], grad_out),
            (flats_hbm.at[3], grad_pass),
        ],
        sems,
    )
    for get in gets:
        get.start()
    spread_taps(taps_five, wide_five, 25)
    spread_taps(taps_three, wide_three, 9)
    gets[0].wait()
    spread_conv(back_three, wide_three, dense, 3, True)
    gets[1].wait()
    finish_older(act_older, 0, dense, made_older)
    gets[2].wait()
    spread_conv(back_five, wide_five, dense, 5, True)
    for get in gets[3:]:
        get.wait()

    def both(rows, c):
        last = last_piece(act_last, 0, dense, grad_out, grad_pass, c, rows)
        return jnp.swapaxes(jnp.stack([last, made_older[rows, lanes(c)]], 0), 0, 1)

    def body(i, carry):
        rows = pl.ds(pl.multiple_of(i * 16, 16), 16)
        for c in range(BLOCKS):
            outgoing[rows, :, lanes(c)] = both(rows, c)
        return carry

    half = 224
    lax.fori_loop(0, half // 16, body, 0)
    put = copies(
        [
            (outgoing.at[pl.ds(0, half)], outgoing_hbm.at[pl.ds(0, half)]),
            (outgoing.at[pl.ds(half, PIXELS - half)], outgoing_hbm.at[pl.ds(half, PIXELS - half)]),
        ],
        sems.at[pl.ds(6, 2)],
    )
    put[0].start()
    lax.fori_loop(half // 16, PIXELS // 16, body, 0)
    at = PIXELS // 16 * 16
    for c in range(BLOCKS):
        outgoing[at:PIXELS, :, lanes(c)] = both(slice(at, at + 16), c)[: PIXELS - at]
    put[1].start()
    put[0].wait()
    put[1].wait()


def total_kernel(landed, five, three, taps_five, taps_three):
    def summed(columns):
        total = landed[0, :, columns].astype(F32)
        for n in range(1, landed.shape[0]):
            total = total + landed[n, :, columns].astype(F32)
        return total

    five[...] = summed(slice(0, CH))
    three[...] = summed(slice(CH, 2 * CH))
    rows = summed(slice(2 * CH, 2 * CH + 128)).T
    for taps, at in ((taps_five, 0), (taps_three, 32)):
        for k in range(taps.shape[0]):
            taps[k] = rows[at + k : at + k + 1, :]


VMEM = pl.BlockSpec(memory_space=pltpu.VMEM)
SMEM = pl.BlockSpec(memory_space=pltpu.SMEM)
ANY = pl.BlockSpec(memory_space=pl.ANY)
ALONE = 16 << 20
FLAT = jax.ShapeDtypeStruct((ROWS, CH), BF16)
PACKED = jax.ShapeDtypeStruct((CH, 2 * CH + 128), BF16)
ACTS = jax.ShapeDtypeStruct((4, ROWS, CH), BF16)
BACK = jax.ShapeDtypeStruct((BLOCKS, PITCHED, 128), F32)
SUMS = (
    jax.ShapeDtypeStruct((CH, CH), F32),
    jax.ShapeDtypeStruct((32, CH), F32),
    jax.ShapeDtypeStruct((CH, CH), F32),
    jax.ShapeDtypeStruct((16, CH), F32),
)
FLAT_SCRATCH = pltpu.VMEM((ROWS, CH), BF16)
PAIR_SCRATCH = pltpu.VMEM((PIXELS, 2, CH), BF16)
WIDE_FIVE = pltpu.VMEM((25, BLOCKS, 8, 128), F32)
WIDE_THREE = pltpu.VMEM((9, BLOCKS, 8, 128), F32)
DENSE = pltpu.VMEM((BLOCKS, ROWS + 8, 128), F32)
PITCHED_SCRATCH = pltpu.VMEM((BLOCKS, PITCHED, 128), F32)


def run(kernel, name, operands, specs, shapes, out_specs, scratch, micros, limit=12 << 20):
    cost = pl.CostEstimate(flops=int(micros * 1e9), bytes_accessed=0, transcendentals=0)
    return pl.pallas_call(
        kernel,
        out_shape=tuple(shapes),
        in_specs=specs,
        out_specs=tuple(out_specs),
        scratch_shapes=scratch,
        compiler_params=pltpu.CompilerParams(vmem_limit_bytes=limit),
        cost_estimate=cost,
        name=name,
    )(*operands)


def call_order(plan):
    (turns,) = run(
        order_kernel,
        "order",
        (plan,),
        [SMEM],
        (jax.ShapeDtypeStruct((plan.shape[1],), jnp.int32),),
        (SMEM,),
        [],
        6,
    )
    return turns


def call_first_three(turns, older, arriving, weight, taps):
    return run(
        first_three_kernel,
        "first_three",
        (turns, older, arriving, weight, taps),
        [SMEM] + [VMEM] * 4,
        (FLAT, ACTS, FLAT, FLAT, BACK),
        (VMEM,) * 5,
        [WIDE_THREE, DENSE],
        4,
    )


def call_first_five(turns, last, grad_out, grad_pass, weight, taps):
    return run(
        first_five_kernel,
        "first_five",
        (turns, last, grad_out, grad_pass, weight, taps),
        [SMEM] + [VMEM] * 5,
        (FLAT, ACTS, BACK),
        (VMEM,) * 3,
        [WIDE_FIVE, DENSE],
        4,
    )


def call_three(t, given, act, weight, taps):
    return run(
        functools.partial(three_kernel, t),
        f"three_{t}",
        (*given, act, weight, taps),
        [SMEM, VMEM, VMEM, ANY] + [VMEM] * 3,
        (FLAT, FLAT, FLAT, BACK),
        (VMEM,) * 4,
        [PAIR_SCRATCH, WIDE_THREE, DENSE, pltpu.SemaphoreType.DMA],
        2,
    )


def call_five(t, grad_out, grad_pass, act, weight, taps):
    return run(
        functools.partial(five_kernel, t),
        f"five_{t}",
        (grad_out, grad_pass, act, weight, taps),
        [VMEM] * 5,
        (FLAT, BACK),
        (VMEM,) * 2,
        [WIDE_FIVE, DENSE],
        3,
    )


def call_grads(t, ahead, grad_out, acts, taps, backs, olds):
    shapes = SUMS if ahead is None else SUMS + (FLAT, FLAT)
    operands = (grad_out, *acts, *taps, *backs, *olds)
    return run(
        functools.partial(grads_kernel, t, ahead),
        f"grads_{t}",
        operands,
        [VMEM] * len(operands),
        shapes,
        (VMEM,) * len(shapes),
        [PITCHED_SCRATCH, DENSE, WIDE_FIVE, FLAT_SCRATCH],
        6 if ahead is None else 8,
    )


def call_last_grads(t, given, acts, weights, mixed, olds):
    return run(
        functools.partial(last_grads_kernel, t),
        "last_grads",
        (*given, *acts, *weights, *mixed, *olds),
        [SMEM, VMEM, VMEM, ANY] + [VMEM] * 10,
        (PACKED, ACTS, jax.ShapeDtypeStruct((2, *BACK.shape), F32)),
        (ANY,) * 3,
        [
            pltpu.VMEM(PACKED.shape, BF16),
            FLAT_SCRATCH,
            FLAT_SCRATCH,
            PITCHED_SCRATCH,
            PITCHED_SCRATCH,
            PAIR_SCRATCH,
            PITCHED_SCRATCH,
            DENSE,
            pltpu.VMEM((128, CH), F32),
            pltpu.SemaphoreType.DMA((9,)),
        ],
        6,
        ALONE,
    )


def call_last(kept, taps):
    (outgoing,) = run(
        last_kernel,
        "last",
        (*kept, *taps),
        [ANY] * 2 + [VMEM] * 2,
        (jax.ShapeDtypeStruct((PIXELS, 2, CH), BF16),),
        (ANY,),
        [
            FLAT_SCRATCH,
            FLAT_SCRATCH,
            PITCHED_SCRATCH,
            PITCHED_SCRATCH,
            pltpu.VMEM((1, ROWS, CH), BF16),
            pltpu.VMEM((1, ROWS, CH), BF16),
            WIDE_FIVE,
            WIDE_THREE,
            DENSE,
            FLAT_SCRATCH,
            PAIR_SCRATCH,
            pltpu.SemaphoreType.DMA((8,)),
        ],
        4,
    )
    return outgoing


def whole(shape):
    zeros = (0,) * len(shape)
    return pl.BlockSpec(shape, lambda i: zeros)


def call_total(landed):
    rows = landed.shape[1]
    shapes = [(rows, CH), (rows, CH), (25, 1, rows), (9, 1, rows)]
    return pl.pallas_call(
        total_kernel,
        grid=(1,),
        out_shape=tuple(jax.ShapeDtypeStruct(shape, F32) for shape in shapes),
        in_specs=[whole(landed.shape)],
        out_specs=tuple(whole(shape) for shape in shapes),
        compiler_params=pltpu.CompilerParams(vmem_limit_bytes=12 << 20),
        name="total",
    )(landed)


def by_pixel(stack):
    return jnp.transpose(stack, (0, 2, 3, 4, 1, 5)).reshape(PIXELS, stack.shape[1], CH)


def local(
    saved_last,
    saved_older,
    arriving,
    head_adjoint,
    plan,
    depth_five,
    depth_three,
    point_five,
    point_three,
):
    turns = saved_last.shape[1]
    top = (lax.axis_index("sec") == lax.axis_size("sec") - 1).astype(jnp.int32)[None]
    turn_of_slot = call_order(plan)
    turn_of_slot, top = lax.optimization_barrier((turn_of_slot, top))
    head = jnp.transpose(head_adjoint, (0, 2, 3, 4, 1, 5)).reshape(turns - 1, PIXELS, 2, CH)
    weights = (point_five[0], point_three[0])
    taps = (depth_five[0], depth_three[0])
    grad_older, act_older, grad_out, grad_pass, back_three = call_first_three(
        turn_of_slot, by_pixel(saved_older), by_pixel(arriving), weights[1], taps[1]
    )
    next_pass = from_next(grad_older)
    grad_last, act_last, back_five = call_first_five(
        turn_of_slot, by_pixel(saved_last), grad_out, grad_pass, weights[0], taps[0]
    )
    acts = (act_last, act_older)
    sums = ()
    for t in range(turns - 1):
        next_out = from_next(grad_last)
        ahead = turns - 1 if t == turns - 2 else None
        made = call_grads(t, ahead, grad_out, acts, taps, (back_five, back_three), sums)
        next_out, next_pass, made = lax.optimization_barrier((next_out, next_pass, made))
        sums = made[:4]
        given = (top, next_out, next_pass, head)
        if t < turns - 2:
            grad_older, grad_out, grad_pass, back_three = call_three(
                t + 1, given, act_older, weights[1], taps[1]
            )
            next_pass = from_next(grad_older)
            grad_last, back_five = call_five(
                t + 1, grad_out, grad_pass, act_last, weights[0], taps[0]
            )
    packed, *kept = call_last_grads(
        turns - 1, given, acts, weights, made[4:], sums
    )
    devices = lax.axis_size("img")
    packed = packed.reshape(devices, CH // devices, packed.shape[1])
    landed = lax.all_to_all(packed, "img", 0, 0, tiled=True)
    outgoing = call_last(kept, taps)
    five, three, tap_five, tap_three = call_total(landed)
    outgoing = outgoing.reshape(1, 1, SIDE, SIDE, 2, CH).transpose(0, 4, 1, 2, 3, 5)
    return (
        outgoing,
        five[None],
        jnp.transpose(tap_five, (1, 2, 0)),
        three[None],
        jnp.transpose(tap_three, (1, 2, 0)),
    )


def solution(mesh):
    placed = (
        P("sec", None, "img", None, None, None),
        P("sec", None, "img", None, None, None),
        P("sec", None, "img", None, None, None),
        P(None, None, "img", None, None, None),
        P("sec", None),
        P("sec", None, None),
        P("sec", None, None),
        P("sec", None, None),
        P("sec", None, None),
    )
    return jax.shard_map(
        local,
        mesh=mesh,
        in_specs=placed,
        out_specs=(
            P("sec", None, "img", None, None, None),
            P("sec", "img", None),
            P("sec", "img", None),
            P("sec", "img", None),
            P("sec", "img", None),
        ),
        check_vma=False,
    )
```

```python
import functools

import jax
import jax.numpy as jnp
from jax import lax
from jax.experimental import pallas as pl
from jax.experimental.pallas import tpu as pltpu
from jax.sharding import PartitionSpec as P

SIDE = 21
PIXELS = SIDE * SIDE
ROWS = 448
CH = 384
BLOCKS = CH // 128
PITCH = 24
EDGE = 8
PITCHED = EDGE + (SIDE + 4) * PITCH + 8
F32 = jnp.float32
BF16 = jnp.bfloat16


def from_next(block):
    size = lax.axis_size("sec")
    return lax.ppermute(block, "sec", [(i + 1, i) for i in range(size - 1)])


def around_rows(block, distance):
    rows = lax.axis_size("img") // 2
    route = [(2 * i + j, (i + distance) % rows * 2 + j) for i in range(rows) for j in range(2)]
    return lax.ppermute(block, "img", route)


def with_partner(block):
    return lax.ppermute(block, "img", [(i, i ^ 1) for i in range(lax.axis_size("img"))])


def lanes(c):
    return slice(c * 128, (c + 1) * 128)


def spread_taps(taps_ref, wide, count):
    for k in range(count):
        row = taps_ref[k : k + 1, :].astype(F32)
        for c in range(BLOCKS):
            wide[k, c] = jnp.broadcast_to(row[:, lanes(c)], (8, 128))


def clear_edges(pitched):
    top = EDGE + 2 * PITCH
    bottom = EDGE + (SIDE + 2) * PITCH
    for c in range(BLOCKS):
        pitched[c, 0:top, :] = jnp.zeros((top, 128), F32)
        pitched[c, bottom:PITCHED, :] = jnp.zeros((PITCHED - bottom, 128), F32)


def to_pitched(dense, pitched):
    inside = lax.broadcasted_iota(jnp.int32, (PITCH, 128), 0) < SIDE
    clear_edges(pitched)

    def row(i, carry):
        for c in range(BLOCKS):
            got = dense[c, pl.ds(i * SIDE, PITCH), :]
            at = pl.multiple_of(EDGE + (i + 2) * PITCH, 8)
            pitched[c, pl.ds(at, PITCH), :] = jnp.where(inside, got, 0.0)
        return carry

    lax.fori_loop(0, SIDE, row, 0, unroll=3)


def add_window(sums, got, weight_of, b, shift, rows, kernel):
    radius = kernel // 2
    for a in range(rows):
        p = b - a
        if p < 0 or p >= kernel:
            continue
        for r in range(3):
            q = shift - r + radius
            if q < 0 or q >= kernel:
                continue
            term = weight_of(p * kernel + q) * got
            old = sums[a][r]
            sums[a][r] = term if old is None else old + term


def spread_conv(pitched, wide, dense, kernel, flipped):
    radius = kernel // 2
    last = kernel * kernel - 1
    rows = 3 if kernel == 5 else 7

    def group(g, carry):
        for c in range(BLOCKS):
            sums = [[None] * 3 for _ in range(rows)]
            start = EDGE + (rows * g + 2 - radius) * PITCH
            for b in range(kernel + rows - 1):
                for shift in range(-radius, 3 + radius):
                    got = pitched[c, pl.ds(start + b * PITCH + shift, 8, stride=3), :]
                    add_window(
                        sums,
                        got,
                        lambda k: wide[last - k if flipped else k, c],
                        b,
                        shift,
                        rows,
                        kernel,
                    )
            for a in range(rows):
                for r in range(3):
                    dense[c, pl.ds((rows * g + a) * SIDE + r, 8, stride=3), :] = sums[a][r]
        return carry

    lax.fori_loop(0, SIDE // rows, group, 0)


def tap_sums(back, active, sums_ref, kernel):
    radius = kernel // 2
    count = kernel * kernel
    rows = 7
    for c in range(BLOCKS):

        def group(g, sums):
            sums = list(sums)
            here = EDGE + (rows * g + 2) * PITCH
            centre = [
                [back[c, pl.ds(here + a * PITCH + r, 8, stride=3), :] for r in range(3)]
                for a in range(rows)
            ]
            for b in range(kernel + rows - 1):
                for shift in range(-radius, 3 + radius):
                    at = here + (b - radius) * PITCH + shift
                    got = active[c, pl.ds(at, 8, stride=3), :]
                    for a in range(rows):
                        p = b - a
                        if p < 0 or p >= kernel:
                            continue
                        for r in range(3):
                            q = shift - r + radius
                            if 0 <= q < kernel:
                                k = p * kernel + q
                                sums[k] = sums[k] + got * centre[a][r]
            return tuple(sums)

        empty = tuple(jnp.zeros((8, 128), F32) for _ in range(count))
        sums = lax.fori_loop(0, SIDE // rows, group, empty)
        for k in range(count):
            sums_ref[k : k + 1, lanes(c)] = jnp.sum(sums[k], axis=0, keepdims=True)


def pieces(ref, width):
    whole = PIXELS // 16

    def read(i):
        return ref[pl.ds(i * 16, 16)]

    tail = jnp.concatenate(
        [ref[whole * 16 : PIXELS], jnp.zeros((16 - PIXELS % 16, width, CH), BF16)], 0
    )
    return whole, read, tail


def unpack(ref, width, put):
    whole, read, tail = pieces(ref, width)

    def body(i, carry):
        put(pl.multiple_of(i * 16, 16), jnp.swapaxes(read(i), 0, 1))
        return carry

    lax.fori_loop(0, whole, body, 0)
    put(whole * 16, jnp.swapaxes(tail, 0, 1))


def dense_product(left, weight_ref, dense):
    for first, blocks in ((0, 2), (2, 1)):
        got = lax.dot_general(
            left,
            weight_ref[first * 128 : (first + blocks) * 128, :],
            (((1,), (1,)), ((), ())),
            preferred_element_type=F32,
        )
        for c in range(blocks):
            dense[first + c, 0:ROWS, :] = got[:, lanes(c)]


def masked(act, t, dense, c, rows):
    return jnp.where(act[t, rows, lanes(c)].astype(F32) > 0, dense[c, rows, :], 0.0)


def finish_older(act_older, t, dense, grad_older):
    def body(i, carry):
        rows = pl.ds(pl.multiple_of(i * 16, 16), 16)
        for c in range(BLOCKS):
            grad_older[rows, lanes(c)] = masked(act_older, t, dense, c, rows).astype(BF16)
        return carry

    lax.fori_loop(0, ROWS // 16, body, 0)


def last_piece(act_last, t, dense, grad_out, grad_pass, c, rows):
    skip = grad_pass[rows, lanes(c)].astype(F32) + grad_out[rows, lanes(c)].astype(F32)
    return (skip + masked(act_last, t, dense, c, rows)).astype(BF16)


def finish_last(act_last, t, dense, grad_out, grad_pass, grad_last):
    def body(i, carry):
        rows = pl.ds(pl.multiple_of(i * 16, 16), 16)
        for c in range(BLOCKS):
            grad_last[rows, lanes(c)] = last_piece(act_last, t, dense, grad_out, grad_pass, c, rows)
        return carry

    lax.fori_loop(0, ROWS // 16, body, 0)


def three_part(t, grad_out, act_older, weight, taps, back, grad_older, wide, dense, ready):
    spread_taps(taps, wide, 9)
    dense_product(grad_out[...], weight, dense)
    to_pitched(dense, back)
    spread_conv(back, wide, dense, 3, True)
    ready()
    finish_older(act_older, t, dense, grad_older)


def five_part(t, grad_out, grad_pass, act_last, weight, taps, back, grad_last, wide, dense, ready):
    spread_taps(taps, wide, 25)
    dense_product(grad_out[...], weight, dense)
    to_pitched(dense, back)
    spread_conv(back, wide, dense, 5, True)
    ready()
    finish_last(act_last, t, dense, grad_out, grad_pass, grad_last)


def order_kernel(plan_hbm, turn_ref, plan_ref, sem):
    get = pltpu.make_async_copy(plan_hbm, plan_ref, sem)
    get.start()
    get.wait()
    for t in range(turn_ref.shape[0]):
        turn_ref[plan_ref[0, t]] = t


def slots_unpacked(turn_ref, source, target):
    def put(at, block):
        block = jnp.maximum(block, 0)
        for k in range(4):
            target[turn_ref[k], pl.ds(at, 16), :] = block[k]

    unpack(source, 4, put)


def pair_unpacked(source, grad_out, grad_pass):
    def put(at, block):
        grad_out[pl.ds(at, 16), :] = block[0]
        grad_pass[pl.ds(at, 16), :] = block[1]

    unpack(source, 2, put)


def first_three_kernel(
    turn_ref, older_in, arriving_in, weight, taps, grad_older, act_older, grad_out, grad_pass, back, wide, dense
):
    pair_unpacked(arriving_in, grad_out, grad_pass)

    def ready():
        slots_unpacked(turn_ref, older_in, act_older)

    three_part(0, grad_out, act_older, weight, taps, back, grad_older, wide, dense, ready)


def first_five_kernel(
    turn_ref, last_in, grad_out, grad_pass, weight, taps, grad_last, act_last, back, wide, dense
):
    def ready():
        slots_unpacked(turn_ref, last_in, act_last)

    five_part(0, grad_out, grad_pass, act_last, weight, taps, back, grad_last, wide, dense, ready)


def take(t, top_ref, out_in, pass_in, head_hbm, grad_out, grad_pass, head_in, sem):
    @pl.when(top_ref[0] == 1)
    def _():
        get = pltpu.make_async_copy(head_hbm.at[t - 1], head_in, sem)
        get.start()
        get.wait()
        pair_unpacked(head_in, grad_out, grad_pass)

    @pl.when(top_ref[0] != 1)
    def _():
        grad_out[...] = out_in[...]
        grad_pass[...] = pass_in[...]


def three_kernel(
    t,
    top_ref,
    out_in,
    pass_in,
    head_hbm,
    act_older,
    weight,
    taps,
    grad_older,
    grad_out,
    grad_pass,
    back,
    head_in,
    wide,
    dense,
    sem,
):
    take(t, top_ref, out_in, pass_in, head_hbm, grad_out, grad_pass, head_in, sem)
    three_part(t, grad_out, act_older, weight, taps, back, grad_older, wide, dense, lambda: None)


def five_kernel(t, grad_out, grad_pass, act_last, weight, taps, grad_last, back, wide, dense):
    five_part(t, grad_out, grad_pass, act_last, weight, taps, back, grad_last, wide, dense, lambda: None)


def both_kernel(
    t,
    top_ref,
    out_in,
    pass_in,
    head_hbm,
    act_last,
    act_older,
    weight_five,
    weight_three,
    taps_five,
    taps_three,
    made,
    grad_out,
    back_five,
    back_three,
    grad_pass,
    head_in,
    wide_five,
    wide_three,
    dense,
    sem,
):
    take(t, top_ref, out_in, pass_in, head_hbm, grad_out, grad_pass, head_in, sem)
    three_part(
        t,
        grad_out,
        act_older,
        weight_three,
        taps_three,
        back_three,
        made.at[1],
        wide_three,
        dense,
        lambda: None,
    )
    five_part(
        t,
        grad_out,
        grad_pass,
        act_last,
        weight_five,
        taps_five,
        back_five,
        made.at[0],
        wide_five,
        dense,
        lambda: None,
    )


def copies(pairs, sems):
    return [pltpu.make_async_copy(a, b, sems.at[n]) for n, (a, b) in enumerate(pairs)]


def widened(act, t, dense):
    def body(i, carry):
        rows = pl.ds(pl.multiple_of(i * 16, 16), 16)
        for c in range(BLOCKS):
            dense[c, rows, :] = act[t, rows, lanes(c)].astype(F32)
        return carry

    lax.fori_loop(0, ROWS // 16, body, 0)


def mix(act, t, taps, mixed, pitched, dense, wide, kernel):
    widened(act, t, dense)
    to_pitched(dense, pitched)
    spread_taps(taps, wide, kernel * kernel)
    for c in range(BLOCKS):
        dense[c, ROWS - 8 : ROWS, :] = jnp.zeros((8, 128), F32)
    spread_conv(pitched, wide, dense, kernel, False)

    def body(i, carry):
        rows = pl.ds(pl.multiple_of(i * 16, 16), 16)
        for c in range(BLOCKS):
            mixed[rows, lanes(c)] = dense[c, rows, :].astype(BF16)
        return carry

    lax.fori_loop(0, ROWS // 16, body, 0)


def across(mixed, left):
    return lax.dot_general(mixed, left, (((0,), (0,)), ((), ())), preferred_element_type=F32)


def grads_kernel(t, ahead, *refs):
    refs = list(refs)
    grad_out, act_last, act_older, taps_five, taps_three, back_five, back_three = refs[:7]
    refs = refs[7:]
    olds = None
    if t > 0:
        olds = refs[:4]
        refs = refs[4:]
    sums = refs[:4]
    refs = refs[4:]
    if ahead is not None:
        later = refs[:2]
        refs = refs[2:]
    pitched, dense, wide, mixed = refs
    left = grad_out[...]
    for n, (act, taps, back, kernel) in enumerate(
        ((act_last, taps_five, back_five, 5), (act_older, taps_three, back_three, 3))
    ):
        if ahead is not None:
            mix(act, ahead, taps, later[n], pitched, dense, wide, kernel)
        mix(act, t, taps, mixed, pitched, dense, wide, kernel)
        got = across(mixed[...], left)
        sums[2 * n][...] = got if olds is None else got + olds[2 * n][...]
        tap_sums(back, pitched, sums[2 * n + 1], kernel)
        if olds is not None:
            sums[2 * n + 1][...] = sums[2 * n + 1][...] + olds[2 * n + 1][...]


def last_grads_kernel(
    t,
    top_ref,
    row_ref,
    pair_in,
    head_hbm,
    act_last,
    act_older,
    weight_five,
    weight_three,
    mixed_five,
    mixed_three,
    old_five,
    old_taps_five,
    old_three,
    old_taps_three,
    *refs,
):
    sends, refs = refs[:3], refs[3:]
    own, grad_out, grad_pass, back_five, back_three = refs[:5]
    packed, head_in, pitched, dense, rows_ref, sem = refs[5:]
    scale = 1.0 / PIXELS
    take(t, top_ref, pair_in.at[0], pair_in.at[1], head_hbm, grad_out, grad_pass, head_in, sem)
    left = grad_out[...]
    packed[:, 0:CH] = (across(mixed_five[...], left) + old_five[...]) * scale
    packed[:, CH : 2 * CH] = (across(mixed_three[...], left) + old_three[...]) * scale
    rows_ref[...] = jnp.zeros(rows_ref.shape, F32)
    for act, weight, back, old, at, kernel in (
        (act_last, weight_five, back_five, old_taps_five, 0, 5),
        (act_older, weight_three, back_three, old_taps_three, 32, 3),
    ):
        dense_product(left, weight, dense)
        to_pitched(dense, back)
        widened(act, t, dense)
        to_pitched(dense, pitched)
        count = kernel * kernel
        tap_sums(back, pitched, rows_ref.at[pl.ds(at, old.shape[0])], kernel)
        rows_ref[at : at + count, :] = (rows_ref[at : at + count, :] + old[0:count, :]) * scale
    for c in range(BLOCKS):
        packed[lanes(c), 2 * CH : 2 * CH + 128] = rows_ref[:, lanes(c)].T
    height = own.shape[0]
    groups = CH // height

    def rows(distance):
        at = lax.rem(row_ref[0] + distance, groups) * height
        return pl.ds(pl.multiple_of(at, 16), height)

    own[...] = packed[rows(0), :]
    for distance, send in enumerate(sends, 1):
        send[...] = packed[rows(distance), :].astype(BF16)


def last_kernel(
    t,
    grad_out,
    grad_pass,
    back_five,
    back_three,
    act_last,
    act_older,
    taps_five,
    taps_three,
    outgoing_hbm,
    wide_five,
    wide_three,
    dense,
    made_older,
    outgoing,
    sems,
):
    spread_taps(taps_five, wide_five, 25)
    spread_taps(taps_three, wide_three, 9)
    spread_conv(back_three, wide_three, dense, 3, True)
    finish_older(act_older, t, dense, made_older)
    spread_conv(back_five, wide_five, dense, 5, True)

    def both(rows, c):
        last = last_piece(act_last, t, dense, grad_out, grad_pass, c, rows)
        return jnp.swapaxes(jnp.stack([last, made_older[rows, lanes(c)]], 0), 0, 1)

    def body(i, carry):
        rows = pl.ds(pl.multiple_of(i * 16, 16), 16)
        for c in range(BLOCKS):
            outgoing[rows, :, lanes(c)] = both(rows, c)
        return carry

    half = 224
    lax.fori_loop(0, half // 16, body, 0)
    put = copies(
        [
            (outgoing.at[pl.ds(0, half)], outgoing_hbm.at[pl.ds(0, half)]),
            (outgoing.at[pl.ds(half, PIXELS - half)], outgoing_hbm.at[pl.ds(half, PIXELS - half)]),
        ],
        sems,
    )
    put[0].start()
    lax.fori_loop(half // 16, PIXELS // 16, body, 0)
    at = PIXELS // 16 * 16
    for c in range(BLOCKS):
        outgoing[at:PIXELS, :, lanes(c)] = both(slice(at, at + 16), c)[: PIXELS - at]
    put[1].start()
    put[0].wait()
    put[1].wait()


def half_total_kernel(half_ref, own, one, two, three, kept, send):
    height = kept.shape[0]

    def summed(which):
        rows = pl.ds(pl.multiple_of(which * height, 16), height)
        total = own[rows, :]
        for landed in (one, two, three):
            total = total + landed[rows, :].astype(F32)
        return total

    kept[...] = summed(half_ref[0])
    send[...] = summed(1 - half_ref[0]).astype(BF16)


def total_kernel(kept, landed, five, three, taps_five, taps_three):
    five[...] = kept[:, 0:CH] + landed[:, 0:CH].astype(F32)
    three[...] = kept[:, CH : 2 * CH] + landed[:, CH : 2 * CH].astype(F32)
    rows = (kept[:, 2 * CH :] + landed[:, 2 * CH :].astype(F32)).T
    for taps, at in ((taps_five, 0), (taps_three, 32)):
        for k in range(taps.shape[0]):
            taps[k] = rows[at + k : at + k + 1, :]


VMEM = pl.BlockSpec(memory_space=pltpu.VMEM)
SMEM = pl.BlockSpec(memory_space=pltpu.SMEM)
ANY = pl.BlockSpec(memory_space=pl.ANY)
FLAT = jax.ShapeDtypeStruct((ROWS, CH), BF16)
WIDE = 2 * CH + 128
ACTS = jax.ShapeDtypeStruct((4, ROWS, CH), BF16)
BACK = jax.ShapeDtypeStruct((BLOCKS, PITCHED, 128), F32)
SUMS = (
    jax.ShapeDtypeStruct((CH, CH), F32),
    jax.ShapeDtypeStruct((32, CH), F32),
    jax.ShapeDtypeStruct((CH, CH), F32),
    jax.ShapeDtypeStruct((16, CH), F32),
)
FLAT_SCRATCH = pltpu.VMEM((ROWS, CH), BF16)
PAIR_SCRATCH = pltpu.VMEM((PIXELS, 2, CH), BF16)
WIDE_FIVE = pltpu.VMEM((25, BLOCKS, 8, 128), F32)
WIDE_THREE = pltpu.VMEM((9, BLOCKS, 8, 128), F32)
DENSE = pltpu.VMEM((BLOCKS, ROWS + 8, 128), F32)
PITCHED_SCRATCH = pltpu.VMEM((BLOCKS, PITCHED, 128), F32)


def run(kernel, name, operands, specs, shapes, out_specs, scratch, micros, limit=12 << 20):
    cost = pl.CostEstimate(flops=int(micros * 1e9), bytes_accessed=0, transcendentals=0)
    return pl.pallas_call(
        kernel,
        out_shape=tuple(shapes),
        in_specs=specs,
        out_specs=tuple(out_specs),
        scratch_shapes=scratch,
        compiler_params=pltpu.CompilerParams(vmem_limit_bytes=limit),
        cost_estimate=cost,
        name=name,
    )(*operands)


def call_order(plan):
    (turns,) = run(
        order_kernel,
        "order",
        (plan,),
        [ANY],
        (jax.ShapeDtypeStruct((plan.shape[1],), jnp.int32),),
        (SMEM,),
        [pltpu.SMEM(plan.shape, jnp.int32), pltpu.SemaphoreType.DMA],
        6,
    )
    return turns


def call_first_three(turns, older, arriving, weight, taps):
    return run(
        first_three_kernel,
        "first_three",
        (turns, older, arriving, weight, taps),
        [SMEM] + [VMEM] * 4,
        (FLAT, ACTS, FLAT, FLAT, BACK),
        (VMEM,) * 5,
        [WIDE_THREE, DENSE],
        4,
    )


def call_first_five(turns, last, grad_out, grad_pass, weight, taps):
    return run(
        first_five_kernel,
        "first_five",
        (turns, last, grad_out, grad_pass, weight, taps),
        [SMEM] + [VMEM] * 5,
        (FLAT, ACTS, BACK),
        (VMEM,) * 3,
        [WIDE_FIVE, DENSE],
        4,
    )


def call_three(t, given, act, weight, taps):
    return run(
        functools.partial(three_kernel, t),
        f"three_{t}",
        (*given, act, weight, taps),
        [SMEM, VMEM, VMEM, ANY] + [VMEM] * 3,
        (FLAT, FLAT, FLAT, BACK),
        (VMEM,) * 4,
        [PAIR_SCRATCH, WIDE_THREE, DENSE, pltpu.SemaphoreType.DMA],
        2,
    )


def call_five(t, grad_out, grad_pass, act, weight, taps):
    return run(
        functools.partial(five_kernel, t),
        f"five_{t}",
        (grad_out, grad_pass, act, weight, taps),
        [VMEM] * 5,
        (FLAT, BACK),
        (VMEM,) * 2,
        [WIDE_FIVE, DENSE],
        3,
    )


def call_both(t, given, acts, weights, taps):
    return run(
        functools.partial(both_kernel, t),
        f"both_{t}",
        (*given, *acts, *weights, *taps),
        [SMEM, VMEM, VMEM, ANY] + [VMEM] * 6,
        (jax.ShapeDtypeStruct((2, ROWS, CH), BF16), FLAT, BACK, BACK),
        (VMEM,) * 4,
        [FLAT_SCRATCH, PAIR_SCRATCH, WIDE_FIVE, WIDE_THREE, DENSE, pltpu.SemaphoreType.DMA],
        5,
    )


def call_grads(t, ahead, grad_out, acts, taps, backs, olds):
    shapes = SUMS if ahead is None else SUMS + (FLAT, FLAT)
    operands = (grad_out, *acts, *taps, *backs, *olds)
    return run(
        functools.partial(grads_kernel, t, ahead),
        f"grads_{t}",
        operands,
        [VMEM] * len(operands),
        shapes,
        (VMEM,) * len(shapes),
        [PITCHED_SCRATCH, DENSE, WIDE_FIVE, FLAT_SCRATCH],
        6 if ahead is None else 8,
    )


def call_last_grads(t, height, given, acts, weights, mixed, olds):
    send = jax.ShapeDtypeStruct((height, WIDE), BF16)
    own = jax.ShapeDtypeStruct((height, WIDE), F32)
    return run(
        functools.partial(last_grads_kernel, t),
        "last_grads",
        (*given, *acts, *weights, *mixed, *olds),
        [SMEM, SMEM, VMEM, ANY] + [VMEM] * 10,
        (send, send, send, own, FLAT, FLAT, BACK, BACK),
        (VMEM,) * 8,
        [
            pltpu.VMEM((CH, WIDE), F32),
            PAIR_SCRATCH,
            PITCHED_SCRATCH,
            DENSE,
            pltpu.VMEM((128, CH), F32),
            pltpu.SemaphoreType.DMA,
        ],
        6,
    )


def call_last(t, grads, backs, acts, taps):
    (outgoing,) = run(
        functools.partial(last_kernel, t),
        "last",
        (*grads, *backs, *acts, *taps),
        [VMEM] * 8,
        (jax.ShapeDtypeStruct((PIXELS, 2, CH), BF16),),
        (ANY,),
        [WIDE_FIVE, WIDE_THREE, DENSE, FLAT_SCRATCH, PAIR_SCRATCH, pltpu.SemaphoreType.DMA((2,))],
        4,
    )
    return outgoing


def call_half_total(half, own, landed):
    height = own.shape[0] // 2
    return run(
        half_total_kernel,
        "half_total",
        (half, own, *landed),
        [SMEM] + [VMEM] * 4,
        (jax.ShapeDtypeStruct((height, WIDE), F32), jax.ShapeDtypeStruct((height, WIDE), BF16)),
        (VMEM,) * 2,
        [],
        1,
    )


def whole(shape):
    zeros = (0,) * len(shape)
    return pl.BlockSpec(shape, lambda i: zeros)


def call_total(kept, landed):
    rows = kept.shape[0]
    shapes = [(rows, CH), (rows, CH), (25, 1, rows), (9, 1, rows)]
    return pl.pallas_call(
        total_kernel,
        grid=(1,),
        out_shape=tuple(jax.ShapeDtypeStruct(shape, F32) for shape in shapes),
        in_specs=[whole(kept.shape), whole(landed.shape)],
        out_specs=tuple(whole(shape) for shape in shapes),
        compiler_params=pltpu.CompilerParams(vmem_limit_bytes=12 << 20),
        name="total",
    )(kept, landed)


def by_pixel(stack):
    return jnp.transpose(stack, (0, 2, 3, 4, 1, 5)).reshape(PIXELS, stack.shape[1], CH)


def local(
    saved_last,
    saved_older,
    arriving,
    head_adjoint,
    plan,
    depth_five,
    depth_three,
    point_five,
    point_three,
):
    turns = saved_last.shape[1]
    top = (lax.axis_index("sec") == lax.axis_size("sec") - 1).astype(jnp.int32)[None]
    turn_of_slot = call_order(plan)
    image = lax.axis_index("img").astype(jnp.int32)
    group, half = (image // 2)[None], (image % 2)[None]
    turn_of_slot, top, group, half = lax.optimization_barrier((turn_of_slot, top, group, half))
    head = jnp.transpose(head_adjoint, (0, 2, 3, 4, 1, 5)).reshape(turns - 1, PIXELS, 2, CH)
    weights = (point_five[0], point_three[0])
    taps = (depth_five[0], depth_three[0])
    grad_older, act_older, grad_out, grad_pass, back_three = call_first_three(
        turn_of_slot, by_pixel(saved_older), by_pixel(arriving), weights[1], taps[1]
    )
    next_pass = from_next(grad_older)
    grad_last, act_last, back_five = call_first_five(
        turn_of_slot, by_pixel(saved_last), grad_out, grad_pass, weights[0], taps[0]
    )
    next_out = from_next(grad_last)
    acts = (act_last, act_older)
    sums = ()
    for t in range(turns - 2):
        made = call_grads(t, None, grad_out, acts, taps, (back_five, back_three), sums)
        next_out, next_pass, sums = lax.optimization_barrier((next_out, next_pass, made))
        given = (top, next_out, next_pass, head)
        if t < turns - 3:
            grad_older, grad_out, grad_pass, back_three = call_three(
                t + 1, given, act_older, weights[1], taps[1]
            )
            next_pass = from_next(grad_older)
            grad_last, back_five = call_five(
                t + 1, grad_out, grad_pass, act_last, weights[0], taps[0]
            )
            next_out = from_next(grad_last)
    both, grad_out, back_five, back_three = call_both(turns - 2, given, acts, weights, taps)
    next_pair = from_next(both)
    made = call_grads(
        turns - 2, turns - 1, grad_out, acts, taps, (back_five, back_three), sums
    )
    next_pair, made = lax.optimization_barrier((next_pair, made))
    *sends, own, grad_out, grad_pass, back_five, back_three = call_last_grads(
        turns - 1,
        CH * 2 // lax.axis_size("img"),
        (top, group, next_pair, head),
        acts,
        weights,
        made[4:],
        made[:4],
    )
    landed = [around_rows(sends[distance - 1], distance) for distance in (2, 1, 3)]
    outgoing = call_last(
        turns - 1, (grad_out, grad_pass), (back_five, back_three), acts, taps
    )
    *landed, outgoing = lax.optimization_barrier((*landed, outgoing))
    kept, send = call_half_total(half, own, landed)
    five, three, tap_five, tap_three = call_total(kept, with_partner(send))
    outgoing = outgoing.reshape(1, 1, SIDE, SIDE, 2, CH).transpose(0, 4, 1, 2, 3, 5)
    return (
        outgoing,
        five[None],
        jnp.transpose(tap_five, (1, 2, 0)),
        three[None],
        jnp.transpose(tap_three, (1, 2, 0)),
    )


def solution(mesh):
    placed = (
        P("sec", None, "img", None, None, None),
        P("sec", None, "img", None, None, None),
        P("sec", None, "img", None, None, None),
        P(None, None, "img", None, None, None),
        P("sec", None),
        P("sec", None, None),
        P("sec", None, None),
        P("sec", None, None),
        P("sec", None, None),
    )
    return jax.shard_map(
        local,
        mesh=mesh,
        in_specs=placed,
        out_specs=(
            P("sec", None, "img", None, None, None),
            P("sec", "img", None),
            P("sec", "img", None),
            P("sec", "img", None),
            P("sec", "img", None),
        ),
        check_vma=False,
    )
```

```python
import functools

import jax
import jax.numpy as jnp
from jax import lax
from jax.experimental import pallas as pl
from jax.experimental.pallas import tpu as pltpu
from jax.sharding import PartitionSpec as P

SIDE = 21
PIXELS = SIDE * SIDE
ROWS = 448
CH = 384
BLOCKS = CH // 128
PITCH = 24
EDGE = 8
PITCHED = EDGE + (SIDE + 4) * PITCH + 8
F32 = jnp.float32
BF16 = jnp.bfloat16


def from_next(block):
    size = lax.axis_size("sec")
    return lax.ppermute(block, "sec", [(i + 1, i) for i in range(size - 1)])


def around_rows(block, distance):
    rows = lax.axis_size("img") // 2
    route = [(2 * i + j, (i + distance) % rows * 2 + j) for i in range(rows) for j in range(2)]
    return lax.ppermute(block, "img", route)


def with_partner(block):
    return lax.ppermute(block, "img", [(i, i ^ 1) for i in range(lax.axis_size("img"))])


def lanes(c):
    return slice(c * 128, (c + 1) * 128)


def spread_taps(taps_ref, wide, count):
    for k in range(count):
        row = taps_ref[k : k + 1, :].astype(F32)
        for c in range(BLOCKS):
            wide[k, c] = jnp.broadcast_to(row[:, lanes(c)], (8, 128))


def clear_edges(pitched):
    top = EDGE + 2 * PITCH
    bottom = EDGE + (SIDE + 2) * PITCH
    for c in range(BLOCKS):
        pitched[c, 0:top, :] = jnp.zeros((top, 128), F32)
        pitched[c, bottom:PITCHED, :] = jnp.zeros((PITCHED - bottom, 128), F32)


def to_pitched(dense, pitched):
    inside = lax.broadcasted_iota(jnp.int32, (PITCH, 128), 0) < SIDE
    clear_edges(pitched)

    def row(i, carry):
        for c in range(BLOCKS):
            got = dense[c, pl.ds(i * SIDE, PITCH), :]
            at = pl.multiple_of(EDGE + (i + 2) * PITCH, 8)
            pitched[c, pl.ds(at, PITCH), :] = jnp.where(inside, got, 0.0)
        return carry

    lax.fori_loop(0, SIDE, row, 0, unroll=3)


def add_window(sums, got, weight_of, b, shift, rows, kernel):
    radius = kernel // 2
    for a in range(rows):
        p = b - a
        if p < 0 or p >= kernel:
            continue
        for r in range(3):
            q = shift - r + radius
            if q < 0 or q >= kernel:
                continue
            term = weight_of(p * kernel + q) * got
            old = sums[a][r]
            sums[a][r] = term if old is None else old + term


def spread_conv(pitched, wide, dense, kernel, flipped):
    radius = kernel // 2
    last = kernel * kernel - 1
    rows = 3 if kernel == 5 else 7

    def group(g, carry):
        for c in range(BLOCKS):
            sums = [[None] * 3 for _ in range(rows)]
            start = EDGE + (rows * g + 2 - radius) * PITCH
            for b in range(kernel + rows - 1):
                for shift in range(-radius, 3 + radius):
                    got = pitched[c, pl.ds(start + b * PITCH + shift, 8, stride=3), :]
                    add_window(
                        sums,
                        got,
                        lambda k: wide[last - k if flipped else k, c],
                        b,
                        shift,
                        rows,
                        kernel,
                    )
            for a in range(rows):
                for r in range(3):
                    dense[c, pl.ds((rows * g + a) * SIDE + r, 8, stride=3), :] = sums[a][r]
        return carry

    lax.fori_loop(0, SIDE // rows, group, 0)


def tap_sums(back, active, sums_ref, kernel):
    radius = kernel // 2
    count = kernel * kernel
    rows = 7
    for c in range(BLOCKS):

        def group(g, sums):
            sums = list(sums)
            here = EDGE + (rows * g + 2) * PITCH
            centre = [
                [back[c, pl.ds(here + a * PITCH + r, 8, stride=3), :] for r in range(3)]
                for a in range(rows)
            ]
            for b in range(kernel + rows - 1):
                for shift in range(-radius, 3 + radius):
                    at = here + (b - radius) * PITCH + shift
                    got = active[c, pl.ds(at, 8, stride=3), :]
                    for a in range(rows):
                        p = b - a
                        if p < 0 or p >= kernel:
                            continue
                        for r in range(3):
                            q = shift - r + radius
                            if 0 <= q < kernel:
                                k = p * kernel + q
                                sums[k] = sums[k] + got * centre[a][r]
            return tuple(sums)

        empty = tuple(jnp.zeros((8, 128), F32) for _ in range(count))
        sums = lax.fori_loop(0, SIDE // rows, group, empty)
        for k in range(count):
            sums_ref[k : k + 1, lanes(c)] = jnp.sum(sums[k], axis=0, keepdims=True)


def pieces(ref, width):
    whole = PIXELS // 16

    def read(i):
        return ref[pl.ds(i * 16, 16)]

    tail = jnp.concatenate(
        [ref[whole * 16 : PIXELS], jnp.zeros((16 - PIXELS % 16, width, CH), BF16)], 0
    )
    return whole, read, tail


def unpack(ref, width, put):
    whole, read, tail = pieces(ref, width)

    def body(i, carry):
        put(pl.multiple_of(i * 16, 16), jnp.swapaxes(read(i), 0, 1))
        return carry

    lax.fori_loop(0, whole, body, 0)
    put(whole * 16, jnp.swapaxes(tail, 0, 1))


def dense_product(left, weight_ref, dense):
    for first, blocks in ((0, 2), (2, 1)):
        got = lax.dot_general(
            left,
            weight_ref[first * 128 : (first + blocks) * 128, :],
            (((1,), (1,)), ((), ())),
            preferred_element_type=F32,
        )
        for c in range(blocks):
            dense[first + c, 0:ROWS, :] = got[:, lanes(c)]


def masked(act, t, dense, c, rows):
    return jnp.where(act[t, rows, lanes(c)].astype(F32) > 0, dense[c, rows, :], 0.0)


def finish_older(act_older, t, dense, grad_older):
    def body(i, carry):
        rows = pl.ds(pl.multiple_of(i * 16, 16), 16)
        for c in range(BLOCKS):
            grad_older[rows, lanes(c)] = masked(act_older, t, dense, c, rows).astype(BF16)
        return carry

    lax.fori_loop(0, ROWS // 16, body, 0)


def last_piece(act_last, t, dense, grad_out, grad_pass, c, rows):
    skip = grad_pass[rows, lanes(c)].astype(F32) + grad_out[rows, lanes(c)].astype(F32)
    return (skip + masked(act_last, t, dense, c, rows)).astype(BF16)


def finish_last(act_last, t, dense, grad_out, grad_pass, grad_last):
    def body(i, carry):
        rows = pl.ds(pl.multiple_of(i * 16, 16), 16)
        for c in range(BLOCKS):
            grad_last[rows, lanes(c)] = last_piece(act_last, t, dense, grad_out, grad_pass, c, rows)
        return carry

    lax.fori_loop(0, ROWS // 16, body, 0)


def three_part(t, grad_out, act_older, weight, taps, back, grad_older, wide, dense, ready):
    spread_taps(taps, wide, 9)
    dense_product(grad_out[...], weight, dense)
    to_pitched(dense, back)
    spread_conv(back, wide, dense, 3, True)
    ready()
    finish_older(act_older, t, dense, grad_older)


def five_part(t, grad_out, grad_pass, act_last, weight, taps, back, grad_last, wide, dense, ready):
    spread_taps(taps, wide, 25)
    dense_product(grad_out[...], weight, dense)
    to_pitched(dense, back)
    spread_conv(back, wide, dense, 5, True)
    ready()
    finish_last(act_last, t, dense, grad_out, grad_pass, grad_last)


def opening_kernel(token_ref):
    token_ref[0] = 0


def slots_unpacked(plan_ref, source, target):
    turns = target.shape[0]
    turn_of = [sum(jnp.where(plan_ref[0, t] == k, t, 0) for t in range(1, turns)) for k in range(turns)]

    def put(at, block):
        block = jnp.maximum(block, 0)
        for k in range(turns):
            target[turn_of[k], pl.ds(at, 16), :] = block[k]

    unpack(source, turns, put)


def pair_unpacked(source, grad_out, grad_pass):
    def put(at, block):
        grad_out[pl.ds(at, 16), :] = block[0]
        grad_pass[pl.ds(at, 16), :] = block[1]

    unpack(source, 2, put)


def first_five_kernel(
    token_ref,
    plan_ref,
    last_in,
    arriving_in,
    weight,
    taps,
    grad_last,
    act_last,
    grad_out,
    back,
    grad_pass,
    wide,
    dense,
):
    pair_unpacked(arriving_in, grad_out, grad_pass)

    def ready():
        slots_unpacked(plan_ref, last_in, act_last)

    five_part(0, grad_out, grad_pass, act_last, weight, taps, back, grad_last, wide, dense, ready)


def first_three_kernel(
    plan_ref, older_in, grad_out, weight, taps, grad_older, act_older, back, wide, dense
):
    def ready():
        slots_unpacked(plan_ref, older_in, act_older)

    three_part(0, grad_out, act_older, weight, taps, back, grad_older, wide, dense, ready)


def take(t, top_ref, out_in, pass_in, head_hbm, grad_out, grad_pass, head_in, sem):
    @pl.when(top_ref[0] == 1)
    def _():
        get = pltpu.make_async_copy(head_hbm.at[t - 1], head_in, sem)
        get.start()
        get.wait()
        pair_unpacked(head_in, grad_out, grad_pass)

    @pl.when(top_ref[0] != 1)
    def _():
        grad_out[...] = out_in[...]
        grad_pass[...] = pass_in[...]


def five_kernel(
    t,
    top_ref,
    out_in,
    pass_in,
    head_hbm,
    act_last,
    weight,
    taps,
    grad_last,
    grad_out,
    back,
    grad_pass,
    head_in,
    wide,
    dense,
    sem,
):
    take(t, top_ref, out_in, pass_in, head_hbm, grad_out, grad_pass, head_in, sem)
    five_part(t, grad_out, grad_pass, act_last, weight, taps, back, grad_last, wide, dense, lambda: None)


def three_kernel(t, grad_out, act_older, weight, taps, grad_older, back, wide, dense):
    three_part(t, grad_out, act_older, weight, taps, back, grad_older, wide, dense, lambda: None)


def both_kernel(
    t,
    top_ref,
    out_in,
    pass_in,
    head_hbm,
    act_last,
    act_older,
    weight_five,
    weight_three,
    taps_five,
    taps_three,
    made,
    grad_out,
    back_five,
    back_three,
    grad_pass,
    head_in,
    wide_five,
    wide_three,
    dense,
    sem,
):
    take(t, top_ref, out_in, pass_in, head_hbm, grad_out, grad_pass, head_in, sem)
    three_part(
        t,
        grad_out,
        act_older,
        weight_three,
        taps_three,
        back_three,
        made.at[1],
        wide_three,
        dense,
        lambda: None,
    )
    five_part(
        t,
        grad_out,
        grad_pass,
        act_last,
        weight_five,
        taps_five,
        back_five,
        made.at[0],
        wide_five,
        dense,
        lambda: None,
    )


def copies(pairs, sems):
    return [pltpu.make_async_copy(a, b, sems.at[n]) for n, (a, b) in enumerate(pairs)]


def widened(act, t, dense):
    def body(i, carry):
        rows = pl.ds(pl.multiple_of(i * 16, 16), 16)
        for c in range(BLOCKS):
            dense[c, rows, :] = act[t, rows, lanes(c)].astype(F32)
        return carry

    lax.fori_loop(0, ROWS // 16, body, 0)


def mix(act, t, taps, mixed, pitched, dense, wide, kernel):
    widened(act, t, dense)
    to_pitched(dense, pitched)
    spread_taps(taps, wide, kernel * kernel)
    for c in range(BLOCKS):
        dense[c, ROWS - 8 : ROWS, :] = jnp.zeros((8, 128), F32)
    spread_conv(pitched, wide, dense, kernel, False)

    def body(i, carry):
        rows = pl.ds(pl.multiple_of(i * 16, 16), 16)
        for c in range(BLOCKS):
            mixed[rows, lanes(c)] = dense[c, rows, :].astype(BF16)
        return carry

    lax.fori_loop(0, ROWS // 16, body, 0)


def across(mixed, left):
    return lax.dot_general(mixed, left, (((0,), (0,)), ((), ())), preferred_element_type=F32)


def grads_kernel(t, ahead, *refs):
    refs = list(refs)
    grad_out, act_last, act_older, taps_five, taps_three, back_five, back_three = refs[:7]
    refs = refs[7:]
    olds = None
    if t > 0:
        olds = refs[:4]
        refs = refs[4:]
    sums = refs[:4]
    refs = refs[4:]
    if ahead is not None:
        later = refs[:4]
        refs = refs[4:]
    pitched, dense, wide, mixed = refs
    left = grad_out[...]
    for n, (act, taps, back, kernel) in enumerate(
        ((act_last, taps_five, back_five, 5), (act_older, taps_three, back_three, 3))
    ):
        if ahead is not None:
            mix(act, ahead, taps, later[n], later[2 + n], dense, wide, kernel)
        mix(act, t, taps, mixed, pitched, dense, wide, kernel)
        got = across(mixed[...], left)
        sums[2 * n][...] = got if olds is None else got + olds[2 * n][...]
        tap_sums(back, pitched, sums[2 * n + 1], kernel)
        if olds is not None:
            sums[2 * n + 1][...] = sums[2 * n + 1][...] + olds[2 * n + 1][...]


def last_grads_kernel(
    t,
    top_ref,
    row_ref,
    pair_in,
    head_hbm,
    weight_five,
    weight_three,
    mixed_five,
    mixed_three,
    pitched_five,
    pitched_three,
    old_five,
    old_taps_five,
    old_three,
    old_taps_three,
    *refs,
):
    sends, refs = refs[:3], refs[3:]
    own, grad_out, grad_pass, back_five, back_three = refs[:5]
    packed, head_in, dense, rows_ref, sem = refs[5:]
    scale = 1.0 / PIXELS
    take(t, top_ref, pair_in.at[0], pair_in.at[1], head_hbm, grad_out, grad_pass, head_in, sem)
    left = grad_out[...]
    packed[:, 0:CH] = (across(mixed_five[...], left) + old_five[...]) * scale
    packed[:, CH : 2 * CH] = (across(mixed_three[...], left) + old_three[...]) * scale
    rows_ref[...] = jnp.zeros(rows_ref.shape, F32)
    for pitched, weight, back, old, at, kernel in (
        (pitched_five, weight_five, back_five, old_taps_five, 0, 5),
        (pitched_three, weight_three, back_three, old_taps_three, 32, 3),
    ):
        dense_product(left, weight, dense)
        to_pitched(dense, back)
        count = kernel * kernel
        tap_sums(back, pitched, rows_ref.at[pl.ds(at, old.shape[0])], kernel)
        rows_ref[at : at + count, :] = (rows_ref[at : at + count, :] + old[0:count, :]) * scale
    for c in range(BLOCKS):
        packed[lanes(c), 2 * CH : 2 * CH + 128] = rows_ref[:, lanes(c)].T
    height = own.shape[0]
    groups = CH // height

    def rows(distance):
        at = lax.rem(row_ref[0] + distance, groups) * height
        return pl.ds(pl.multiple_of(at, 16), height)

    own[...] = packed[rows(0), :]
    for distance, send in enumerate(sends, 1):
        send[...] = packed[rows(distance), :].astype(BF16)


def last_kernel(
    t,
    grad_out,
    grad_pass,
    back_five,
    back_three,
    act_last,
    act_older,
    taps_five,
    taps_three,
    outgoing_hbm,
    wide_five,
    wide_three,
    dense,
    made_older,
    outgoing,
    sems,
):
    spread_taps(taps_five, wide_five, 25)
    spread_taps(taps_three, wide_three, 9)
    spread_conv(back_three, wide_three, dense, 3, True)
    finish_older(act_older, t, dense, made_older)
    spread_conv(back_five, wide_five, dense, 5, True)

    def both(rows, c):
        last = last_piece(act_last, t, dense, grad_out, grad_pass, c, rows)
        return jnp.swapaxes(jnp.stack([last, made_older[rows, lanes(c)]], 0), 0, 1)

    def body(i, carry):
        rows = pl.ds(pl.multiple_of(i * 16, 16), 16)
        for c in range(BLOCKS):
            outgoing[rows, :, lanes(c)] = both(rows, c)
        return carry

    half = 224
    lax.fori_loop(0, half // 16, body, 0)
    put = copies(
        [
            (outgoing.at[pl.ds(0, half)], outgoing_hbm.at[pl.ds(0, half)]),
            (outgoing.at[pl.ds(half, PIXELS - half)], outgoing_hbm.at[pl.ds(half, PIXELS - half)]),
        ],
        sems,
    )
    put[0].start()
    lax.fori_loop(half // 16, PIXELS // 16, body, 0)
    at = PIXELS // 16 * 16
    for c in range(BLOCKS):
        outgoing[at:PIXELS, :, lanes(c)] = both(slice(at, at + 16), c)[: PIXELS - at]
    put[1].start()
    put[0].wait()
    put[1].wait()


def half_total_kernel(half_ref, own, one, two, three, kept, send):
    height = kept.shape[0]

    def summed(which):
        rows = pl.ds(pl.multiple_of(which * height, 16), height)
        total = own[rows, :]
        for landed in (one, two, three):
            total = total + landed[rows, :].astype(F32)
        return total

    kept[...] = summed(half_ref[0])
    send[...] = summed(1 - half_ref[0]).astype(BF16)


def total_kernel(kept, landed, five, three, taps_five, taps_three):
    five[...] = kept[:, 0:CH] + landed[:, 0:CH].astype(F32)
    three[...] = kept[:, CH : 2 * CH] + landed[:, CH : 2 * CH].astype(F32)
    rows = (kept[:, 2 * CH :] + landed[:, 2 * CH :].astype(F32)).T
    for taps, at in ((taps_five, 0), (taps_three, 32)):
        for k in range(taps.shape[0]):
            taps[k] = rows[at + k : at + k + 1, :]


VMEM = pl.BlockSpec(memory_space=pltpu.VMEM)
SMEM = pl.BlockSpec(memory_space=pltpu.SMEM)
ANY = pl.BlockSpec(memory_space=pl.ANY)
FLAT = jax.ShapeDtypeStruct((ROWS, CH), BF16)
WIDE = 2 * CH + 128
ACTS = jax.ShapeDtypeStruct((4, ROWS, CH), BF16)
BACK = jax.ShapeDtypeStruct((BLOCKS, PITCHED, 128), F32)
SUMS = (
    jax.ShapeDtypeStruct((CH, CH), F32),
    jax.ShapeDtypeStruct((32, CH), F32),
    jax.ShapeDtypeStruct((CH, CH), F32),
    jax.ShapeDtypeStruct((16, CH), F32),
)
FLAT_SCRATCH = pltpu.VMEM((ROWS, CH), BF16)
PAIR_SCRATCH = pltpu.VMEM((PIXELS, 2, CH), BF16)
WIDE_FIVE = pltpu.VMEM((25, BLOCKS, 8, 128), F32)
WIDE_THREE = pltpu.VMEM((9, BLOCKS, 8, 128), F32)
DENSE = pltpu.VMEM((BLOCKS, ROWS + 8, 128), F32)
PITCHED_SCRATCH = pltpu.VMEM((BLOCKS, PITCHED, 128), F32)


def run(kernel, name, operands, specs, shapes, out_specs, scratch, micros, limit=12 << 20):
    cost = pl.CostEstimate(flops=int(micros * 1e9), bytes_accessed=0, transcendentals=0)
    return pl.pallas_call(
        kernel,
        out_shape=tuple(shapes),
        in_specs=specs,
        out_specs=tuple(out_specs),
        scratch_shapes=scratch,
        compiler_params=pltpu.CompilerParams(vmem_limit_bytes=limit),
        cost_estimate=cost,
        name=name,
    )(*operands)


def call_opening():
    (token,) = run(
        opening_kernel,
        "opening",
        (),
        [],
        (jax.ShapeDtypeStruct((1,), jnp.int32),),
        (SMEM,),
        [],
        6,
    )
    return token


def call_first_five(token, plan, last, arriving, weight, taps):
    return run(
        first_five_kernel,
        "first_five",
        (token, plan, last, arriving, weight, taps),
        [SMEM, SMEM] + [VMEM] * 4,
        (FLAT, ACTS, FLAT, BACK),
        (VMEM,) * 4,
        [FLAT_SCRATCH, WIDE_FIVE, DENSE],
        4,
    )


def call_first_three(plan, older, grad_out, weight, taps):
    return run(
        first_three_kernel,
        "first_three",
        (plan, older, grad_out, weight, taps),
        [SMEM] + [VMEM] * 4,
        (FLAT, ACTS, BACK),
        (VMEM,) * 3,
        [WIDE_THREE, DENSE],
        3,
    )


def call_five(t, given, act, weight, taps):
    return run(
        functools.partial(five_kernel, t),
        f"five_{t}",
        (*given, act, weight, taps),
        [SMEM, VMEM, VMEM, ANY] + [VMEM] * 3,
        (FLAT, FLAT, BACK),
        (VMEM,) * 3,
        [FLAT_SCRATCH, PAIR_SCRATCH, WIDE_FIVE, DENSE, pltpu.SemaphoreType.DMA],
        3,
    )


def call_three(t, grad_out, act, weight, taps):
    return run(
        functools.partial(three_kernel, t),
        f"three_{t}",
        (grad_out, act, weight, taps),
        [VMEM] * 4,
        (FLAT, BACK),
        (VMEM,) * 2,
        [WIDE_THREE, DENSE],
        2,
    )


def call_both(t, given, acts, weights, taps):
    return run(
        functools.partial(both_kernel, t),
        f"both_{t}",
        (*given, *acts, *weights, *taps),
        [SMEM, VMEM, VMEM, ANY] + [VMEM] * 6,
        (jax.ShapeDtypeStruct((2, ROWS, CH), BF16), FLAT, BACK, BACK),
        (VMEM,) * 4,
        [FLAT_SCRATCH, PAIR_SCRATCH, WIDE_FIVE, WIDE_THREE, DENSE, pltpu.SemaphoreType.DMA],
        5,
    )


def call_grads(t, ahead, grad_out, acts, taps, backs, olds):
    shapes = SUMS if ahead is None else SUMS + (FLAT, FLAT, BACK, BACK)
    operands = (grad_out, *acts, *taps, *backs, *olds)
    return run(
        functools.partial(grads_kernel, t, ahead),
        f"grads_{t}",
        operands,
        [VMEM] * len(operands),
        shapes,
        (VMEM,) * len(shapes),
        [PITCHED_SCRATCH, DENSE, WIDE_FIVE, FLAT_SCRATCH],
        6 if ahead is None else 8,
    )


def call_last_grads(t, height, given, weights, mixed, olds):
    send = jax.ShapeDtypeStruct((height, WIDE), BF16)
    own = jax.ShapeDtypeStruct((height, WIDE), F32)
    return run(
        functools.partial(last_grads_kernel, t),
        "last_grads",
        (*given, *weights, *mixed, *olds),
        [SMEM, SMEM, VMEM, ANY] + [VMEM] * 10,
        (send, send, send, own, FLAT, FLAT, BACK, BACK),
        (VMEM,) * 8,
        [
            pltpu.VMEM((CH, WIDE), F32),
            PAIR_SCRATCH,
            DENSE,
            pltpu.VMEM((128, CH), F32),
            pltpu.SemaphoreType.DMA,
        ],
        6,
    )


def call_last(t, grads, backs, acts, taps):
    (outgoing,) = run(
        functools.partial(last_kernel, t),
        "last",
        (*grads, *backs, *acts, *taps),
        [VMEM] * 8,
        (jax.ShapeDtypeStruct((PIXELS, 2, CH), BF16),),
        (ANY,),
        [WIDE_FIVE, WIDE_THREE, DENSE, FLAT_SCRATCH, PAIR_SCRATCH, pltpu.SemaphoreType.DMA((2,))],
        4,
    )
    return outgoing


def call_half_total(half, own, landed):
    height = own.shape[0] // 2
    return run(
        half_total_kernel,
        "half_total",
        (half, own, *landed),
        [SMEM] + [VMEM] * 4,
        (jax.ShapeDtypeStruct((height, WIDE), F32), jax.ShapeDtypeStruct((height, WIDE), BF16)),
        (VMEM,) * 2,
        [],
        1,
    )


def whole(shape):
    zeros = (0,) * len(shape)
    return pl.BlockSpec(shape, lambda i: zeros)


def call_total(kept, landed):
    rows = kept.shape[0]
    shapes = [(rows, CH), (rows, CH), (25, 1, rows), (9, 1, rows)]
    return pl.pallas_call(
        total_kernel,
        grid=(1,),
        out_shape=tuple(jax.ShapeDtypeStruct(shape, F32) for shape in shapes),
        in_specs=[whole(kept.shape), whole(landed.shape)],
        out_specs=tuple(whole(shape) for shape in shapes),
        compiler_params=pltpu.CompilerParams(vmem_limit_bytes=12 << 20),
        name="total",
    )(kept, landed)


def by_pixel(stack):
    return jnp.transpose(stack, (0, 2, 3, 4, 1, 5)).reshape(PIXELS, stack.shape[1], CH)


def local(
    saved_last,
    saved_older,
    arriving,
    head_adjoint,
    plan,
    depth_five,
    depth_three,
    point_five,
    point_three,
):
    turns = saved_last.shape[1]
    top = (lax.axis_index("sec") == lax.axis_size("sec") - 1).astype(jnp.int32)[None]
    image = lax.axis_index("img").astype(jnp.int32)
    group, half = (image // 2)[None], (image % 2)[None]
    token, top, group, half = lax.optimization_barrier((call_opening(), top, group, half))
    head = jnp.transpose(head_adjoint, (0, 2, 3, 4, 1, 5)).reshape(turns - 1, PIXELS, 2, CH)
    weights = (point_five[0], point_three[0])
    taps = (depth_five[0], depth_three[0])
    grad_last, act_last, grad_out, back_five = call_first_five(
        token, plan, by_pixel(saved_last), by_pixel(arriving), weights[0], taps[0]
    )
    next_out = from_next(grad_last)
    grad_older, act_older, back_three = call_first_three(
        plan, by_pixel(saved_older), grad_out, weights[1], taps[1]
    )
    next_pass = from_next(grad_older)
    acts = (act_last, act_older)
    sums = ()
    for t in range(turns - 2):
        made = call_grads(t, None, grad_out, acts, taps, (back_five, back_three), sums)
        next_out, next_pass, sums = lax.optimization_barrier((next_out, next_pass, made))
        given = (top, next_out, next_pass, head)
        if t < turns - 3:
            grad_last, grad_out, back_five = call_five(
                t + 1, given, act_last, weights[0], taps[0]
            )
            next_out = from_next(grad_last)
            grad_older, back_three = call_three(t + 1, grad_out, act_older, weights[1], taps[1])
            next_pass = from_next(grad_older)
    both, grad_out, back_five, back_three = call_both(turns - 2, given, acts, weights, taps)
    next_pair = from_next(both)
    made = call_grads(
        turns - 2, turns - 1, grad_out, acts, taps, (back_five, back_three), sums
    )
    next_pair, made = lax.optimization_barrier((next_pair, made))
    *sends, own, grad_out, grad_pass, back_five, back_three = call_last_grads(
        turns - 1,
        CH * 2 // lax.axis_size("img"),
        (top, group, next_pair, head),
        weights,
        made[4:],
        made[:4],
    )
    landed = [around_rows(sends[distance - 1], distance) for distance in (2, 1, 3)]
    outgoing = call_last(
        turns - 1, (grad_out, grad_pass), (back_five, back_three), acts, taps
    )
    *landed, outgoing = lax.optimization_barrier((*landed, outgoing))
    kept, send = call_half_total(half, own, landed)
    five, three, tap_five, tap_three = call_total(kept, with_partner(send))
    outgoing = outgoing.reshape(1, 1, SIDE, SIDE, 2, CH).transpose(0, 4, 1, 2, 3, 5)
    return (
        outgoing,
        five[None],
        jnp.transpose(tap_five, (1, 2, 0)),
        three[None],
        jnp.transpose(tap_three, (1, 2, 0)),
    )


def solution(mesh):
    placed = (
        P("sec", None, "img", None, None, None),
        P("sec", None, "img", None, None, None),
        P("sec", None, "img", None, None, None),
        P(None, None, "img", None, None, None),
        P("sec", None),
        P("sec", None, None),
        P("sec", None, None),
        P("sec", None, None),
        P("sec", None, None),
    )
    return jax.shard_map(
        local,
        mesh=mesh,
        in_specs=placed,
        out_specs=(
            P("sec", None, "img", None, None, None),
            P("sec", "img", None),
            P("sec", "img", None),
            P("sec", "img", None),
            P("sec", "img", None),
        ),
        check_vma=False,
    )
```

```python
import functools

import jax
import jax.numpy as jnp
from jax import lax
from jax.experimental import pallas as pl
from jax.experimental.pallas import tpu as pltpu
from jax.sharding import PartitionSpec as P

SIDE = 21
PIXELS = SIDE * SIDE
ROWS = 448
CH = 384
BLOCKS = CH // 128
PITCH = 24
EDGE = 8
PITCHED = EDGE + (SIDE + 4) * PITCH + 8
F32 = jnp.float32
BF16 = jnp.bfloat16


def from_next(block):
    size = lax.axis_size("sec")
    return lax.ppermute(block, "sec", [(i + 1, i) for i in range(size - 1)])


def around_rows(block, distance):
    rows = lax.axis_size("img") // 2
    route = [(2 * i + j, (i + distance) % rows * 2 + j) for i in range(rows) for j in range(2)]
    return lax.ppermute(block, "img", route)


def with_partner(block):
    return lax.ppermute(block, "img", [(i, i ^ 1) for i in range(lax.axis_size("img"))])


def lanes(c):
    return slice(c * 128, (c + 1) * 128)


def spread_taps(taps_ref, wide, count):
    for k in range(count):
        row = taps_ref[k : k + 1, :].astype(F32)
        for c in range(BLOCKS):
            wide[k, c] = jnp.broadcast_to(row[:, lanes(c)], (8, 128))


def clear_edges(pitched):
    top = EDGE + 2 * PITCH
    bottom = EDGE + (SIDE + 2) * PITCH
    for c in range(BLOCKS):
        pitched[c, 0:top, :] = jnp.zeros((top, 128), F32)
        pitched[c, bottom:PITCHED, :] = jnp.zeros((PITCHED - bottom, 128), F32)


def to_pitched(dense, pitched):
    inside = lax.broadcasted_iota(jnp.int32, (PITCH, 128), 0) < SIDE
    clear_edges(pitched)

    def row(i, carry):
        for c in range(BLOCKS):
            got = dense[c, pl.ds(i * SIDE, PITCH), :]
            at = pl.multiple_of(EDGE + (i + 2) * PITCH, 8)
            pitched[c, pl.ds(at, PITCH), :] = jnp.where(inside, got, 0.0)
        return carry

    lax.fori_loop(0, SIDE, row, 0, unroll=3)


def add_window(sums, got, weight_of, b, shift, rows, kernel):
    radius = kernel // 2
    for a in range(rows):
        p = b - a
        if p < 0 or p >= kernel:
            continue
        for r in range(3):
            q = shift - r + radius
            if q < 0 or q >= kernel:
                continue
            term = weight_of(p * kernel + q) * got
            old = sums[a][r]
            sums[a][r] = term if old is None else old + term


def spread_conv(pitched, wide, dense, kernel, flipped):
    radius = kernel // 2
    last = kernel * kernel - 1
    rows = 3 if kernel == 5 else 7

    def group(g, carry):
        for c in range(BLOCKS):
            sums = [[None] * 3 for _ in range(rows)]
            start = EDGE + (rows * g + 2 - radius) * PITCH
            for b in range(kernel + rows - 1):
                for shift in range(-radius, 3 + radius):
                    got = pitched[c, pl.ds(start + b * PITCH + shift, 8, stride=3), :]
                    add_window(
                        sums,
                        got,
                        lambda k: wide[last - k if flipped else k, c],
                        b,
                        shift,
                        rows,
                        kernel,
                    )
            for a in range(rows):
                for r in range(3):
                    dense[c, pl.ds((rows * g + a) * SIDE + r, 8, stride=3), :] = sums[a][r]
        return carry

    lax.fori_loop(0, SIDE // rows, group, 0)


def tap_sums(back, active, sums_ref, kernel):
    radius = kernel // 2
    count = kernel * kernel
    rows = 7
    for c in range(BLOCKS):

        def group(g, sums):
            sums = list(sums)
            here = EDGE + (rows * g + 2) * PITCH
            centre = [
                [back[c, pl.ds(here + a * PITCH + r, 8, stride=3), :] for r in range(3)]
                for a in range(rows)
            ]
            for b in range(kernel + rows - 1):
                for shift in range(-radius, 3 + radius):
                    at = here + (b - radius) * PITCH + shift
                    got = active[c, pl.ds(at, 8, stride=3), :]
                    for a in range(rows):
                        p = b - a
                        if p < 0 or p >= kernel:
                            continue
                        for r in range(3):
                            q = shift - r + radius
                            if 0 <= q < kernel:
                                k = p * kernel + q
                                sums[k] = sums[k] + got * centre[a][r]
            return tuple(sums)

        empty = tuple(jnp.zeros((8, 128), F32) for _ in range(count))
        sums = lax.fori_loop(0, SIDE // rows, group, empty)
        for k in range(count):
            sums_ref[k : k + 1, lanes(c)] = jnp.sum(sums[k], axis=0, keepdims=True)


def pieces(ref, width):
    whole = PIXELS // 16

    def read(i):
        return ref[pl.ds(i * 16, 16)]

    tail = jnp.concatenate(
        [ref[whole * 16 : PIXELS], jnp.zeros((16 - PIXELS % 16, width, CH), BF16)], 0
    )
    return whole, read, tail


def unpack(ref, width, put):
    whole, read, tail = pieces(ref, width)

    def body(i, carry):
        put(pl.multiple_of(i * 16, 16), jnp.swapaxes(read(i), 0, 1))
        return carry

    lax.fori_loop(0, whole, body, 0)
    put(whole * 16, jnp.swapaxes(tail, 0, 1))


def dense_product(left, weight_ref, dense):
    for first, blocks in ((0, 2), (2, 1)):
        got = lax.dot_general(
            left,
            weight_ref[first * 128 : (first + blocks) * 128, :],
            (((1,), (1,)), ((), ())),
            preferred_element_type=F32,
        )
        for c in range(blocks):
            dense[first + c, 0:ROWS, :] = got[:, lanes(c)]


def masked(act, t, dense, c, rows):
    return jnp.where(act[t, rows, lanes(c)].astype(F32) > 0, dense[c, rows, :], 0.0)


def finish_older(act_older, t, dense, grad_older):
    def body(i, carry):
        rows = pl.ds(pl.multiple_of(i * 16, 16), 16)
        for c in range(BLOCKS):
            grad_older[rows, lanes(c)] = masked(act_older, t, dense, c, rows).astype(BF16)
        return carry

    lax.fori_loop(0, ROWS // 16, body, 0)


def last_piece(act_last, t, dense, grad_out, grad_pass, c, rows):
    skip = grad_pass[rows, lanes(c)].astype(F32) + grad_out[rows, lanes(c)].astype(F32)
    return (skip + masked(act_last, t, dense, c, rows)).astype(BF16)


def finish_last(act_last, t, dense, grad_out, grad_pass, grad_last):
    def body(i, carry):
        rows = pl.ds(pl.multiple_of(i * 16, 16), 16)
        for c in range(BLOCKS):
            grad_last[rows, lanes(c)] = last_piece(act_last, t, dense, grad_out, grad_pass, c, rows)
        return carry

    lax.fori_loop(0, ROWS // 16, body, 0)


def three_part(t, grad_out, act_older, weight, taps, back, grad_older, wide, dense, ready):
    spread_taps(taps, wide, 9)
    dense_product(grad_out[...], weight, dense)
    to_pitched(dense, back)
    spread_conv(back, wide, dense, 3, True)
    ready()
    finish_older(act_older, t, dense, grad_older)


def five_part(t, grad_out, grad_pass, act_last, weight, taps, back, grad_last, wide, dense, ready):
    spread_taps(taps, wide, 25)
    dense_product(grad_out[...], weight, dense)
    to_pitched(dense, back)
    spread_conv(back, wide, dense, 5, True)
    ready()
    finish_last(act_last, t, dense, grad_out, grad_pass, grad_last)


def opening_kernel(token_ref):
    token_ref[0] = 0


def slots_unpacked(plan_ref, source, target):
    turns = target.shape[0]
    turn_of = [sum(jnp.where(plan_ref[0, t] == k, t, 0) for t in range(1, turns)) for k in range(turns)]

    def put(at, block):
        block = jnp.maximum(block, 0)
        for k in range(turns):
            target[turn_of[k], pl.ds(at, 16), :] = block[k]

    unpack(source, turns, put)


def pair_unpacked(source, grad_out, grad_pass):
    def put(at, block):
        grad_out[pl.ds(at, 16), :] = block[0]
        grad_pass[pl.ds(at, 16), :] = block[1]

    unpack(source, 2, put)


def first_five_kernel(
    token_ref,
    plan_ref,
    last_in,
    arriving_in,
    weight,
    taps,
    grad_last,
    act_last,
    grad_out,
    back,
    grad_pass,
    wide,
    dense,
):
    pair_unpacked(arriving_in, grad_out, grad_pass)

    def ready():
        slots_unpacked(plan_ref, last_in, act_last)

    five_part(0, grad_out, grad_pass, act_last, weight, taps, back, grad_last, wide, dense, ready)


def first_three_kernel(
    plan_ref, older_in, grad_out, weight, taps, grad_older, act_older, back, wide, dense
):
    def ready():
        slots_unpacked(plan_ref, older_in, act_older)

    three_part(0, grad_out, act_older, weight, taps, back, grad_older, wide, dense, ready)


def take(t, top_ref, out_in, head_hbm, grad_out, head_pass, head_in, sem):
    @pl.when(top_ref[0] == 1)
    def _():
        get = pltpu.make_async_copy(head_hbm.at[t - 1], head_in, sem)
        get.start()
        get.wait()
        pair_unpacked(head_in, grad_out, head_pass)

    @pl.when(top_ref[0] != 1)
    def _():
        grad_out[...] = out_in[...]


def five_kernel(
    t, top_ref, out_in, head_hbm, weight, taps, through, grad_out, head_pass, back, head_in, wide, dense, sem
):
    take(t, top_ref, out_in, head_hbm, grad_out, head_pass, head_in, sem)
    spread_taps(taps, wide, 25)
    dense_product(grad_out[...], weight, dense)
    to_pitched(dense, back)
    spread_conv(back, wide, through, 5, True)


def finish(t, top_ref, pass_in, head_pass, grad_out, act_last, through, grad_last):
    @pl.when(top_ref[0] == 1)
    def _():
        finish_last(act_last, t, through, grad_out, head_pass, grad_last)

    @pl.when(top_ref[0] != 1)
    def _():
        finish_last(act_last, t, through, grad_out, pass_in, grad_last)


def finish_kernel(t, top_ref, pass_in, head_pass, grad_out, act_last, through, grad_last):
    finish(t, top_ref, pass_in, head_pass, grad_out, act_last, through, grad_last)


def three_kernel(t, grad_out, act_older, weight, taps, grad_older, back, wide, dense):
    three_part(t, grad_out, act_older, weight, taps, back, grad_older, wide, dense, lambda: None)


def both_kernel(
    t,
    top_ref,
    pass_in,
    head_pass,
    grad_out,
    act_last,
    act_older,
    through,
    weight,
    taps,
    made,
    back,
    wide,
    dense,
):
    three_part(t, grad_out, act_older, weight, taps, back, made.at[1], wide, dense, lambda: None)
    finish(t, top_ref, pass_in, head_pass, grad_out, act_last, through, made.at[0])


def copies(pairs, sems):
    return [pltpu.make_async_copy(a, b, sems.at[n]) for n, (a, b) in enumerate(pairs)]


def widened(act, t, dense):
    def body(i, carry):
        rows = pl.ds(pl.multiple_of(i * 16, 16), 16)
        for c in range(BLOCKS):
            dense[c, rows, :] = act[t, rows, lanes(c)].astype(F32)
        return carry

    lax.fori_loop(0, ROWS // 16, body, 0)


def mix(act, t, taps, mixed, pitched, dense, wide, kernel):
    widened(act, t, dense)
    to_pitched(dense, pitched)
    spread_taps(taps, wide, kernel * kernel)
    for c in range(BLOCKS):
        dense[c, ROWS - 8 : ROWS, :] = jnp.zeros((8, 128), F32)
    spread_conv(pitched, wide, dense, kernel, False)

    def body(i, carry):
        rows = pl.ds(pl.multiple_of(i * 16, 16), 16)
        for c in range(BLOCKS):
            mixed[rows, lanes(c)] = dense[c, rows, :].astype(BF16)
        return carry

    lax.fori_loop(0, ROWS // 16, body, 0)


def across(mixed, left):
    return lax.dot_general(mixed, left, (((0,), (0,)), ((), ())), preferred_element_type=F32)


def grads_kernel(t, *refs):
    act_last, act_older, taps_five, taps_three, back_five, back_three = refs[:6]
    refs = refs[6:]
    olds = (None, None)
    if t > 0:
        olds, refs = refs[:2], refs[2:]
    sums, mixes = refs[:2], refs[2:4]
    pitched, dense, wide = refs[4:]
    for act, taps, back, kernel, old, total, mixed in (
        (act_last, taps_five, back_five, 5, olds[0], sums[0], mixes[0]),
        (act_older, taps_three, back_three, 3, olds[1], sums[1], mixes[1]),
    ):
        mix(act, t, taps, mixed, pitched, dense, wide, kernel)
        tap_sums(back, pitched, total, kernel)
        if old is not None:
            total[...] = total[...] + old[...]


def gather_kernel(t, *refs):
    act_last, act_older, taps_five, taps_three, back_five, back_three = refs[:6]
    old_taps, refs = refs[6:8], refs[8:]
    grads, refs = refs[: t + 1], refs[t + 1 :]
    mixed_before, refs = refs[: 2 * t], refs[2 * t :]
    points, sums, ahead, refs = refs[:2], refs[2:4], refs[4:8], refs[8:]
    pitched, dense, wide, mixed = refs
    for n, (act, taps, back, kernel) in enumerate(
        ((act_last, taps_five, back_five, 5), (act_older, taps_three, back_three, 3))
    ):
        mix(act, t + 1, taps, ahead[n], ahead[2 + n], dense, wide, kernel)
        mix(act, t, taps, mixed, pitched, dense, wide, kernel)
        points[n][...] = across(mixed[...], grads[t][...])
        for before in range(t):
            points[n][...] += across(mixed_before[2 * before + n][...], grads[before][...])
        tap_sums(back, pitched, sums[n], kernel)
        sums[n][...] = sums[n][...] + old_taps[n][...]


def last_grads_kernel(
    t,
    top_ref,
    row_ref,
    pair_in,
    head_hbm,
    weight_five,
    weight_three,
    mixed_five,
    mixed_three,
    pitched_five,
    pitched_three,
    old_five,
    old_three,
    old_taps_five,
    old_taps_three,
    *refs,
):
    sends, refs = refs[:3], refs[3:]
    own, grad_out, grad_pass, back_five, back_three = refs[:5]
    packed, head_in, dense, rows_ref, sem = refs[5:]
    scale = 1.0 / PIXELS
    take(t, top_ref, pair_in.at[0], head_hbm, grad_out, grad_pass, head_in, sem)

    @pl.when(top_ref[0] != 1)
    def _():
        grad_pass[...] = pair_in[1]

    left = grad_out[...]
    packed[:, 0:CH] = (across(mixed_five[...], left) + old_five[...]) * scale
    packed[:, CH : 2 * CH] = (across(mixed_three[...], left) + old_three[...]) * scale
    rows_ref[...] = jnp.zeros(rows_ref.shape, F32)
    for pitched, weight, back, old, at, kernel in (
        (pitched_five, weight_five, back_five, old_taps_five, 0, 5),
        (pitched_three, weight_three, back_three, old_taps_three, 32, 3),
    ):
        dense_product(left, weight, dense)
        to_pitched(dense, back)
        count = kernel * kernel
        tap_sums(back, pitched, rows_ref.at[pl.ds(at, old.shape[0])], kernel)
        rows_ref[at : at + count, :] = (rows_ref[at : at + count, :] + old[0:count, :]) * scale
    for c in range(BLOCKS):
        packed[lanes(c), 2 * CH : 2 * CH + 128] = rows_ref[:, lanes(c)].T
    height = own.shape[0]
    groups = CH // height

    def rows(distance):
        at = lax.rem(row_ref[0] + distance, groups) * height
        return pl.ds(pl.multiple_of(at, 16), height)

    own[...] = packed[rows(0), :]
    for distance, send in enumerate(sends, 1):
        send[...] = packed[rows(distance), :].astype(BF16)


def last_kernel(
    t,
    grad_out,
    grad_pass,
    back_five,
    back_three,
    act_last,
    act_older,
    taps_five,
    taps_three,
    outgoing_hbm,
    wide_five,
    wide_three,
    dense,
    made_older,
    outgoing,
    sems,
):
    spread_taps(taps_five, wide_five, 25)
    spread_taps(taps_three, wide_three, 9)
    spread_conv(back_three, wide_three, dense, 3, True)
    finish_older(act_older, t, dense, made_older)
    spread_conv(back_five, wide_five, dense, 5, True)

    def both(rows, c):
        last = last_piece(act_last, t, dense, grad_out, grad_pass, c, rows)
        return jnp.swapaxes(jnp.stack([last, made_older[rows, lanes(c)]], 0), 0, 1)

    def body(i, carry):
        rows = pl.ds(pl.multiple_of(i * 16, 16), 16)
        for c in range(BLOCKS):
            outgoing[rows, :, lanes(c)] = both(rows, c)
        return carry

    half = 224
    lax.fori_loop(0, half // 16, body, 0)
    put = copies(
        [
            (outgoing.at[pl.ds(0, half)], outgoing_hbm.at[pl.ds(0, half)]),
            (outgoing.at[pl.ds(half, PIXELS - half)], outgoing_hbm.at[pl.ds(half, PIXELS - half)]),
        ],
        sems,
    )
    put[0].start()
    lax.fori_loop(half // 16, PIXELS // 16, body, 0)
    at = PIXELS // 16 * 16
    for c in range(BLOCKS):
        outgoing[at:PIXELS, :, lanes(c)] = both(slice(at, at + 16), c)[: PIXELS - at]
    put[1].start()
    put[0].wait()
    put[1].wait()


def half_total_kernel(half_ref, own, one, two, three, kept, send):
    height = kept.shape[0]

    def summed(which):
        rows = pl.ds(pl.multiple_of(which * height, 16), height)
        total = own[rows, :]
        for landed in (one, two, three):
            total = total + landed[rows, :].astype(F32)
        return total

    kept[...] = summed(half_ref[0])
    send[...] = summed(1 - half_ref[0]).astype(BF16)


def total_kernel(kept, landed, five, three, taps_five, taps_three):
    five[...] = kept[:, 0:CH] + landed[:, 0:CH].astype(F32)
    three[...] = kept[:, CH : 2 * CH] + landed[:, CH : 2 * CH].astype(F32)
    rows = (kept[:, 2 * CH :] + landed[:, 2 * CH :].astype(F32)).T
    for taps, at in ((taps_five, 0), (taps_three, 32)):
        for k in range(taps.shape[0]):
            taps[k] = rows[at + k : at + k + 1, :]


VMEM = pl.BlockSpec(memory_space=pltpu.VMEM)
SMEM = pl.BlockSpec(memory_space=pltpu.SMEM)
ANY = pl.BlockSpec(memory_space=pl.ANY)
FLAT = jax.ShapeDtypeStruct((ROWS, CH), BF16)
WIDE = 2 * CH + 128
THROUGH = jax.ShapeDtypeStruct((BLOCKS, ROWS + 8, 128), F32)
ACTS = jax.ShapeDtypeStruct((4, ROWS, CH), BF16)
BACK = jax.ShapeDtypeStruct((BLOCKS, PITCHED, 128), F32)
POINTS = jax.ShapeDtypeStruct((CH, CH), F32)
SUMS = (jax.ShapeDtypeStruct((32, CH), F32), jax.ShapeDtypeStruct((16, CH), F32))
FLAT_SCRATCH = pltpu.VMEM((ROWS, CH), BF16)
PAIR_SCRATCH = pltpu.VMEM((PIXELS, 2, CH), BF16)
WIDE_FIVE = pltpu.VMEM((25, BLOCKS, 8, 128), F32)
WIDE_THREE = pltpu.VMEM((9, BLOCKS, 8, 128), F32)
DENSE = pltpu.VMEM((BLOCKS, ROWS + 8, 128), F32)
PITCHED_SCRATCH = pltpu.VMEM((BLOCKS, PITCHED, 128), F32)


def run(kernel, name, operands, specs, shapes, out_specs, scratch, micros, limit=12 << 20):
    cost = pl.CostEstimate(flops=int(micros * 1e9), bytes_accessed=0, transcendentals=0)
    return pl.pallas_call(
        kernel,
        out_shape=tuple(shapes),
        in_specs=specs,
        out_specs=tuple(out_specs),
        scratch_shapes=scratch,
        compiler_params=pltpu.CompilerParams(vmem_limit_bytes=limit),
        cost_estimate=cost,
        name=name,
    )(*operands)


def call_opening():
    (token,) = run(
        opening_kernel,
        "opening",
        (),
        [],
        (jax.ShapeDtypeStruct((1,), jnp.int32),),
        (SMEM,),
        [],
        6,
    )
    return token


def call_first_five(token, plan, last, arriving, weight, taps):
    return run(
        first_five_kernel,
        "first_five",
        (token, plan, last, arriving, weight, taps),
        [SMEM, SMEM] + [VMEM] * 4,
        (FLAT, ACTS, FLAT, BACK),
        (VMEM,) * 4,
        [FLAT_SCRATCH, WIDE_FIVE, DENSE],
        4,
    )


def call_first_three(plan, older, grad_out, weight, taps):
    return run(
        first_three_kernel,
        "first_three",
        (plan, older, grad_out, weight, taps),
        [SMEM] + [VMEM] * 4,
        (FLAT, ACTS, BACK),
        (VMEM,) * 3,
        [WIDE_THREE, DENSE],
        3,
    )


def call_five(t, given, weight, taps):
    return run(
        functools.partial(five_kernel, t),
        f"five_{t}",
        (*given, weight, taps),
        [SMEM, VMEM, ANY] + [VMEM] * 2,
        (THROUGH, FLAT, FLAT, BACK),
        (VMEM,) * 4,
        [PAIR_SCRATCH, WIDE_FIVE, DENSE, pltpu.SemaphoreType.DMA],
        3,
    )


def call_finish(t, *operands):
    (grad_last,) = run(
        functools.partial(finish_kernel, t),
        f"finish_{t}",
        operands,
        [SMEM] + [VMEM] * 5,
        (FLAT,),
        (VMEM,),
        [],
        1,
    )
    return grad_last


def call_three(t, grad_out, act, weight, taps):
    return run(
        functools.partial(three_kernel, t),
        f"three_{t}",
        (grad_out, act, weight, taps),
        [VMEM] * 4,
        (FLAT, BACK),
        (VMEM,) * 2,
        [WIDE_THREE, DENSE],
        2,
    )


def call_both(t, *operands):
    return run(
        functools.partial(both_kernel, t),
        f"both_{t}",
        operands,
        [SMEM] + [VMEM] * 8,
        (jax.ShapeDtypeStruct((2, ROWS, CH), BF16), BACK),
        (VMEM,) * 2,
        [WIDE_THREE, DENSE],
        2,
    )


def call_grads(t, acts, taps, backs, olds):
    operands = (*acts, *taps, *backs, *olds)
    return run(
        functools.partial(grads_kernel, t),
        f"grads_{t}",
        operands,
        [VMEM] * len(operands),
        (*SUMS, FLAT, FLAT),
        (VMEM,) * 4,
        [PITCHED_SCRATCH, DENSE, WIDE_FIVE],
        5,
    )


def call_gather(t, acts, taps, backs, olds, grads, mixes):
    operands = (*acts, *taps, *backs, *olds, *grads, *mixes)
    return run(
        functools.partial(gather_kernel, t),
        f"gather_{t}",
        operands,
        [VMEM] * len(operands),
        (POINTS, POINTS, *SUMS, FLAT, FLAT, BACK, BACK),
        (VMEM,) * 8,
        [PITCHED_SCRATCH, DENSE, WIDE_FIVE, FLAT_SCRATCH],
        10,
    )


def call_last_grads(t, height, given, weights, mixed, olds):
    send = jax.ShapeDtypeStruct((height, WIDE), BF16)
    own = jax.ShapeDtypeStruct((height, WIDE), F32)
    return run(
        functools.partial(last_grads_kernel, t),
        "last_grads",
        (*given, *weights, *mixed, *olds),
        [SMEM, SMEM, VMEM, ANY] + [VMEM] * 10,
        (send, send, send, own, FLAT, FLAT, BACK, BACK),
        (VMEM,) * 8,
        [
            pltpu.VMEM((CH, WIDE), F32),
            PAIR_SCRATCH,
            DENSE,
            pltpu.VMEM((128, CH), F32),
            pltpu.SemaphoreType.DMA,
        ],
        6,
    )


def call_last(t, grads, backs, acts, taps):
    (outgoing,) = run(
        functools.partial(last_kernel, t),
        "last",
        (*grads, *backs, *acts, *taps),
        [VMEM] * 8,
        (jax.ShapeDtypeStruct((PIXELS, 2, CH), BF16),),
        (ANY,),
        [WIDE_FIVE, WIDE_THREE, DENSE, FLAT_SCRATCH, PAIR_SCRATCH, pltpu.SemaphoreType.DMA((2,))],
        4,
    )
    return outgoing


def call_half_total(half, own, landed):
    height = own.shape[0] // 2
    return run(
        half_total_kernel,
        "half_total",
        (half, own, *landed),
        [SMEM] + [VMEM] * 4,
        (jax.ShapeDtypeStruct((height, WIDE), F32), jax.ShapeDtypeStruct((height, WIDE), BF16)),
        (VMEM,) * 2,
        [],
        1,
    )


def whole(shape):
    zeros = (0,) * len(shape)
    return pl.BlockSpec(shape, lambda i: zeros)


def call_total(kept, landed):
    rows = kept.shape[0]
    shapes = [(rows, CH), (rows, CH), (25, 1, rows), (9, 1, rows)]
    return pl.pallas_call(
        total_kernel,
        grid=(1,),
        out_shape=tuple(jax.ShapeDtypeStruct(shape, F32) for shape in shapes),
        in_specs=[whole(kept.shape), whole(landed.shape)],
        out_specs=tuple(whole(shape) for shape in shapes),
        compiler_params=pltpu.CompilerParams(vmem_limit_bytes=12 << 20),
        name="total",
    )(kept, landed)


def by_pixel(stack):
    return jnp.transpose(stack, (0, 2, 3, 4, 1, 5)).reshape(PIXELS, stack.shape[1], CH)


def local(
    saved_last,
    saved_older,
    arriving,
    head_adjoint,
    plan,
    depth_five,
    depth_three,
    point_five,
    point_three,
):
    turns = saved_last.shape[1]
    top = (lax.axis_index("sec") == lax.axis_size("sec") - 1).astype(jnp.int32)[None]
    image = lax.axis_index("img").astype(jnp.int32)
    group, half = (image // 2)[None], (image % 2)[None]
    token, top, group, half = lax.optimization_barrier((call_opening(), top, group, half))
    head = jnp.transpose(head_adjoint, (0, 2, 3, 4, 1, 5)).reshape(turns - 1, PIXELS, 2, CH)
    weights = (point_five[0], point_three[0])
    taps = (depth_five[0], depth_three[0])
    grad_last, act_last, grad_out, back_five = call_first_five(
        token, plan, by_pixel(saved_last), by_pixel(arriving), weights[0], taps[0]
    )
    next_out = from_next(grad_last)
    grad_older, act_older, back_three = call_first_three(
        plan, by_pixel(saved_older), grad_out, weights[1], taps[1]
    )
    next_pass = from_next(grad_older)
    acts = (act_last, act_older)
    sums, mixes, grads = (), (), (grad_out,)
    for t in range(turns - 2):
        made = call_grads(t, acts, taps, (back_five, back_three), sums)
        next_out, made = lax.optimization_barrier((next_out, made))
        sums, mixes = made[:2], (*mixes, *made[2:])
        through, grad_out, head_pass, back_five = call_five(
            t + 1, (top, next_out, head), weights[0], taps[0]
        )
        grads = (*grads, grad_out)
        skip = (top, next_pass, head_pass, grad_out)
        if t < turns - 3:
            grad_last = call_finish(t + 1, *skip, act_last, through)
            next_out = from_next(grad_last)
            ready, _ = lax.optimization_barrier((grad_out, grad_last))
            grad_older, back_three = call_three(t + 1, ready, act_older, weights[1], taps[1])
            next_pass = from_next(grad_older)
    both, back_three = call_both(turns - 2, *skip, *acts, through, weights[1], taps[1])
    next_pair = from_next(both)
    made = call_gather(turns - 2, acts, taps, (back_five, back_three), sums, grads, mixes)
    next_pair, made = lax.optimization_barrier((next_pair, made))
    *sends, own, grad_out, grad_pass, back_five, back_three = call_last_grads(
        turns - 1,
        CH * 2 // lax.axis_size("img"),
        (top, group, next_pair, head),
        weights,
        made[4:],
        made[:4],
    )
    landed = [around_rows(sends[distance - 1], distance) for distance in (2, 1, 3)]
    outgoing = call_last(
        turns - 1, (grad_out, grad_pass), (back_five, back_three), acts, taps
    )
    *landed, outgoing = lax.optimization_barrier((*landed, outgoing))
    kept, send = call_half_total(half, own, landed)
    five, three, tap_five, tap_three = call_total(kept, with_partner(send))
    outgoing = outgoing.reshape(1, 1, SIDE, SIDE, 2, CH).transpose(0, 4, 1, 2, 3, 5)
    return (
        outgoing,
        five[None],
        jnp.transpose(tap_five, (1, 2, 0)),
        three[None],
        jnp.transpose(tap_three, (1, 2, 0)),
    )


def solution(mesh):
    placed = (
        P("sec", None, "img", None, None, None),
        P("sec", None, "img", None, None, None),
        P("sec", None, "img", None, None, None),
        P(None, None, "img", None, None, None),
        P("sec", None),
        P("sec", None, None),
        P("sec", None, None),
        P("sec", None, None),
        P("sec", None, None),
    )
    return jax.shard_map(
        local,
        mesh=mesh,
        in_specs=placed,
        out_specs=(
            P("sec", None, "img", None, None, None),
            P("sec", "img", None),
            P("sec", "img", None),
            P("sec", "img", None),
            P("sec", "img", None),
        ),
        check_vma=False,
    )
```

```python
import functools

import jax
import jax.numpy as jnp
from jax import lax
from jax.experimental import pallas as pl
from jax.experimental.pallas import tpu as pltpu
from jax.sharding import PartitionSpec as P

SIDE = 21
PIXELS = SIDE * SIDE
ROWS = 448
CH = 384
BLOCKS = CH // 128
PITCH = 24
EDGE = 8
PITCHED = EDGE + (SIDE + 4) * PITCH + 8
F32 = jnp.float32
BF16 = jnp.bfloat16


def from_next(block):
    size = lax.axis_size("sec")
    return lax.ppermute(block, "sec", [(i + 1, i) for i in range(size - 1)])


def around_rows(block, distance):
    rows = lax.axis_size("img") // 2
    route = [(2 * i + j, (i + distance) % rows * 2 + j) for i in range(rows) for j in range(2)]
    return lax.ppermute(block, "img", route)


def with_partner(block):
    return lax.ppermute(block, "img", [(i, i ^ 1) for i in range(lax.axis_size("img"))])


def lanes(c):
    return slice(c * 128, (c + 1) * 128)


def spread_taps(taps_ref, wide, count):
    for k in range(count):
        row = taps_ref[k : k + 1, :].astype(F32)
        for c in range(BLOCKS):
            wide[k, c] = jnp.broadcast_to(row[:, lanes(c)], (8, 128))


def clear_edges(pitched):
    top = EDGE + 2 * PITCH
    bottom = EDGE + (SIDE + 2) * PITCH
    for c in range(BLOCKS):
        pitched[c, 0:top, :] = jnp.zeros((top, 128), F32)
        pitched[c, bottom:PITCHED, :] = jnp.zeros((PITCHED - bottom, 128), F32)


def to_pitched(dense, pitched):
    inside = lax.broadcasted_iota(jnp.int32, (PITCH, 128), 0) < SIDE
    clear_edges(pitched)

    def row(i, carry):
        for c in range(BLOCKS):
            got = dense[c, pl.ds(i * SIDE, PITCH), :]
            at = pl.multiple_of(EDGE + (i + 2) * PITCH, 8)
            pitched[c, pl.ds(at, PITCH), :] = jnp.where(inside, got, 0.0)
        return carry

    lax.fori_loop(0, SIDE, row, 0, unroll=7)


def add_window(sums, got, weight_of, b, shift, rows, kernel):
    radius = kernel // 2
    for a in range(rows):
        p = b - a
        if p < 0 or p >= kernel:
            continue
        for r in range(3):
            q = shift - r + radius
            if q < 0 or q >= kernel:
                continue
            term = weight_of(p * kernel + q) * got
            old = sums[a][r]
            sums[a][r] = term if old is None else old + term


def spread_conv(pitched, wide, dense, kernel, flipped):
    radius = kernel // 2
    last = kernel * kernel - 1
    rows = 3 if kernel == 5 else 7

    def group(g, carry):
        for c in range(BLOCKS):
            sums = [[None] * 3 for _ in range(rows)]
            start = EDGE + (rows * g + 2 - radius) * PITCH
            for b in range(kernel + rows - 1):
                for shift in range(-radius, 3 + radius):
                    got = pitched[c, pl.ds(start + b * PITCH + shift, 8, stride=3), :]
                    add_window(
                        sums,
                        got,
                        lambda k: wide[last - k if flipped else k, c],
                        b,
                        shift,
                        rows,
                        kernel,
                    )
            for a in range(rows):
                for r in range(3):
                    dense[c, pl.ds((rows * g + a) * SIDE + r, 8, stride=3), :] = sums[a][r]
        return carry

    lax.fori_loop(0, SIDE // rows, group, 0)


def tap_sums(back, active, sums_ref, kernel):
    radius = kernel // 2
    count = kernel * kernel
    rows = 7
    for c in range(BLOCKS):

        def group(g, sums):
            sums = list(sums)
            here = EDGE + (rows * g + 2) * PITCH
            centre = [
                [back[c, pl.ds(here + a * PITCH + r, 8, stride=3), :] for r in range(3)]
                for a in range(rows)
            ]
            for b in range(kernel + rows - 1):
                for shift in range(-radius, 3 + radius):
                    at = here + (b - radius) * PITCH + shift
                    got = active[c, pl.ds(at, 8, stride=3), :]
                    for a in range(rows):
                        p = b - a
                        if p < 0 or p >= kernel:
                            continue
                        for r in range(3):
                            q = shift - r + radius
                            if 0 <= q < kernel:
                                k = p * kernel + q
                                sums[k] = sums[k] + got * centre[a][r]
            return tuple(sums)

        empty = tuple(jnp.zeros((8, 128), F32) for _ in range(count))
        sums = lax.fori_loop(0, SIDE // rows, group, empty)
        for k in range(count):
            sums_ref[k : k + 1, lanes(c)] = jnp.sum(sums[k], axis=0, keepdims=True)


def pieces(ref, width):
    whole = PIXELS // 16

    def read(i):
        return ref[pl.ds(i * 16, 16)]

    tail = jnp.concatenate(
        [ref[whole * 16 : PIXELS], jnp.zeros((16 - PIXELS % 16, width, CH), BF16)], 0
    )
    return whole, read, tail


def unpack(ref, width, put):
    whole, read, tail = pieces(ref, width)

    def body(i, carry):
        put(pl.multiple_of(i * 16, 16), jnp.swapaxes(read(i), 0, 1))
        return carry

    lax.fori_loop(0, whole, body, 0, unroll=9)
    put(whole * 16, jnp.swapaxes(tail, 0, 1))


def dense_product(left, weight_ref, dense):
    for first, blocks in ((0, 2), (2, 1)):
        got = lax.dot_general(
            left,
            weight_ref[first * 128 : (first + blocks) * 128, :],
            (((1,), (1,)), ((), ())),
            preferred_element_type=F32,
        )
        for c in range(blocks):
            dense[first + c, 0:ROWS, :] = got[:, lanes(c)]


def masked(act, t, dense, c, rows):
    return jnp.where(act[t, rows, lanes(c)].astype(F32) > 0, dense[c, rows, :], 0.0)


def finish_older(act_older, t, dense, grad_older):
    def body(i, carry):
        rows = pl.ds(pl.multiple_of(i * 16, 16), 16)
        for c in range(BLOCKS):
            grad_older[rows, lanes(c)] = masked(act_older, t, dense, c, rows).astype(BF16)
        return carry

    lax.fori_loop(0, ROWS // 16, body, 0, unroll=7)


def last_piece(act_last, t, dense, grad_out, grad_pass, c, rows):
    skip = grad_pass[rows, lanes(c)].astype(F32) + grad_out[rows, lanes(c)].astype(F32)
    return (skip + masked(act_last, t, dense, c, rows)).astype(BF16)


def finish_last(act_last, t, dense, grad_out, grad_pass, grad_last):
    def body(i, carry):
        rows = pl.ds(pl.multiple_of(i * 16, 16), 16)
        for c in range(BLOCKS):
            grad_last[rows, lanes(c)] = last_piece(act_last, t, dense, grad_out, grad_pass, c, rows)
        return carry

    lax.fori_loop(0, ROWS // 16, body, 0, unroll=7)


def three_part(t, grad_out, act_older, weight, taps, back, grad_older, wide, dense, ready):
    spread_taps(taps, wide, 9)
    dense_product(grad_out[...], weight, dense)
    to_pitched(dense, back)
    spread_conv(back, wide, dense, 3, True)
    ready()
    finish_older(act_older, t, dense, grad_older)


def five_part(t, grad_out, grad_pass, act_last, weight, taps, back, grad_last, wide, dense, ready):
    spread_taps(taps, wide, 25)
    dense_product(grad_out[...], weight, dense)
    to_pitched(dense, back)
    spread_conv(back, wide, dense, 5, True)
    ready()
    finish_last(act_last, t, dense, grad_out, grad_pass, grad_last)


def opening_kernel(token_ref):
    token_ref[0] = 0


def slots_unpacked(plan_ref, source, target):
    turns = target.shape[0]
    turn_of = [sum(jnp.where(plan_ref[0, t] == k, t, 0) for t in range(1, turns)) for k in range(turns)]

    def put(at, block):
        block = jnp.maximum(block, 0)
        for k in range(turns):
            target[turn_of[k], pl.ds(at, 16), :] = block[k]

    unpack(source, turns, put)


def pair_unpacked(source, grad_out, grad_pass):
    def put(at, block):
        grad_out[pl.ds(at, 16), :] = block[0]
        grad_pass[pl.ds(at, 16), :] = block[1]

    unpack(source, 2, put)


def first_five_kernel(
    token_ref,
    plan_ref,
    last_in,
    arriving_in,
    weight,
    taps,
    grad_last,
    act_last,
    grad_out,
    back,
    grad_pass,
    wide,
    dense,
):
    pair_unpacked(arriving_in, grad_out, grad_pass)

    def ready():
        slots_unpacked(plan_ref, last_in, act_last)

    five_part(0, grad_out, grad_pass, act_last, weight, taps, back, grad_last, wide, dense, ready)


def first_three_kernel(
    plan_ref, older_in, grad_out, weight, taps, grad_older, act_older, back, wide, dense
):
    def ready():
        slots_unpacked(plan_ref, older_in, act_older)

    three_part(0, grad_out, act_older, weight, taps, back, grad_older, wide, dense, ready)


def take(t, top_ref, out_in, head_hbm, grad_out, head_pass, head_in, sem):
    @pl.when(top_ref[0] == 1)
    def _():
        get = pltpu.make_async_copy(head_hbm.at[t - 1], head_in, sem)
        get.start()
        get.wait()
        pair_unpacked(head_in, grad_out, head_pass)

    @pl.when(top_ref[0] != 1)
    def _():
        grad_out[...] = out_in[...]


def five_kernel(
    t, top_ref, out_in, head_hbm, weight, taps, through, grad_out, head_pass, back, head_in, wide, dense, sem
):
    take(t, top_ref, out_in, head_hbm, grad_out, head_pass, head_in, sem)
    spread_taps(taps, wide, 25)
    dense_product(grad_out[...], weight, dense)
    to_pitched(dense, back)
    spread_conv(back, wide, through, 5, True)


def finish(t, top_ref, pass_in, head_pass, grad_out, act_last, through, grad_last):
    @pl.when(top_ref[0] == 1)
    def _():
        finish_last(act_last, t, through, grad_out, head_pass, grad_last)

    @pl.when(top_ref[0] != 1)
    def _():
        finish_last(act_last, t, through, grad_out, pass_in, grad_last)


def finish_kernel(t, top_ref, pass_in, head_pass, grad_out, act_last, through, grad_last):
    finish(t, top_ref, pass_in, head_pass, grad_out, act_last, through, grad_last)


def three_kernel(t, grad_out, act_older, weight, taps, grad_older, back, wide, dense):
    three_part(t, grad_out, act_older, weight, taps, back, grad_older, wide, dense, lambda: None)


def both_kernel(
    t,
    top_ref,
    pass_in,
    head_pass,
    grad_out,
    act_last,
    act_older,
    through,
    weight,
    taps,
    made,
    back,
    wide,
    dense,
):
    three_part(t, grad_out, act_older, weight, taps, back, made.at[1], wide, dense, lambda: None)
    finish(t, top_ref, pass_in, head_pass, grad_out, act_last, through, made.at[0])


def copies(pairs, sems):
    return [pltpu.make_async_copy(a, b, sems.at[n]) for n, (a, b) in enumerate(pairs)]


def widened(act, t, dense):
    def body(i, carry):
        rows = pl.ds(pl.multiple_of(i * 16, 16), 16)
        for c in range(BLOCKS):
            dense[c, rows, :] = act[t, rows, lanes(c)].astype(F32)
        return carry

    lax.fori_loop(0, ROWS // 16, body, 0, unroll=14)


def mix(act, t, taps, mixed, pitched, dense, wide, kernel):
    widened(act, t, dense)
    to_pitched(dense, pitched)
    spread_taps(taps, wide, kernel * kernel)
    for c in range(BLOCKS):
        dense[c, ROWS - 8 : ROWS, :] = jnp.zeros((8, 128), F32)
    spread_conv(pitched, wide, dense, kernel, False)

    def body(i, carry):
        rows = pl.ds(pl.multiple_of(i * 16, 16), 16)
        for c in range(BLOCKS):
            mixed[rows, lanes(c)] = dense[c, rows, :].astype(BF16)
        return carry

    lax.fori_loop(0, ROWS // 16, body, 0, unroll=14)


def across(mixed, left):
    return lax.dot_general(mixed, left, (((0,), (0,)), ((), ())), preferred_element_type=F32)


def grads_kernel(t, *refs):
    act_last, act_older, taps_five, taps_three, back_five, back_three = refs[:6]
    refs = refs[6:]
    olds = (None, None)
    if t > 0:
        olds, refs = refs[:2], refs[2:]
    sums, mixes = refs[:2], refs[2:4]
    pitched, dense, wide = refs[4:]
    for act, taps, back, kernel, old, total, mixed in (
        (act_last, taps_five, back_five, 5, olds[0], sums[0], mixes[0]),
        (act_older, taps_three, back_three, 3, olds[1], sums[1], mixes[1]),
    ):
        mix(act, t, taps, mixed, pitched, dense, wide, kernel)
        tap_sums(back, pitched, total, kernel)
        if old is not None:
            total[...] = total[...] + old[...]


def gather_kernel(t, *refs):
    act_last, act_older, taps_five, taps_three, back_five, back_three = refs[:6]
    old_taps, refs = refs[6:8], refs[8:]
    grads, refs = refs[: t + 1], refs[t + 1 :]
    mixed_before, refs = refs[: 2 * t], refs[2 * t :]
    points, sums, ahead, refs = refs[:2], refs[2:4], refs[4:8], refs[8:]
    pitched, dense, wide, mixed = refs
    for n, (act, taps, back, kernel) in enumerate(
        ((act_last, taps_five, back_five, 5), (act_older, taps_three, back_three, 3))
    ):
        mix(act, t + 1, taps, ahead[n], ahead[2 + n], dense, wide, kernel)
        mix(act, t, taps, mixed, pitched, dense, wide, kernel)
        points[n][...] = across(mixed[...], grads[t][...])
        for before in range(t):
            points[n][...] += across(mixed_before[2 * before + n][...], grads[before][...])
        tap_sums(back, pitched, sums[n], kernel)
        sums[n][...] = sums[n][...] + old_taps[n][...]


def last_grads_kernel(
    t,
    top_ref,
    row_ref,
    pair_in,
    head_hbm,
    weight_five,
    weight_three,
    mixed_five,
    mixed_three,
    pitched_five,
    pitched_three,
    old_five,
    old_three,
    old_taps_five,
    old_taps_three,
    *refs,
):
    sends, refs = refs[:3], refs[3:]
    own, grad_out, grad_pass, back_five, back_three = refs[:5]
    packed, head_in, dense, rows_ref, sem = refs[5:]
    scale = 1.0 / PIXELS
    take(t, top_ref, pair_in.at[0], head_hbm, grad_out, grad_pass, head_in, sem)

    @pl.when(top_ref[0] != 1)
    def _():
        grad_pass[...] = pair_in[1]

    left = grad_out[...]
    packed[:, 0:CH] = (across(mixed_five[...], left) + old_five[...]) * scale
    packed[:, CH : 2 * CH] = (across(mixed_three[...], left) + old_three[...]) * scale
    rows_ref[...] = jnp.zeros(rows_ref.shape, F32)
    for pitched, weight, back, old, at, kernel in (
        (pitched_five, weight_five, back_five, old_taps_five, 0, 5),
        (pitched_three, weight_three, back_three, old_taps_three, 32, 3),
    ):
        dense_product(left, weight, dense)
        to_pitched(dense, back)
        count = kernel * kernel
        tap_sums(back, pitched, rows_ref.at[pl.ds(at, old.shape[0])], kernel)
        rows_ref[at : at + count, :] = (rows_ref[at : at + count, :] + old[0:count, :]) * scale
    for c in range(BLOCKS):
        packed[lanes(c), 2 * CH : 2 * CH + 128] = rows_ref[:, lanes(c)].T
    height = own.shape[0]
    groups = CH // height

    def rows(distance):
        at = lax.rem(row_ref[0] + distance, groups) * height
        return pl.ds(pl.multiple_of(at, 16), height)

    own[...] = packed[rows(0), :]
    for distance, send in enumerate(sends, 1):
        send[...] = packed[rows(distance), :].astype(BF16)


def last_kernel(
    t,
    grad_out,
    grad_pass,
    back_five,
    back_three,
    act_last,
    act_older,
    taps_five,
    taps_three,
    outgoing_hbm,
    wide_five,
    wide_three,
    dense,
    made_older,
    outgoing,
    sems,
):
    spread_taps(taps_five, wide_five, 25)
    spread_taps(taps_three, wide_three, 9)
    spread_conv(back_three, wide_three, dense, 3, True)
    finish_older(act_older, t, dense, made_older)
    spread_conv(back_five, wide_five, dense, 5, True)

    def both(rows, c):
        last = last_piece(act_last, t, dense, grad_out, grad_pass, c, rows)
        return jnp.swapaxes(jnp.stack([last, made_older[rows, lanes(c)]], 0), 0, 1)

    def body(i, carry):
        rows = pl.ds(pl.multiple_of(i * 16, 16), 16)
        for c in range(BLOCKS):
            outgoing[rows, :, lanes(c)] = both(rows, c)
        return carry

    half = 224
    lax.fori_loop(0, half // 16, body, 0)
    put = copies(
        [
            (outgoing.at[pl.ds(0, half)], outgoing_hbm.at[pl.ds(0, half)]),
            (outgoing.at[pl.ds(half, PIXELS - half)], outgoing_hbm.at[pl.ds(half, PIXELS - half)]),
        ],
        sems,
    )
    put[0].start()
    lax.fori_loop(half // 16, PIXELS // 16, body, 0)
    at = PIXELS // 16 * 16
    for c in range(BLOCKS):
        outgoing[at:PIXELS, :, lanes(c)] = both(slice(at, at + 16), c)[: PIXELS - at]
    put[1].start()
    put[0].wait()
    put[1].wait()


def half_total_kernel(half_ref, own, one, two, three, kept, send):
    height = kept.shape[0]

    def summed(which):
        rows = pl.ds(pl.multiple_of(which * height, 16), height)
        total = own[rows, :]
        for landed in (one, two, three):
            total = total + landed[rows, :].astype(F32)
        return total

    kept[...] = summed(half_ref[0])
    send[...] = summed(1 - half_ref[0]).astype(BF16)


def total_kernel(kept, landed, five, three, taps_five, taps_three):
    five[...] = kept[:, 0:CH] + landed[:, 0:CH].astype(F32)
    three[...] = kept[:, CH : 2 * CH] + landed[:, CH : 2 * CH].astype(F32)
    rows = (kept[:, 2 * CH :] + landed[:, 2 * CH :].astype(F32)).T
    for taps, at in ((taps_five, 0), (taps_three, 32)):
        for k in range(taps.shape[0]):
            taps[k] = rows[at + k : at + k + 1, :]


VMEM = pl.BlockSpec(memory_space=pltpu.VMEM)
SMEM = pl.BlockSpec(memory_space=pltpu.SMEM)
ANY = pl.BlockSpec(memory_space=pl.ANY)
FLAT = jax.ShapeDtypeStruct((ROWS, CH), BF16)
WIDE = 2 * CH + 128
THROUGH = jax.ShapeDtypeStruct((BLOCKS, ROWS + 8, 128), F32)
ACTS = jax.ShapeDtypeStruct((4, ROWS, CH), BF16)
BACK = jax.ShapeDtypeStruct((BLOCKS, PITCHED, 128), F32)
POINTS = jax.ShapeDtypeStruct((CH, CH), F32)
SUMS = (jax.ShapeDtypeStruct((32, CH), F32), jax.ShapeDtypeStruct((16, CH), F32))
FLAT_SCRATCH = pltpu.VMEM((ROWS, CH), BF16)
PAIR_SCRATCH = pltpu.VMEM((PIXELS, 2, CH), BF16)
WIDE_FIVE = pltpu.VMEM((25, BLOCKS, 8, 128), F32)
WIDE_THREE = pltpu.VMEM((9, BLOCKS, 8, 128), F32)
DENSE = pltpu.VMEM((BLOCKS, ROWS + 8, 128), F32)
PITCHED_SCRATCH = pltpu.VMEM((BLOCKS, PITCHED, 128), F32)


def run(kernel, name, operands, specs, shapes, out_specs, scratch, micros, limit=12 << 20):
    cost = pl.CostEstimate(flops=int(micros * 1e9), bytes_accessed=0, transcendentals=0)
    return pl.pallas_call(
        kernel,
        out_shape=tuple(shapes),
        in_specs=specs,
        out_specs=tuple(out_specs),
        scratch_shapes=scratch,
        compiler_params=pltpu.CompilerParams(vmem_limit_bytes=limit),
        cost_estimate=cost,
        name=name,
    )(*operands)


def call_opening():
    (token,) = run(
        opening_kernel,
        "opening",
        (),
        [],
        (jax.ShapeDtypeStruct((1,), jnp.int32),),
        (SMEM,),
        [],
        6,
    )
    return token


def call_first_five(token, plan, last, arriving, weight, taps):
    return run(
        first_five_kernel,
        "first_five",
        (token, plan, last, arriving, weight, taps),
        [SMEM, SMEM] + [VMEM] * 4,
        (FLAT, ACTS, FLAT, BACK),
        (VMEM,) * 4,
        [FLAT_SCRATCH, WIDE_FIVE, DENSE],
        4,
    )


def call_first_three(plan, older, grad_out, weight, taps):
    return run(
        first_three_kernel,
        "first_three",
        (plan, older, grad_out, weight, taps),
        [SMEM] + [VMEM] * 4,
        (FLAT, ACTS, BACK),
        (VMEM,) * 3,
        [WIDE_THREE, DENSE],
        3,
    )


def call_five(t, given, weight, taps):
    return run(
        functools.partial(five_kernel, t),
        f"five_{t}",
        (*given, weight, taps),
        [SMEM, VMEM, ANY] + [VMEM] * 2,
        (THROUGH, FLAT, FLAT, BACK),
        (VMEM,) * 4,
        [PAIR_SCRATCH, WIDE_FIVE, DENSE, pltpu.SemaphoreType.DMA],
        3,
    )


def call_finish(t, *operands):
    (grad_last,) = run(
        functools.partial(finish_kernel, t),
        f"finish_{t}",
        operands,
        [SMEM] + [VMEM] * 5,
        (FLAT,),
        (VMEM,),
        [],
        1,
    )
    return grad_last


def call_three(t, grad_out, act, weight, taps):
    return run(
        functools.partial(three_kernel, t),
        f"three_{t}",
        (grad_out, act, weight, taps),
        [VMEM] * 4,
        (FLAT, BACK),
        (VMEM,) * 2,
        [WIDE_THREE, DENSE],
        2,
    )


def call_both(t, *operands):
    return run(
        functools.partial(both_kernel, t),
        f"both_{t}",
        operands,
        [SMEM] + [VMEM] * 8,
        (jax.ShapeDtypeStruct((2, ROWS, CH), BF16), BACK),
        (VMEM,) * 2,
        [WIDE_THREE, DENSE],
        2,
    )


def call_grads(t, acts, taps, backs, olds):
    operands = (*acts, *taps, *backs, *olds)
    return run(
        functools.partial(grads_kernel, t),
        f"grads_{t}",
        operands,
        [VMEM] * len(operands),
        (*SUMS, FLAT, FLAT),
        (VMEM,) * 4,
        [PITCHED_SCRATCH, DENSE, WIDE_FIVE],
        5,
    )


def call_gather(t, acts, taps, backs, olds, grads, mixes):
    operands = (*acts, *taps, *backs, *olds, *grads, *mixes)
    return run(
        functools.partial(gather_kernel, t),
        f"gather_{t}",
        operands,
        [VMEM] * len(operands),
        (POINTS, POINTS, *SUMS, FLAT, FLAT, BACK, BACK),
        (VMEM,) * 8,
        [PITCHED_SCRATCH, DENSE, WIDE_FIVE, FLAT_SCRATCH],
        10,
    )


def call_last_grads(t, height, given, weights, mixed, olds):
    send = jax.ShapeDtypeStruct((height, WIDE), BF16)
    own = jax.ShapeDtypeStruct((height, WIDE), F32)
    return run(
        functools.partial(last_grads_kernel, t),
        "last_grads",
        (*given, *weights, *mixed, *olds),
        [SMEM, SMEM, VMEM, ANY] + [VMEM] * 10,
        (send, send, send, own, FLAT, FLAT, BACK, BACK),
        (VMEM,) * 8,
        [
            pltpu.VMEM((CH, WIDE), F32),
            PAIR_SCRATCH,
            DENSE,
            pltpu.VMEM((128, CH), F32),
            pltpu.SemaphoreType.DMA,
        ],
        6,
    )


def call_last(t, grads, backs, acts, taps):
    (outgoing,) = run(
        functools.partial(last_kernel, t),
        "last",
        (*grads, *backs, *acts, *taps),
        [VMEM] * 8,
        (jax.ShapeDtypeStruct((PIXELS, 2, CH), BF16),),
        (ANY,),
        [WIDE_FIVE, WIDE_THREE, DENSE, FLAT_SCRATCH, PAIR_SCRATCH, pltpu.SemaphoreType.DMA((2,))],
        4,
    )
    return outgoing


def call_half_total(half, own, landed):
    height = own.shape[0] // 2
    return run(
        half_total_kernel,
        "half_total",
        (half, own, *landed),
        [SMEM] + [VMEM] * 4,
        (jax.ShapeDtypeStruct((height, WIDE), F32), jax.ShapeDtypeStruct((height, WIDE), BF16)),
        (VMEM,) * 2,
        [],
        1,
    )


def whole(shape):
    zeros = (0,) * len(shape)
    return pl.BlockSpec(shape, lambda i: zeros)


def call_total(kept, landed):
    rows = kept.shape[0]
    shapes = [(rows, CH), (rows, CH), (25, 1, rows), (9, 1, rows)]
    return pl.pallas_call(
        total_kernel,
        grid=(1,),
        out_shape=tuple(jax.ShapeDtypeStruct(shape, F32) for shape in shapes),
        in_specs=[whole(kept.shape), whole(landed.shape)],
        out_specs=tuple(whole(shape) for shape in shapes),
        compiler_params=pltpu.CompilerParams(vmem_limit_bytes=12 << 20),
        name="total",
    )(kept, landed)


def by_pixel(stack):
    return jnp.transpose(stack, (0, 2, 3, 4, 1, 5)).reshape(PIXELS, stack.shape[1], CH)


def local(
    saved_last,
    saved_older,
    arriving,
    head_adjoint,
    plan,
    depth_five,
    depth_three,
    point_five,
    point_three,
):
    turns = saved_last.shape[1]
    top = (lax.axis_index("sec") == lax.axis_size("sec") - 1).astype(jnp.int32)[None]
    image = lax.axis_index("img").astype(jnp.int32)
    group, half = (image // 2)[None], (image % 2)[None]
    token, top, group, half = lax.optimization_barrier((call_opening(), top, group, half))
    head = jnp.transpose(head_adjoint, (0, 2, 3, 4, 1, 5)).reshape(turns - 1, PIXELS, 2, CH)
    weights = (point_five[0], point_three[0])
    taps = (depth_five[0], depth_three[0])
    grad_last, act_last, grad_out, back_five = call_first_five(
        token, plan, by_pixel(saved_last), by_pixel(arriving), weights[0], taps[0]
    )
    next_out = from_next(grad_last)
    grad_older, act_older, back_three = call_first_three(
        plan, by_pixel(saved_older), grad_out, weights[1], taps[1]
    )
    next_pass = from_next(grad_older)
    acts = (act_last, act_older)
    sums, mixes, grads = (), (), (grad_out,)
    for t in range(turns - 2):
        made = call_grads(t, acts, taps, (back_five, back_three), sums)
        next_out, made = lax.optimization_barrier((next_out, made))
        sums, mixes = made[:2], (*mixes, *made[2:])
        through, grad_out, head_pass, back_five = call_five(
            t + 1, (top, next_out, head), weights[0], taps[0]
        )
        grads = (*grads, grad_out)
        skip = (top, next_pass, head_pass, grad_out)
        if t < turns - 3:
            grad_last = call_finish(t + 1, *skip, act_last, through)
            next_out = from_next(grad_last)
            ready, _ = lax.optimization_barrier((grad_out, grad_last))
            grad_older, back_three = call_three(t + 1, ready, act_older, weights[1], taps[1])
            next_pass = from_next(grad_older)
    both, back_three = call_both(turns - 2, *skip, *acts, through, weights[1], taps[1])
    next_pair = from_next(both)
    made = call_gather(turns - 2, acts, taps, (back_five, back_three), sums, grads, mixes)
    next_pair, made = lax.optimization_barrier((next_pair, made))
    *sends, own, grad_out, grad_pass, back_five, back_three = call_last_grads(
        turns - 1,
        CH * 2 // lax.axis_size("img"),
        (top, group, next_pair, head),
        weights,
        made[4:],
        made[:4],
    )
    landed = [around_rows(sends[distance - 1], distance) for distance in (2, 1, 3)]
    outgoing = call_last(
        turns - 1, (grad_out, grad_pass), (back_five, back_three), acts, taps
    )
    *landed, outgoing = lax.optimization_barrier((*landed, outgoing))
    kept, send = call_half_total(half, own, landed)
    five, three, tap_five, tap_three = call_total(kept, with_partner(send))
    outgoing = outgoing.reshape(1, 1, SIDE, SIDE, 2, CH).transpose(0, 4, 1, 2, 3, 5)
    return (
        outgoing,
        five[None],
        jnp.transpose(tap_five, (1, 2, 0)),
        three[None],
        jnp.transpose(tap_three, (1, 2, 0)),
    )


def solution(mesh):
    placed = (
        P("sec", None, "img", None, None, None),
        P("sec", None, "img", None, None, None),
        P("sec", None, "img", None, None, None),
        P(None, None, "img", None, None, None),
        P("sec", None),
        P("sec", None, None),
        P("sec", None, None),
        P("sec", None, None),
        P("sec", None, None),
    )
    return jax.shard_map(
        local,
        mesh=mesh,
        in_specs=placed,
        out_specs=(
            P("sec", None, "img", None, None, None),
            P("sec", "img", None),
            P("sec", "img", None),
            P("sec", "img", None),
            P("sec", "img", None),
        ),
        check_vma=False,
    )
```

```python
import functools

import jax
import jax.numpy as jnp
from jax import lax
from jax.experimental import pallas as pl
from jax.experimental.pallas import tpu as pltpu
from jax.sharding import PartitionSpec as P

SIDE = 21
PIXELS = SIDE * SIDE
ROWS = 448
CH = 384
BLOCKS = CH // 128
PITCH = 24
EDGE = 8
PITCHED = EDGE + (SIDE + 4) * PITCH + 8
F32 = jnp.float32
BF16 = jnp.bfloat16


def from_next(block):
    size = lax.axis_size("sec")
    return lax.ppermute(block, "sec", [(i + 1, i) for i in range(size - 1)])


def around_rows(block, distance):
    rows = lax.axis_size("img") // 2
    route = [(2 * i + j, (i + distance) % rows * 2 + j) for i in range(rows) for j in range(2)]
    return lax.ppermute(block, "img", route)


def with_partner(block):
    return lax.ppermute(block, "img", [(i, i ^ 1) for i in range(lax.axis_size("img"))])


def lanes(c):
    return slice(c * 128, (c + 1) * 128)


def spread_taps(taps_ref, wide, count):
    for k in range(count):
        row = taps_ref[k : k + 1, :].astype(F32)
        for c in range(BLOCKS):
            wide[k, c] = jnp.broadcast_to(row[:, lanes(c)], (8, 128))


def clear_edges(pitched):
    top = EDGE + 2 * PITCH
    bottom = EDGE + (SIDE + 2) * PITCH
    for c in range(BLOCKS):
        pitched[c, 0:top, :] = jnp.zeros((top, 128), F32)
        pitched[c, bottom:PITCHED, :] = jnp.zeros((PITCHED - bottom, 128), F32)


def to_pitched(dense, pitched):
    inside = lax.broadcasted_iota(jnp.int32, (PITCH, 128), 0) < SIDE
    clear_edges(pitched)

    def row(i, carry):
        for c in range(BLOCKS):
            got = dense[c, pl.ds(i * SIDE, PITCH), :]
            at = pl.multiple_of(EDGE + (i + 2) * PITCH, 8)
            pitched[c, pl.ds(at, PITCH), :] = jnp.where(inside, got, 0.0)
        return carry

    lax.fori_loop(0, SIDE, row, 0, unroll=7)


def add_window(sums, got, weight_of, b, shift, rows, kernel):
    radius = kernel // 2
    for a in range(rows):
        p = b - a
        if p < 0 or p >= kernel:
            continue
        for r in range(3):
            q = shift - r + radius
            if q < 0 or q >= kernel:
                continue
            term = weight_of(p * kernel + q) * got
            old = sums[a][r]
            sums[a][r] = term if old is None else old + term


def spread_conv(pitched, wide, dense, kernel, flipped):
    radius = kernel // 2
    last = kernel * kernel - 1
    rows = 3 if kernel == 5 else 7

    def group(g, carry):
        for c in range(BLOCKS):
            sums = [[None] * 3 for _ in range(rows)]
            start = EDGE + (rows * g + 2 - radius) * PITCH
            for b in range(kernel + rows - 1):
                for shift in range(-radius, 3 + radius):
                    got = pitched[c, pl.ds(start + b * PITCH + shift, 8, stride=3), :]
                    add_window(
                        sums,
                        got,
                        lambda k: wide[last - k if flipped else k, c],
                        b,
                        shift,
                        rows,
                        kernel,
                    )
            for a in range(rows):
                for r in range(3):
                    dense[c, pl.ds((rows * g + a) * SIDE + r, 8, stride=3), :] = sums[a][r]
        return carry

    lax.fori_loop(0, SIDE // rows, group, 0)


def tap_sums(back, active, sums_ref, kernel):
    radius = kernel // 2
    count = kernel * kernel
    rows = 7
    for c in range(BLOCKS):

        def group(g, sums):
            sums = list(sums)
            here = EDGE + (rows * g + 2) * PITCH
            centre = [
                [back[c, pl.ds(here + a * PITCH + r, 8, stride=3), :] for r in range(3)]
                for a in range(rows)
            ]
            for b in range(kernel + rows - 1):
                for shift in range(-radius, 3 + radius):
                    at = here + (b - radius) * PITCH + shift
                    got = active[c, pl.ds(at, 8, stride=3), :]
                    for a in range(rows):
                        p = b - a
                        if p < 0 or p >= kernel:
                            continue
                        for r in range(3):
                            q = shift - r + radius
                            if 0 <= q < kernel:
                                k = p * kernel + q
                                sums[k] = sums[k] + got * centre[a][r]
            return tuple(sums)

        empty = tuple(jnp.zeros((8, 128), F32) for _ in range(count))
        sums = lax.fori_loop(0, SIDE // rows, group, empty)
        for k in range(count):
            sums_ref[k : k + 1, lanes(c)] = jnp.sum(sums[k], axis=0, keepdims=True)


def pieces(ref, width):
    whole = PIXELS // 16

    def read(i):
        return ref[pl.ds(i * 16, 16)]

    tail = jnp.concatenate(
        [ref[whole * 16 : PIXELS], jnp.zeros((16 - PIXELS % 16, width, CH), BF16)], 0
    )
    return whole, read, tail


def unpack(ref, width, put):
    whole, read, tail = pieces(ref, width)

    def body(i, carry):
        put(pl.multiple_of(i * 16, 16), jnp.swapaxes(read(i), 0, 1))
        return carry

    lax.fori_loop(0, whole, body, 0, unroll=9)
    put(whole * 16, jnp.swapaxes(tail, 0, 1))


def dense_product(left, weight_ref, dense):
    for first, blocks in ((0, 2), (2, 1)):
        got = lax.dot_general(
            left,
            weight_ref[first * 128 : (first + blocks) * 128, :],
            (((1,), (1,)), ((), ())),
            preferred_element_type=F32,
        )
        for c in range(blocks):
            dense[first + c, 0:ROWS, :] = got[:, lanes(c)]


def masked(act, t, dense, c, rows):
    return jnp.where(act[t, rows, lanes(c)].astype(F32) > 0, dense[c, rows, :], 0.0)


def finish_older(act_older, t, dense, grad_older):
    def body(i, carry):
        rows = pl.ds(pl.multiple_of(i * 16, 16), 16)
        for c in range(BLOCKS):
            grad_older[rows, lanes(c)] = masked(act_older, t, dense, c, rows).astype(BF16)
        return carry

    lax.fori_loop(0, ROWS // 16, body, 0, unroll=7)


def last_piece(act_last, t, dense, grad_out, grad_pass, c, rows):
    skip = grad_pass[rows, lanes(c)].astype(F32) + grad_out[rows, lanes(c)].astype(F32)
    return (skip + masked(act_last, t, dense, c, rows)).astype(BF16)


def finish_last(act_last, t, dense, grad_out, grad_pass, grad_last):
    def body(i, carry):
        rows = pl.ds(pl.multiple_of(i * 16, 16), 16)
        for c in range(BLOCKS):
            grad_last[rows, lanes(c)] = last_piece(act_last, t, dense, grad_out, grad_pass, c, rows)
        return carry

    lax.fori_loop(0, ROWS // 16, body, 0, unroll=7)


def three_part(t, grad_out, act_older, weight, taps, back, grad_older, wide, dense, ready):
    spread_taps(taps, wide, 9)
    dense_product(grad_out[...], weight, dense)
    to_pitched(dense, back)
    spread_conv(back, wide, dense, 3, True)
    ready()
    finish_older(act_older, t, dense, grad_older)


def five_part(t, grad_out, grad_pass, act_last, weight, taps, back, grad_last, wide, dense, ready):
    spread_taps(taps, wide, 25)
    dense_product(grad_out[...], weight, dense)
    to_pitched(dense, back)
    spread_conv(back, wide, dense, 5, True)
    ready()
    finish_last(act_last, t, dense, grad_out, grad_pass, grad_last)


def opening_kernel(token_ref):
    token_ref[0] = 0


def slots_unpacked(plan_ref, source, target):
    turns = target.shape[0]
    turn_of = [sum(jnp.where(plan_ref[0, t] == k, t, 0) for t in range(1, turns)) for k in range(turns)]

    def put(at, block):
        block = jnp.maximum(block, 0)
        for k in range(turns):
            target[turn_of[k], pl.ds(at, 16), :] = block[k]

    unpack(source, turns, put)


def pair_unpacked(source, grad_out, grad_pass):
    def put(at, block):
        grad_out[pl.ds(at, 16), :] = block[0]
        grad_pass[pl.ds(at, 16), :] = block[1]

    unpack(source, 2, put)


def first_five_kernel(
    token_ref,
    plan_ref,
    last_in,
    arriving_in,
    weight,
    taps,
    grad_last,
    act_last,
    grad_out,
    back,
    grad_pass,
    wide,
    dense,
):
    pair_unpacked(arriving_in, grad_out, grad_pass)

    def ready():
        slots_unpacked(plan_ref, last_in, act_last)

    five_part(0, grad_out, grad_pass, act_last, weight, taps, back, grad_last, wide, dense, ready)


def first_three_kernel(
    plan_ref, older_in, grad_out, weight, taps, grad_older, act_older, back, wide, dense
):
    def ready():
        slots_unpacked(plan_ref, older_in, act_older)

    three_part(0, grad_out, act_older, weight, taps, back, grad_older, wide, dense, ready)


def take(t, top_ref, out_in, head_hbm, grad_out, head_pass, head_in, sem):
    @pl.when(top_ref[0] == 1)
    def _():
        get = pltpu.make_async_copy(head_hbm.at[t - 1], head_in, sem)
        get.start()
        get.wait()
        pair_unpacked(head_in, grad_out, head_pass)

    @pl.when(top_ref[0] != 1)
    def _():
        grad_out[...] = out_in[...]


def five_kernel(
    t, top_ref, out_in, head_hbm, weight, taps, through, grad_out, head_pass, back, head_in, wide, dense, sem
):
    take(t, top_ref, out_in, head_hbm, grad_out, head_pass, head_in, sem)
    spread_taps(taps, wide, 25)
    dense_product(grad_out[...], weight, dense)
    to_pitched(dense, back)
    spread_conv(back, wide, through, 5, True)


def finish(t, top_ref, pass_in, head_pass, grad_out, act_last, through, grad_last):
    @pl.when(top_ref[0] == 1)
    def _():
        finish_last(act_last, t, through, grad_out, head_pass, grad_last)

    @pl.when(top_ref[0] != 1)
    def _():
        finish_last(act_last, t, through, grad_out, pass_in, grad_last)


def finish_kernel(t, top_ref, pass_in, head_pass, grad_out, act_last, through, grad_last):
    finish(t, top_ref, pass_in, head_pass, grad_out, act_last, through, grad_last)


def three_kernel(t, grad_out, act_older, weight, taps, grad_older, back, wide, dense):
    three_part(t, grad_out, act_older, weight, taps, back, grad_older, wide, dense, lambda: None)


def copies(pairs, sems):
    return [pltpu.make_async_copy(a, b, sems.at[n]) for n, (a, b) in enumerate(pairs)]


def widened(act, t, dense):
    def body(i, carry):
        rows = pl.ds(pl.multiple_of(i * 16, 16), 16)
        for c in range(BLOCKS):
            dense[c, rows, :] = act[t, rows, lanes(c)].astype(F32)
        return carry

    lax.fori_loop(0, ROWS // 16, body, 0, unroll=14)


def mix(act, t, taps, mixed, pitched, dense, wide, kernel):
    widened(act, t, dense)
    to_pitched(dense, pitched)
    spread_taps(taps, wide, kernel * kernel)
    for c in range(BLOCKS):
        dense[c, ROWS - 8 : ROWS, :] = jnp.zeros((8, 128), F32)
    spread_conv(pitched, wide, dense, kernel, False)

    def body(i, carry):
        rows = pl.ds(pl.multiple_of(i * 16, 16), 16)
        for c in range(BLOCKS):
            mixed[rows, lanes(c)] = dense[c, rows, :].astype(BF16)
        return carry

    lax.fori_loop(0, ROWS // 16, body, 0, unroll=14)


def across(mixed, left):
    return lax.dot_general(mixed, left, (((0,), (0,)), ((), ())), preferred_element_type=F32)


def grads_kernel(t, *refs):
    act_last, act_older, taps_five, taps_three, back_five, back_three = refs[:6]
    refs = refs[6:]
    olds = (None, None)
    if t > 0:
        olds, refs = refs[:2], refs[2:]
    sums, mixes = refs[:2], refs[2:4]
    pitched, dense, wide = refs[4:]
    for act, taps, back, kernel, old, total, mixed in (
        (act_last, taps_five, back_five, 5, olds[0], sums[0], mixes[0]),
        (act_older, taps_three, back_three, 3, olds[1], sums[1], mixes[1]),
    ):
        mix(act, t, taps, mixed, pitched, dense, wide, kernel)
        tap_sums(back, pitched, total, kernel)
        if old is not None:
            total[...] = total[...] + old[...]


def gather_kernel(t, *refs):
    act_last, act_older, taps_five, taps_three, back_five, back_three = refs[:6]
    old_taps, refs = refs[6:8], refs[8:]
    grads, refs = refs[: t + 1], refs[t + 1 :]
    mixed_before, refs = refs[: 2 * t], refs[2 * t :]
    points, sums, ahead, refs = refs[:2], refs[2:4], refs[4:8], refs[8:]
    pitched, dense, wide, mixed = refs
    for n, (act, taps, back, kernel) in enumerate(
        ((act_last, taps_five, back_five, 5), (act_older, taps_three, back_three, 3))
    ):
        mix(act, t + 1, taps, ahead[n], ahead[2 + n], dense, wide, kernel)
        mix(act, t, taps, mixed, pitched, dense, wide, kernel)
        points[n][...] = across(mixed[...], grads[t][...])
        for before in range(t):
            points[n][...] += across(mixed_before[2 * before + n][...], grads[before][...])
        tap_sums(back, pitched, sums[n], kernel)
        sums[n][...] = sums[n][...] + old_taps[n][...]


def last_grads_kernel(
    t,
    top_ref,
    row_ref,
    out_in,
    head_hbm,
    weight_five,
    weight_three,
    mixed_five,
    mixed_three,
    pitched_five,
    pitched_three,
    old_five,
    old_three,
    old_taps_five,
    old_taps_three,
    *refs,
):
    sends, refs = refs[:3], refs[3:]
    own, grad_out, head_pass, back_five, back_three = refs[:5]
    packed, head_in, dense, rows_ref, sem = refs[5:]
    scale = 1.0 / PIXELS
    take(t, top_ref, out_in, head_hbm, grad_out, head_pass, head_in, sem)
    left = grad_out[...]
    packed[:, 0:CH] = (across(mixed_five[...], left) + old_five[...]) * scale
    packed[:, CH : 2 * CH] = (across(mixed_three[...], left) + old_three[...]) * scale
    rows_ref[...] = jnp.zeros(rows_ref.shape, F32)
    for pitched, weight, back, old, at, kernel in (
        (pitched_five, weight_five, back_five, old_taps_five, 0, 5),
        (pitched_three, weight_three, back_three, old_taps_three, 32, 3),
    ):
        dense_product(left, weight, dense)
        to_pitched(dense, back)
        count = kernel * kernel
        tap_sums(back, pitched, rows_ref.at[pl.ds(at, old.shape[0])], kernel)
        rows_ref[at : at + count, :] = (rows_ref[at : at + count, :] + old[0:count, :]) * scale
    for c in range(BLOCKS):
        packed[lanes(c), 2 * CH : 2 * CH + 128] = rows_ref[:, lanes(c)].T
    height = own.shape[0]
    groups = CH // height

    def rows(distance):
        at = lax.rem(row_ref[0] + distance, groups) * height
        return pl.ds(pl.multiple_of(at, 16), height)

    own[...] = packed[rows(0), :]
    for distance, send in enumerate(sends, 1):
        send[...] = packed[rows(distance), :].astype(BF16)


def last_convs_kernel(
    t, back_five, back_three, act_older, taps_five, taps_three, through, grad_older, wide_five, wide_three, dense
):
    spread_taps(taps_five, wide_five, 25)
    spread_taps(taps_three, wide_three, 9)
    spread_conv(back_three, wide_three, dense, 3, True)
    finish_older(act_older, t, dense, grad_older)
    spread_conv(back_five, wide_five, through, 5, True)


def last_kernel(
    t, top_ref, pass_in, head_pass, grad_out, act_last, through, grad_older, outgoing_hbm, outgoing, grad_pass, sems
):
    @pl.when(top_ref[0] == 1)
    def _():
        grad_pass[...] = head_pass[...]

    @pl.when(top_ref[0] != 1)
    def _():
        grad_pass[...] = pass_in[...]

    def both(rows, c):
        last = last_piece(act_last, t, through, grad_out, grad_pass, c, rows)
        return jnp.swapaxes(jnp.stack([last, grad_older[rows, lanes(c)]], 0), 0, 1)

    def body(i, carry):
        rows = pl.ds(pl.multiple_of(i * 16, 16), 16)
        for c in range(BLOCKS):
            outgoing[rows, :, lanes(c)] = both(rows, c)
        return carry

    half = 224
    lax.fori_loop(0, half // 16, body, 0, unroll=7)
    put = copies(
        [
            (outgoing.at[pl.ds(0, half)], outgoing_hbm.at[pl.ds(0, half)]),
            (outgoing.at[pl.ds(half, PIXELS - half)], outgoing_hbm.at[pl.ds(half, PIXELS - half)]),
        ],
        sems,
    )
    put[0].start()
    lax.fori_loop(half // 16, PIXELS // 16, body, 0, unroll=13)
    at = PIXELS // 16 * 16
    for c in range(BLOCKS):
        outgoing[at:PIXELS, :, lanes(c)] = both(slice(at, at + 16), c)[: PIXELS - at]
    put[1].start()
    put[0].wait()
    put[1].wait()


def half_total_kernel(half_ref, own, one, two, three, kept, send):
    height = kept.shape[0]

    def summed(which):
        rows = pl.ds(pl.multiple_of(which * height, 16), height)
        total = own[rows, :]
        for landed in (one, two, three):
            total = total + landed[rows, :].astype(F32)
        return total

    kept[...] = summed(half_ref[0])
    send[...] = summed(1 - half_ref[0]).astype(BF16)


def total_kernel(kept, landed, five, three, taps_five, taps_three):
    five[...] = kept[:, 0:CH] + landed[:, 0:CH].astype(F32)
    three[...] = kept[:, CH : 2 * CH] + landed[:, CH : 2 * CH].astype(F32)
    rows = (kept[:, 2 * CH :] + landed[:, 2 * CH :].astype(F32)).T
    for taps, at in ((taps_five, 0), (taps_three, 32)):
        for k in range(taps.shape[0]):
            taps[k] = rows[at + k : at + k + 1, :]


VMEM = pl.BlockSpec(memory_space=pltpu.VMEM)
SMEM = pl.BlockSpec(memory_space=pltpu.SMEM)
ANY = pl.BlockSpec(memory_space=pl.ANY)
FLAT = jax.ShapeDtypeStruct((ROWS, CH), BF16)
WIDE = 2 * CH + 128
THROUGH = jax.ShapeDtypeStruct((BLOCKS, ROWS + 8, 128), F32)
ACTS = jax.ShapeDtypeStruct((4, ROWS, CH), BF16)
BACK = jax.ShapeDtypeStruct((BLOCKS, PITCHED, 128), F32)
POINTS = jax.ShapeDtypeStruct((CH, CH), F32)
SUMS = (jax.ShapeDtypeStruct((32, CH), F32), jax.ShapeDtypeStruct((16, CH), F32))
FLAT_SCRATCH = pltpu.VMEM((ROWS, CH), BF16)
PAIR_SCRATCH = pltpu.VMEM((PIXELS, 2, CH), BF16)
WIDE_FIVE = pltpu.VMEM((25, BLOCKS, 8, 128), F32)
WIDE_THREE = pltpu.VMEM((9, BLOCKS, 8, 128), F32)
DENSE = pltpu.VMEM((BLOCKS, ROWS + 8, 128), F32)
PITCHED_SCRATCH = pltpu.VMEM((BLOCKS, PITCHED, 128), F32)


def run(kernel, name, operands, specs, shapes, out_specs, scratch, micros, limit=12 << 20):
    cost = pl.CostEstimate(flops=int(micros * 1e9), bytes_accessed=0, transcendentals=0)
    return pl.pallas_call(
        kernel,
        out_shape=tuple(shapes),
        in_specs=specs,
        out_specs=tuple(out_specs),
        scratch_shapes=scratch,
        compiler_params=pltpu.CompilerParams(vmem_limit_bytes=limit),
        cost_estimate=cost,
        name=name,
    )(*operands)


def call_opening():
    (token,) = run(
        opening_kernel,
        "opening",
        (),
        [],
        (jax.ShapeDtypeStruct((1,), jnp.int32),),
        (SMEM,),
        [],
        6,
    )
    return token


def call_first_five(token, plan, last, arriving, weight, taps):
    return run(
        first_five_kernel,
        "first_five",
        (token, plan, last, arriving, weight, taps),
        [SMEM, SMEM] + [VMEM] * 4,
        (FLAT, ACTS, FLAT, BACK),
        (VMEM,) * 4,
        [FLAT_SCRATCH, WIDE_FIVE, DENSE],
        4,
    )


def call_first_three(plan, older, grad_out, weight, taps):
    return run(
        first_three_kernel,
        "first_three",
        (plan, older, grad_out, weight, taps),
        [SMEM] + [VMEM] * 4,
        (FLAT, ACTS, BACK),
        (VMEM,) * 3,
        [WIDE_THREE, DENSE],
        3,
    )


def call_five(t, given, weight, taps):
    return run(
        functools.partial(five_kernel, t),
        f"five_{t}",
        (*given, weight, taps),
        [SMEM, VMEM, ANY] + [VMEM] * 2,
        (THROUGH, FLAT, FLAT, BACK),
        (VMEM,) * 4,
        [PAIR_SCRATCH, WIDE_FIVE, DENSE, pltpu.SemaphoreType.DMA],
        3,
    )


def call_finish(t, *operands):
    (grad_last,) = run(
        functools.partial(finish_kernel, t),
        f"finish_{t}",
        operands,
        [SMEM] + [VMEM] * 5,
        (FLAT,),
        (VMEM,),
        [],
        1,
    )
    return grad_last


def call_three(t, grad_out, act, weight, taps):
    return run(
        functools.partial(three_kernel, t),
        f"three_{t}",
        (grad_out, act, weight, taps),
        [VMEM] * 4,
        (FLAT, BACK),
        (VMEM,) * 2,
        [WIDE_THREE, DENSE],
        2,
    )


def call_grads(t, acts, taps, backs, olds):
    operands = (*acts, *taps, *backs, *olds)
    return run(
        functools.partial(grads_kernel, t),
        f"grads_{t}",
        operands,
        [VMEM] * len(operands),
        (*SUMS, FLAT, FLAT),
        (VMEM,) * 4,
        [PITCHED_SCRATCH, DENSE, WIDE_FIVE],
        5,
    )


def call_gather(t, acts, taps, backs, olds, grads, mixes):
    operands = (*acts, *taps, *backs, *olds, *grads, *mixes)
    return run(
        functools.partial(gather_kernel, t),
        f"gather_{t}",
        operands,
        [VMEM] * len(operands),
        (POINTS, POINTS, *SUMS, FLAT, FLAT, BACK, BACK),
        (VMEM,) * 8,
        [PITCHED_SCRATCH, DENSE, WIDE_FIVE, FLAT_SCRATCH],
        10,
    )


def call_last_grads(t, height, given, weights, mixed, olds):
    send = jax.ShapeDtypeStruct((height, WIDE), BF16)
    own = jax.ShapeDtypeStruct((height, WIDE), F32)
    return run(
        functools.partial(last_grads_kernel, t),
        "last_grads",
        (*given, *weights, *mixed, *olds),
        [SMEM, SMEM, VMEM, ANY] + [VMEM] * 10,
        (send, send, send, own, FLAT, FLAT, BACK, BACK),
        (VMEM,) * 8,
        [
            pltpu.VMEM((CH, WIDE), F32),
            PAIR_SCRATCH,
            DENSE,
            pltpu.VMEM((128, CH), F32),
            pltpu.SemaphoreType.DMA,
        ],
        6,
    )


def call_last_convs(t, *operands):
    return run(
        functools.partial(last_convs_kernel, t),
        "last_convs",
        operands,
        [VMEM] * 5,
        (THROUGH, FLAT),
        (VMEM,) * 2,
        [WIDE_FIVE, WIDE_THREE, DENSE],
        3,
    )


def call_last(t, *operands):
    (outgoing,) = run(
        functools.partial(last_kernel, t),
        "last",
        operands,
        [SMEM] + [VMEM] * 6,
        (jax.ShapeDtypeStruct((PIXELS, 2, CH), BF16),),
        (ANY,),
        [PAIR_SCRATCH, FLAT_SCRATCH, pltpu.SemaphoreType.DMA((2,))],
        2,
    )
    return outgoing


def call_half_total(half, own, landed):
    height = own.shape[0] // 2
    return run(
        half_total_kernel,
        "half_total",
        (half, own, *landed),
        [SMEM] + [VMEM] * 4,
        (jax.ShapeDtypeStruct((height, WIDE), F32), jax.ShapeDtypeStruct((height, WIDE), BF16)),
        (VMEM,) * 2,
        [],
        1,
    )


def whole(shape):
    zeros = (0,) * len(shape)
    return pl.BlockSpec(shape, lambda i: zeros)


def call_total(kept, landed):
    rows = kept.shape[0]
    shapes = [(rows, CH), (rows, CH), (25, 1, rows), (9, 1, rows)]
    return pl.pallas_call(
        total_kernel,
        grid=(1,),
        out_shape=tuple(jax.ShapeDtypeStruct(shape, F32) for shape in shapes),
        in_specs=[whole(kept.shape), whole(landed.shape)],
        out_specs=tuple(whole(shape) for shape in shapes),
        compiler_params=pltpu.CompilerParams(vmem_limit_bytes=12 << 20),
        name="total",
    )(kept, landed)


def by_pixel(stack):
    return jnp.transpose(stack, (0, 2, 3, 4, 1, 5)).reshape(PIXELS, stack.shape[1], CH)


def local(
    saved_last,
    saved_older,
    arriving,
    head_adjoint,
    plan,
    depth_five,
    depth_three,
    point_five,
    point_three,
):
    turns = saved_last.shape[1]
    top = (lax.axis_index("sec") == lax.axis_size("sec") - 1).astype(jnp.int32)[None]
    image = lax.axis_index("img").astype(jnp.int32)
    group, half = (image // 2)[None], (image % 2)[None]
    token, top, group, half = lax.optimization_barrier((call_opening(), top, group, half))
    head = jnp.transpose(head_adjoint, (0, 2, 3, 4, 1, 5)).reshape(turns - 1, PIXELS, 2, CH)
    weights = (point_five[0], point_three[0])
    taps = (depth_five[0], depth_three[0])
    grad_last, act_last, grad_out, back_five = call_first_five(
        token, plan, by_pixel(saved_last), by_pixel(arriving), weights[0], taps[0]
    )
    next_out = from_next(grad_last)
    grad_older, act_older, back_three = call_first_three(
        plan, by_pixel(saved_older), grad_out, weights[1], taps[1]
    )
    next_pass = from_next(grad_older)
    acts = (act_last, act_older)
    sums, mixes, grads = (), (), (grad_out,)
    for t in range(turns - 2):
        made = call_grads(t, acts, taps, (back_five, back_three), sums)
        next_out, made = lax.optimization_barrier((next_out, made))
        sums, mixes = made[:2], (*mixes, *made[2:])
        through, grad_out, head_pass, back_five = call_five(
            t + 1, (top, next_out, head), weights[0], taps[0]
        )
        grads = (*grads, grad_out)
        grad_last = call_finish(t + 1, top, next_pass, head_pass, grad_out, act_last, through)
        next_out = from_next(grad_last)
        ready, _ = lax.optimization_barrier((grad_out, grad_last))
        grad_older, back_three = call_three(t + 1, ready, act_older, weights[1], taps[1])
        if t < turns - 3:
            next_pass = from_next(grad_older)
    made = call_gather(turns - 2, acts, taps, (back_five, back_three), sums, grads, mixes)
    next_out, made = lax.optimization_barrier((next_out, made))
    *sends, own, grad_out, head_pass, back_five, back_three = call_last_grads(
        turns - 1,
        CH * 2 // lax.axis_size("img"),
        (top, group, next_out, head),
        weights,
        made[4:],
        made[:4],
    )
    *sends, grad_older = lax.optimization_barrier((*sends, grad_older))
    landed = [around_rows(sends[distance - 1], distance) for distance in (2, 1, 3)]
    next_pass = from_next(grad_older)
    through, made_older = call_last_convs(
        turns - 1, back_five, back_three, act_older, taps[0], taps[1]
    )
    *landed, through = lax.optimization_barrier((*landed, through))
    kept, send = call_half_total(half, own, landed)
    through, kept, send = lax.optimization_barrier((through, kept, send))
    partner = with_partner(send)
    outgoing = call_last(
        turns - 1, top, next_pass, head_pass, grad_out, act_last, through, made_older
    )
    partner, outgoing = lax.optimization_barrier((partner, outgoing))
    five, three, tap_five, tap_three = call_total(kept, partner)
    outgoing = outgoing.reshape(1, 1, SIDE, SIDE, 2, CH).transpose(0, 4, 1, 2, 3, 5)
    return (
        outgoing,
        five[None],
        jnp.transpose(tap_five, (1, 2, 0)),
        three[None],
        jnp.transpose(tap_three, (1, 2, 0)),
    )


def solution(mesh):
    placed = (
        P("sec", None, "img", None, None, None),
        P("sec", None, "img", None, None, None),
        P("sec", None, "img", None, None, None),
        P(None, None, "img", None, None, None),
        P("sec", None),
        P("sec", None, None),
        P("sec", None, None),
        P("sec", None, None),
        P("sec", None, None),
    )
    return jax.shard_map(
        local,
        mesh=mesh,
        in_specs=placed,
        out_specs=(
            P("sec", None, "img", None, None, None),
            P("sec", "img", None),
            P("sec", "img", None),
            P("sec", "img", None),
            P("sec", "img", None),
        ),
        check_vma=False,
    )
```

```python
import functools

import jax
import jax.numpy as jnp
from jax import lax
from jax.experimental import pallas as pl
from jax.experimental.pallas import tpu as pltpu
from jax.sharding import PartitionSpec as P

SIDE = 21
PIXELS = SIDE * SIDE
ROWS = 448
CH = 384
BLOCKS = CH // 128
PITCH = 24
EDGE = 8
PITCHED = EDGE + (SIDE + 4) * PITCH + 8
F32 = jnp.float32
BF16 = jnp.bfloat16


def from_next(block):
    size = lax.axis_size("sec")
    return lax.ppermute(block, "sec", [(i + 1, i) for i in range(size - 1)])


def around_rows(block, distance):
    rows = lax.axis_size("img") // 2
    route = [(2 * i + j, (i + distance) % rows * 2 + j) for i in range(rows) for j in range(2)]
    return lax.ppermute(block, "img", route)


def with_partner(block):
    return lax.ppermute(block, "img", [(i, i ^ 1) for i in range(lax.axis_size("img"))])


def lanes(c):
    return slice(c * 128, (c + 1) * 128)


def spread_taps(taps_ref, wide, count):
    for k in range(count):
        row = taps_ref[k : k + 1, :].astype(F32)
        for c in range(BLOCKS):
            wide[k, c] = jnp.broadcast_to(row[:, lanes(c)], (8, 128))


def clear_edges(pitched):
    top = EDGE + 2 * PITCH
    bottom = EDGE + (SIDE + 2) * PITCH
    for c in range(BLOCKS):
        pitched[c, 0:top, :] = jnp.zeros((top, 128), F32)
        pitched[c, bottom:PITCHED, :] = jnp.zeros((PITCHED - bottom, 128), F32)


def to_pitched(dense, pitched):
    inside = lax.broadcasted_iota(jnp.int32, (PITCH, 128), 0) < SIDE
    clear_edges(pitched)

    def row(i, carry):
        for c in range(BLOCKS):
            got = dense[c, pl.ds(i * SIDE, PITCH), :]
            at = pl.multiple_of(EDGE + (i + 2) * PITCH, 8)
            pitched[c, pl.ds(at, PITCH), :] = jnp.where(inside, got, 0.0)
        return carry

    lax.fori_loop(0, SIDE, row, 0, unroll=21)


def add_window(sums, got, weight_of, b, shift, rows, kernel):
    radius = kernel // 2
    for a in range(rows):
        p = b - a
        if p < 0 or p >= kernel:
            continue
        for r in range(3):
            q = shift - r + radius
            if q < 0 or q >= kernel:
                continue
            term = weight_of(p * kernel + q) * got
            old = sums[a][r]
            sums[a][r] = term if old is None else old + term


def spread_conv(pitched, wide, dense, kernel, flipped):
    radius = kernel // 2
    last = kernel * kernel - 1
    rows = 3 if kernel == 5 else 7

    def group(g, carry):
        for c in range(BLOCKS):
            sums = [[None] * 3 for _ in range(rows)]
            start = EDGE + (rows * g + 2 - radius) * PITCH
            for b in range(kernel + rows - 1):
                for shift in range(-radius, 3 + radius):
                    got = pitched[c, pl.ds(start + b * PITCH + shift, 8, stride=3), :]
                    add_window(
                        sums,
                        got,
                        lambda k: wide[last - k if flipped else k, c],
                        b,
                        shift,
                        rows,
                        kernel,
                    )
            for a in range(rows):
                for r in range(3):
                    dense[c, pl.ds((rows * g + a) * SIDE + r, 8, stride=3), :] = sums[a][r]
        return carry

    lax.fori_loop(0, SIDE // rows, group, 0)


def tap_sums(back, active, sums_ref, kernel):
    radius = kernel // 2
    count = kernel * kernel
    rows = 7
    for c in range(BLOCKS):

        def group(g, sums):
            sums = list(sums)
            here = EDGE + (rows * g + 2) * PITCH
            centre = [
                [back[c, pl.ds(here + a * PITCH + r, 8, stride=3), :] for r in range(3)]
                for a in range(rows)
            ]
            for b in range(kernel + rows - 1):
                for shift in range(-radius, 3 + radius):
                    at = here + (b - radius) * PITCH + shift
                    got = active[c, pl.ds(at, 8, stride=3), :]
                    for a in range(rows):
                        p = b - a
                        if p < 0 or p >= kernel:
                            continue
                        for r in range(3):
                            q = shift - r + radius
                            if 0 <= q < kernel:
                                k = p * kernel + q
                                sums[k] = sums[k] + got * centre[a][r]
            return tuple(sums)

        empty = tuple(jnp.zeros((8, 128), F32) for _ in range(count))
        sums = lax.fori_loop(0, SIDE // rows, group, empty)
        for k in range(count):
            sums_ref[k : k + 1, lanes(c)] = jnp.sum(sums[k], axis=0, keepdims=True)


def pieces(ref, width):
    whole = PIXELS // 16

    def read(i):
        return ref[pl.ds(i * 16, 16)]

    tail = jnp.concatenate(
        [ref[whole * 16 : PIXELS], jnp.zeros((16 - PIXELS % 16, width, CH), BF16)], 0
    )
    return whole, read, tail


def unpack(ref, width, put):
    whole, read, tail = pieces(ref, width)

    def body(i, carry):
        put(pl.multiple_of(i * 16, 16), jnp.swapaxes(read(i), 0, 1))
        return carry

    lax.fori_loop(0, whole, body, 0, unroll=9)
    put(whole * 16, jnp.swapaxes(tail, 0, 1))


def dense_product(left, weight_ref, dense):
    for first, blocks in ((0, 2), (2, 1)):
        got = lax.dot_general(
            left,
            weight_ref[first * 128 : (first + blocks) * 128, :],
            (((1,), (1,)), ((), ())),
            preferred_element_type=F32,
        )
        for c in range(blocks):
            dense[first + c, 0:ROWS, :] = got[:, lanes(c)]


def masked(act, t, dense, c, rows):
    return jnp.where(act[t, rows, lanes(c)].astype(F32) > 0, dense[c, rows, :], 0.0)


def finish_older(act_older, t, dense, grad_older):
    def body(i, carry):
        rows = pl.ds(pl.multiple_of(i * 16, 16), 16)
        for c in range(BLOCKS):
            grad_older[rows, lanes(c)] = masked(act_older, t, dense, c, rows).astype(BF16)
        return carry

    lax.fori_loop(0, ROWS // 16, body, 0, unroll=7)


def last_piece(act_last, t, dense, grad_out, grad_pass, c, rows):
    skip = grad_pass[rows, lanes(c)].astype(F32) + grad_out[rows, lanes(c)].astype(F32)
    return (skip + masked(act_last, t, dense, c, rows)).astype(BF16)


def finish_last(act_last, t, dense, grad_out, grad_pass, grad_last):
    def body(i, carry):
        rows = pl.ds(pl.multiple_of(i * 16, 16), 16)
        for c in range(BLOCKS):
            grad_last[rows, lanes(c)] = last_piece(act_last, t, dense, grad_out, grad_pass, c, rows)
        return carry

    lax.fori_loop(0, ROWS // 16, body, 0, unroll=7)


def three_part(t, grad_out, act_older, weight, taps, back, grad_older, wide, dense, ready):
    spread_taps(taps, wide, 9)
    dense_product(grad_out[...], weight, dense)
    to_pitched(dense, back)
    spread_conv(back, wide, dense, 3, True)
    ready()
    finish_older(act_older, t, dense, grad_older)


def five_part(t, grad_out, grad_pass, act_last, weight, taps, back, grad_last, wide, dense, ready):
    spread_taps(taps, wide, 25)
    dense_product(grad_out[...], weight, dense)
    to_pitched(dense, back)
    spread_conv(back, wide, dense, 5, True)
    ready()
    finish_last(act_last, t, dense, grad_out, grad_pass, grad_last)


def opening_kernel(token_ref):
    token_ref[0] = 0


def slots_unpacked(plan_ref, source, target):
    turns = target.shape[0]
    turn_of = [sum(jnp.where(plan_ref[0, t] == k, t, 0) for t in range(1, turns)) for k in range(turns)]

    def put(at, block):
        block = jnp.maximum(block, 0)
        for k in range(turns):
            target[turn_of[k], pl.ds(at, 16), :] = block[k]

    unpack(source, turns, put)


def pair_unpacked(source, grad_out, grad_pass):
    def put(at, block):
        grad_out[pl.ds(at, 16), :] = block[0]
        grad_pass[pl.ds(at, 16), :] = block[1]

    unpack(source, 2, put)


def first_five_kernel(
    token_ref,
    plan_ref,
    last_in,
    arriving_in,
    weight,
    taps,
    grad_last,
    act_last,
    grad_out,
    back,
    grad_pass,
    wide,
    dense,
):
    pair_unpacked(arriving_in, grad_out, grad_pass)

    def ready():
        slots_unpacked(plan_ref, last_in, act_last)

    five_part(0, grad_out, grad_pass, act_last, weight, taps, back, grad_last, wide, dense, ready)


def first_three_kernel(
    plan_ref, older_in, grad_out, weight, taps, grad_older, act_older, back, wide, dense
):
    def ready():
        slots_unpacked(plan_ref, older_in, act_older)

    three_part(0, grad_out, act_older, weight, taps, back, grad_older, wide, dense, ready)


def take(t, top_ref, out_in, head_hbm, grad_out, head_pass, head_in, sem):
    @pl.when(top_ref[0] == 1)
    def _():
        get = pltpu.make_async_copy(head_hbm.at[t - 1], head_in, sem)
        get.start()
        get.wait()
        pair_unpacked(head_in, grad_out, head_pass)

    @pl.when(top_ref[0] != 1)
    def _():
        grad_out[...] = out_in[...]


def five_kernel(
    t, top_ref, out_in, head_hbm, weight, taps, through, grad_out, head_pass, back, head_in, wide, dense, sem
):
    take(t, top_ref, out_in, head_hbm, grad_out, head_pass, head_in, sem)
    spread_taps(taps, wide, 25)
    dense_product(grad_out[...], weight, dense)
    to_pitched(dense, back)
    spread_conv(back, wide, through, 5, True)


def finish(t, top_ref, pass_in, head_pass, grad_out, act_last, through, grad_last):
    @pl.when(top_ref[0] == 1)
    def _():
        finish_last(act_last, t, through, grad_out, head_pass, grad_last)

    @pl.when(top_ref[0] != 1)
    def _():
        finish_last(act_last, t, through, grad_out, pass_in, grad_last)


def finish_kernel(t, top_ref, pass_in, head_pass, grad_out, act_last, through, grad_last):
    finish(t, top_ref, pass_in, head_pass, grad_out, act_last, through, grad_last)


def three_kernel(t, grad_out, act_older, weight, taps, grad_older, back, wide, dense):
    three_part(t, grad_out, act_older, weight, taps, back, grad_older, wide, dense, lambda: None)


def copies(pairs, sems):
    return [pltpu.make_async_copy(a, b, sems.at[n]) for n, (a, b) in enumerate(pairs)]


def widened(act, t, dense):
    def body(i, carry):
        rows = pl.ds(pl.multiple_of(i * 16, 16), 16)
        for c in range(BLOCKS):
            dense[c, rows, :] = act[t, rows, lanes(c)].astype(F32)
        return carry

    lax.fori_loop(0, ROWS // 16, body, 0, unroll=14)


def mix(act, t, taps, mixed, pitched, dense, wide, kernel):
    widened(act, t, dense)
    to_pitched(dense, pitched)
    spread_taps(taps, wide, kernel * kernel)
    for c in range(BLOCKS):
        dense[c, ROWS - 8 : ROWS, :] = jnp.zeros((8, 128), F32)
    spread_conv(pitched, wide, dense, kernel, False)

    def body(i, carry):
        rows = pl.ds(pl.multiple_of(i * 16, 16), 16)
        for c in range(BLOCKS):
            mixed[rows, lanes(c)] = dense[c, rows, :].astype(BF16)
        return carry

    lax.fori_loop(0, ROWS // 16, body, 0, unroll=14)


def across(mixed, left):
    return lax.dot_general(mixed, left, (((0,), (0,)), ((), ())), preferred_element_type=F32)


def grads_kernel(t, *refs):
    act_last, act_older, taps_five, taps_three, back_five, back_three = refs[:6]
    refs = refs[6:]
    olds = (None, None)
    if t > 0:
        olds, refs = refs[:2], refs[2:]
    sums, mixes = refs[:2], refs[2:4]
    pitched, dense, wide = refs[4:]
    for act, taps, back, kernel, old, total, mixed in (
        (act_last, taps_five, back_five, 5, olds[0], sums[0], mixes[0]),
        (act_older, taps_three, back_three, 3, olds[1], sums[1], mixes[1]),
    ):
        mix(act, t, taps, mixed, pitched, dense, wide, kernel)
        tap_sums(back, pitched, total, kernel)
        if old is not None:
            total[...] = total[...] + old[...]


def gather_kernel(t, *refs):
    act_last, act_older, taps_five, taps_three, back_five, back_three = refs[:6]
    old_taps, refs = refs[6:8], refs[8:]
    grads, refs = refs[: t + 1], refs[t + 1 :]
    mixed_before, refs = refs[: 2 * t], refs[2 * t :]
    points, sums, ahead, refs = refs[:2], refs[2:4], refs[4:8], refs[8:]
    pitched, dense, wide, mixed = refs
    for n, (act, taps, back, kernel) in enumerate(
        ((act_last, taps_five, back_five, 5), (act_older, taps_three, back_three, 3))
    ):
        mix(act, t + 1, taps, ahead[n], ahead[2 + n], dense, wide, kernel)
        mix(act, t, taps, mixed, pitched, dense, wide, kernel)
        points[n][...] = across(mixed[...], grads[t][...])
        for before in range(t):
            points[n][...] += across(mixed_before[2 * before + n][...], grads[before][...])
        tap_sums(back, pitched, sums[n], kernel)
        sums[n][...] = sums[n][...] + old_taps[n][...]


def last_grads_kernel(
    t,
    top_ref,
    row_ref,
    out_in,
    head_hbm,
    weight_five,
    weight_three,
    mixed_five,
    mixed_three,
    pitched_five,
    pitched_three,
    old_five,
    old_three,
    old_taps_five,
    old_taps_three,
    *refs,
):
    sends, refs = refs[:3], refs[3:]
    own, grad_out, head_pass, back_five, back_three = refs[:5]
    packed, head_in, dense, rows_ref, sem = refs[5:]
    scale = 1.0 / PIXELS
    take(t, top_ref, out_in, head_hbm, grad_out, head_pass, head_in, sem)
    left = grad_out[...]
    packed[:, 0:CH] = (across(mixed_five[...], left) + old_five[...]) * scale
    packed[:, CH : 2 * CH] = (across(mixed_three[...], left) + old_three[...]) * scale
    rows_ref[...] = jnp.zeros(rows_ref.shape, F32)
    for pitched, weight, back, old, at, kernel in (
        (pitched_five, weight_five, back_five, old_taps_five, 0, 5),
        (pitched_three, weight_three, back_three, old_taps_three, 32, 3),
    ):
        dense_product(left, weight, dense)
        to_pitched(dense, back)
        count = kernel * kernel
        tap_sums(back, pitched, rows_ref.at[pl.ds(at, old.shape[0])], kernel)
        rows_ref[at : at + count, :] = (rows_ref[at : at + count, :] + old[0:count, :]) * scale
    for c in range(BLOCKS):
        packed[lanes(c), 2 * CH : 2 * CH + 128] = rows_ref[:, lanes(c)].T
    height = own.shape[0]
    groups = CH // height

    def rows(distance):
        at = lax.rem(row_ref[0] + distance, groups) * height
        return pl.ds(pl.multiple_of(at, 16), height)

    own[...] = packed[rows(0), :]
    for distance, send in enumerate(sends, 1):
        send[...] = packed[rows(distance), :].astype(BF16)


def last_convs_kernel(
    t, back_five, back_three, act_older, taps_five, taps_three, through, grad_older, wide_five, wide_three, dense
):
    spread_taps(taps_five, wide_five, 25)
    spread_taps(taps_three, wide_three, 9)
    spread_conv(back_three, wide_three, dense, 3, True)
    finish_older(act_older, t, dense, grad_older)
    spread_conv(back_five, wide_five, through, 5, True)


def last_kernel(
    t, top_ref, pass_in, head_pass, grad_out, act_last, through, grad_older, outgoing_hbm, outgoing, grad_pass, sems
):
    @pl.when(top_ref[0] == 1)
    def _():
        grad_pass[...] = head_pass[...]

    @pl.when(top_ref[0] != 1)
    def _():
        grad_pass[...] = pass_in[...]

    def both(rows, c):
        last = last_piece(act_last, t, through, grad_out, grad_pass, c, rows)
        return jnp.swapaxes(jnp.stack([last, grad_older[rows, lanes(c)]], 0), 0, 1)

    def body(i, carry):
        rows = pl.ds(pl.multiple_of(i * 16, 16), 16)
        for c in range(BLOCKS):
            outgoing[rows, :, lanes(c)] = both(rows, c)
        return carry

    half = 224
    lax.fori_loop(0, half // 16, body, 0, unroll=7)
    put = copies(
        [
            (outgoing.at[pl.ds(0, half)], outgoing_hbm.at[pl.ds(0, half)]),
            (outgoing.at[pl.ds(half, PIXELS - half)], outgoing_hbm.at[pl.ds(half, PIXELS - half)]),
        ],
        sems,
    )
    put[0].start()
    lax.fori_loop(half // 16, PIXELS // 16, body, 0, unroll=13)
    at = PIXELS // 16 * 16
    for c in range(BLOCKS):
        outgoing[at:PIXELS, :, lanes(c)] = both(slice(at, at + 16), c)[: PIXELS - at]
    put[1].start()
    put[0].wait()
    put[1].wait()


def half_total_kernel(half_ref, own, one, two, three, kept, send):
    height = kept.shape[0]

    def summed(which):
        rows = pl.ds(pl.multiple_of(which * height, 16), height)
        total = own[rows, :]
        for landed in (one, two, three):
            total = total + landed[rows, :].astype(F32)
        return total

    kept[...] = summed(half_ref[0])
    send[...] = summed(1 - half_ref[0]).astype(BF16)


def total_kernel(kept, landed, five, three, taps_five, taps_three):
    five[...] = kept[:, 0:CH] + landed[:, 0:CH].astype(F32)
    three[...] = kept[:, CH : 2 * CH] + landed[:, CH : 2 * CH].astype(F32)
    rows = (kept[:, 2 * CH :] + landed[:, 2 * CH :].astype(F32)).T
    for taps, at in ((taps_five, 0), (taps_three, 32)):
        for k in range(taps.shape[0]):
            taps[k] = rows[at + k : at + k + 1, :]


VMEM = pl.BlockSpec(memory_space=pltpu.VMEM)
SMEM = pl.BlockSpec(memory_space=pltpu.SMEM)
ANY = pl.BlockSpec(memory_space=pl.ANY)
FLAT = jax.ShapeDtypeStruct((ROWS, CH), BF16)
WIDE = 2 * CH + 128
THROUGH = jax.ShapeDtypeStruct((BLOCKS, ROWS + 8, 128), F32)
ACTS = jax.ShapeDtypeStruct((4, ROWS, CH), BF16)
BACK = jax.ShapeDtypeStruct((BLOCKS, PITCHED, 128), F32)
POINTS = jax.ShapeDtypeStruct((CH, CH), F32)
SUMS = (jax.ShapeDtypeStruct((32, CH), F32), jax.ShapeDtypeStruct((16, CH), F32))
FLAT_SCRATCH = pltpu.VMEM((ROWS, CH), BF16)
PAIR_SCRATCH = pltpu.VMEM((PIXELS, 2, CH), BF16)
WIDE_FIVE = pltpu.VMEM((25, BLOCKS, 8, 128), F32)
WIDE_THREE = pltpu.VMEM((9, BLOCKS, 8, 128), F32)
DENSE = pltpu.VMEM((BLOCKS, ROWS + 8, 128), F32)
PITCHED_SCRATCH = pltpu.VMEM((BLOCKS, PITCHED, 128), F32)


def run(kernel, name, operands, specs, shapes, out_specs, scratch, micros, limit=12 << 20):
    cost = pl.CostEstimate(flops=int(micros * 1e9), bytes_accessed=0, transcendentals=0)
    return pl.pallas_call(
        kernel,
        out_shape=tuple(shapes),
        in_specs=specs,
        out_specs=tuple(out_specs),
        scratch_shapes=scratch,
        compiler_params=pltpu.CompilerParams(vmem_limit_bytes=limit),
        cost_estimate=cost,
        name=name,
    )(*operands)


def call_opening():
    (token,) = run(
        opening_kernel,
        "opening",
        (),
        [],
        (jax.ShapeDtypeStruct((1,), jnp.int32),),
        (SMEM,),
        [],
        6,
    )
    return token


def call_first_five(token, plan, last, arriving, weight, taps):
    return run(
        first_five_kernel,
        "first_five",
        (token, plan, last, arriving, weight, taps),
        [SMEM, SMEM] + [VMEM] * 4,
        (FLAT, ACTS, FLAT, BACK),
        (VMEM,) * 4,
        [FLAT_SCRATCH, WIDE_FIVE, DENSE],
        4,
    )


def call_first_three(plan, older, grad_out, weight, taps):
    return run(
        first_three_kernel,
        "first_three",
        (plan, older, grad_out, weight, taps),
        [SMEM] + [VMEM] * 4,
        (FLAT, ACTS, BACK),
        (VMEM,) * 3,
        [WIDE_THREE, DENSE],
        3,
    )


def call_five(t, given, weight, taps):
    return run(
        functools.partial(five_kernel, t),
        f"five_{t}",
        (*given, weight, taps),
        [SMEM, VMEM, ANY] + [VMEM] * 2,
        (THROUGH, FLAT, FLAT, BACK),
        (VMEM,) * 4,
        [PAIR_SCRATCH, WIDE_FIVE, DENSE, pltpu.SemaphoreType.DMA],
        3,
    )


def call_finish(t, *operands):
    (grad_last,) = run(
        functools.partial(finish_kernel, t),
        f"finish_{t}",
        operands,
        [SMEM] + [VMEM] * 5,
        (FLAT,),
        (VMEM,),
        [],
        1,
    )
    return grad_last


def call_three(t, grad_out, act, weight, taps):
    return run(
        functools.partial(three_kernel, t),
        f"three_{t}",
        (grad_out, act, weight, taps),
        [VMEM] * 4,
        (FLAT, BACK),
        (VMEM,) * 2,
        [WIDE_THREE, DENSE],
        2,
    )


def call_grads(t, acts, taps, backs, olds):
    operands = (*acts, *taps, *backs, *olds)
    return run(
        functools.partial(grads_kernel, t),
        f"grads_{t}",
        operands,
        [VMEM] * len(operands),
        (*SUMS, FLAT, FLAT),
        (VMEM,) * 4,
        [PITCHED_SCRATCH, DENSE, WIDE_FIVE],
        5,
    )


def call_gather(t, acts, taps, backs, olds, grads, mixes):
    operands = (*acts, *taps, *backs, *olds, *grads, *mixes)
    return run(
        functools.partial(gather_kernel, t),
        f"gather_{t}",
        operands,
        [VMEM] * len(operands),
        (POINTS, POINTS, *SUMS, FLAT, FLAT, BACK, BACK),
        (VMEM,) * 8,
        [PITCHED_SCRATCH, DENSE, WIDE_FIVE, FLAT_SCRATCH],
        10,
    )


def call_last_grads(t, height, given, weights, mixed, olds):
    send = jax.ShapeDtypeStruct((height, WIDE), BF16)
    own = jax.ShapeDtypeStruct((height, WIDE), F32)
    return run(
        functools.partial(last_grads_kernel, t),
        "last_grads",
        (*given, *weights, *mixed, *olds),
        [SMEM, SMEM, VMEM, ANY] + [VMEM] * 10,
        (send, send, send, own, FLAT, FLAT, BACK, BACK),
        (VMEM,) * 8,
        [
            pltpu.VMEM((CH, WIDE), F32),
            PAIR_SCRATCH,
            DENSE,
            pltpu.VMEM((128, CH), F32),
            pltpu.SemaphoreType.DMA,
        ],
        6,
    )


def call_last_convs(t, *operands):
    return run(
        functools.partial(last_convs_kernel, t),
        "last_convs",
        operands,
        [VMEM] * 5,
        (THROUGH, FLAT),
        (VMEM,) * 2,
        [WIDE_FIVE, WIDE_THREE, DENSE],
        3,
    )


def call_last(t, *operands):
    (outgoing,) = run(
        functools.partial(last_kernel, t),
        "last",
        operands,
        [SMEM] + [VMEM] * 6,
        (jax.ShapeDtypeStruct((PIXELS, 2, CH), BF16),),
        (ANY,),
        [PAIR_SCRATCH, FLAT_SCRATCH, pltpu.SemaphoreType.DMA((2,))],
        2,
    )
    return outgoing


def call_half_total(half, own, landed):
    height = own.shape[0] // 2
    return run(
        half_total_kernel,
        "half_total",
        (half, own, *landed),
        [SMEM] + [VMEM] * 4,
        (jax.ShapeDtypeStruct((height, WIDE), F32), jax.ShapeDtypeStruct((height, WIDE), BF16)),
        (VMEM,) * 2,
        [],
        1,
    )


def whole(shape):
    zeros = (0,) * len(shape)
    return pl.BlockSpec(shape, lambda i: zeros)


def call_total(kept, landed):
    rows = kept.shape[0]
    shapes = [(rows, CH), (rows, CH), (25, 1, rows), (9, 1, rows)]
    return pl.pallas_call(
        total_kernel,
        grid=(1,),
        out_shape=tuple(jax.ShapeDtypeStruct(shape, F32) for shape in shapes),
        in_specs=[whole(kept.shape), whole(landed.shape)],
        out_specs=tuple(whole(shape) for shape in shapes),
        compiler_params=pltpu.CompilerParams(vmem_limit_bytes=12 << 20),
        name="total",
    )(kept, landed)


def by_pixel(stack):
    return jnp.transpose(stack, (0, 2, 3, 4, 1, 5)).reshape(PIXELS, stack.shape[1], CH)


def local(
    saved_last,
    saved_older,
    arriving,
    head_adjoint,
    plan,
    depth_five,
    depth_three,
    point_five,
    point_three,
):
    turns = saved_last.shape[1]
    top = (lax.axis_index("sec") == lax.axis_size("sec") - 1).astype(jnp.int32)[None]
    image = lax.axis_index("img").astype(jnp.int32)
    group, half = (image // 2)[None], (image % 2)[None]
    token, top, group, half = lax.optimization_barrier((call_opening(), top, group, half))
    head = jnp.transpose(head_adjoint, (0, 2, 3, 4, 1, 5)).reshape(turns - 1, PIXELS, 2, CH)
    weights = (point_five[0], point_three[0])
    taps = (depth_five[0], depth_three[0])
    grad_last, act_last, grad_out, back_five = call_first_five(
        token, plan, by_pixel(saved_last), by_pixel(arriving), weights[0], taps[0]
    )
    next_out = from_next(grad_last)
    grad_older, act_older, back_three = call_first_three(
        plan, by_pixel(saved_older), grad_out, weights[1], taps[1]
    )
    next_pass = from_next(grad_older)
    acts = (act_last, act_older)
    sums, mixes, grads = (), (), (grad_out,)
    for t in range(turns - 2):
        made = call_grads(t, acts, taps, (back_five, back_three), sums)
        next_out, made = lax.optimization_barrier((next_out, made))
        sums, mixes = made[:2], (*mixes, *made[2:])
        through, grad_out, head_pass, back_five = call_five(
            t + 1, (top, next_out, head), weights[0], taps[0]
        )
        grads = (*grads, grad_out)
        grad_last = call_finish(t + 1, top, next_pass, head_pass, grad_out, act_last, through)
        next_out = from_next(grad_last)
        ready, _ = lax.optimization_barrier((grad_out, grad_last))
        grad_older, back_three = call_three(t + 1, ready, act_older, weights[1], taps[1])
        if t < turns - 3:
            next_pass = from_next(grad_older)
    made = call_gather(turns - 2, acts, taps, (back_five, back_three), sums, grads, mixes)
    next_out, made = lax.optimization_barrier((next_out, made))
    *sends, own, grad_out, head_pass, back_five, back_three = call_last_grads(
        turns - 1,
        CH * 2 // lax.axis_size("img"),
        (top, group, next_out, head),
        weights,
        made[4:],
        made[:4],
    )
    *sends, grad_older = lax.optimization_barrier((*sends, grad_older))
    landed = [around_rows(sends[distance - 1], distance) for distance in (1, 3, 2)]
    next_pass = from_next(grad_older)
    through, made_older = call_last_convs(
        turns - 1, back_five, back_three, act_older, taps[0], taps[1]
    )
    *landed, through = lax.optimization_barrier((*landed, through))
    kept, send = call_half_total(half, own, landed)
    through, kept, send = lax.optimization_barrier((through, kept, send))
    partner = with_partner(send)
    outgoing = call_last(
        turns - 1, top, next_pass, head_pass, grad_out, act_last, through, made_older
    )
    partner, outgoing = lax.optimization_barrier((partner, outgoing))
    five, three, tap_five, tap_three = call_total(kept, partner)
    outgoing = outgoing.reshape(1, 1, SIDE, SIDE, 2, CH).transpose(0, 4, 1, 2, 3, 5)
    return (
        outgoing,
        five[None],
        jnp.transpose(tap_five, (1, 2, 0)),
        three[None],
        jnp.transpose(tap_three, (1, 2, 0)),
    )


def solution(mesh):
    placed = (
        P("sec", None, "img", None, None, None),
        P("sec", None, "img", None, None, None),
        P("sec", None, "img", None, None, None),
        P(None, None, "img", None, None, None),
        P("sec", None),
        P("sec", None, None),
        P("sec", None, None),
        P("sec", None, None),
        P("sec", None, None),
    )
    return jax.shard_map(
        local,
        mesh=mesh,
        in_specs=placed,
        out_specs=(
            P("sec", None, "img", None, None, None),
            P("sec", "img", None),
            P("sec", "img", None),
            P("sec", "img", None),
            P("sec", "img", None),
        ),
        check_vma=False,
    )
```
